128 devices in a mesh: rows: 8 (over z_lo, x), seq: 16 (over y, z_hi, core).
Axes of the slice: x: 4, y: 4, z: 4 (z_hi: 2, z_lo: 2; z = z_hi * 2 + z_lo), core: 2. Of those that a mesh axis runs over, the one named last changes fastest.
Arguments:
- tokens: bfloat16 [16, 2048, 768], P('rows', 'seq'), may hold values from -6 to 6
- lengths: int32 [16], P('rows'), may hold values from 1 to 2048, as said below
- cotangent: bfloat16 [16, 2048, 768], P('rows', 'seq'), may hold values from -6 to 6
- query_weight: float32 [768, 768], P(('rows', 'seq')), may hold values from -0.0546875 to 0.0546875
- key_weight: float32 [768, 768], P(('rows', 'seq')), may hold values from -0.21875 to 0.21875
- value_weight: float32 [768, 768], P(('rows', 'seq')), may hold values from -0.21875 to 0.21875
- out_weight: float32 [768, 768], P(('rows', 'seq')), may hold values from -2.5 to 2.5
- gate_weight: float32 [768, 2048], P(('rows', 'seq')), may hold values from -0.21875 to 0.21875
- up_weight: float32 [768, 2048], P(('rows', 'seq')), may hold values from -0.21875 to 0.21875
- down_weight: float32 [2048, 768], P(('rows', 'seq')), may hold values from -0.125 to 0.125
- first_gain: float32 [768], P(('rows', 'seq')), may hold values from 0.25 to 1.75
- second_gain: float32 [768], P(('rows', 'seq')), may hold values from 0.25 to 1.75
- bias_table: float32 [384], P(('rows', 'seq')), may hold values from -3 to 3
Outputs:
- output: bfloat16 [16, 2048, 768], P('rows', 'seq')
- input_grad: float32 [16, 2048, 768], P('rows', 'seq')
- query_weight_grad: float32 [768, 768], P(('rows', 'seq'))
- key_weight_grad: float32 [768, 768], P(('rows', 'seq'))
- value_weight_grad: float32 [768, 768], P(('rows', 'seq'))
- out_weight_grad: float32 [768, 768], P(('rows', 'seq'))
- gate_weight_grad: float32 [768, 2048], P(('rows', 'seq'))
- up_weight_grad: float32 [768, 2048], P(('rows', 'seq'))
- down_weight_grad: float32 [2048, 768], P(('rows', 'seq'))
- first_gain_grad: float32 [768], P(('rows', 'seq'))
- second_gain_grad: float32 [768], P(('rows', 'seq'))
- bias_table_grad: float32 [384], P(('rows', 'seq'))
The draws below stay inside these ranges and needn't reach their ends.
Inputs may be any that keep to these rules, and one draw needn't show every extreme that they name: Row b's first lengths[b] tokens are valid, the rest are padding; at least one row has all 2048 tokens valid.
All inputs are finite; a program needn't handle non-finite values.
Results may differ from the reference program's by a relative error of at most 0.039.
Values may be sent and summed in bfloat16 or wider, within the bound.
A program may use at most 192 MiB of HBM per device.

```python
import math
import jax
import jax.numpy as jnp
from jax import lax

D = 768
HEADS = 12
HEAD_DIM = 64
FF = 2048
BUCKETS = 32
BATCH = 16
SEQ = 2048


def draw_lengths(key, part):
    full_key, short_key, pick_key = jax.random.split(key, 3)
    full_rows = jax.random.randint(full_key, (BATCH,), 0, 5) < 3
    short_rows = jax.random.randint(short_key, (BATCH,), 1, SEQ)
    forced_row = jax.random.randint(pick_key, (), 0, BATCH)
    full_rows = full_rows | (jnp.arange(BATCH) == forced_row)
    return jnp.where(full_rows, SEQ, short_rows).astype(jnp.int32)


def levels(stream_key, dims, cuts, low, high):
    level, own = 1.0, jax.random.fold_in(stream_key, 6)
    for dim, shards_of in cuts:
        steps = jnp.exp(jax.random.uniform(jax.random.fold_in(own, dim), (shards_of,), jnp.float32, low / len(cuts), high / len(cuts)))
        level = level * jnp.repeat(steps, dims[dim] // shards_of).reshape([-1 if axis == dim else 1 for axis in range(len(dims))])
    return level


def centred(key, dims, scale, most, pieces=(), held_as=jnp.bfloat16):
    level = levels(key, dims, pieces, -0.22, 0.18) if pieces else 1.0
    values = jax.random.normal(key, dims, jnp.float32) * scale * level
    return jnp.minimum(jnp.maximum(values, -most), most).astype(held_as)


def setup_inputs(seed: int = 0) -> dict:
    seeds = jax.random.split(jax.random.key(seed), 14)
    return {
        "tokens": centred(seeds[0], (BATCH, SEQ, D), 1.0, 6.0, ((0, 8), (1, 16))),
        "lengths": draw_lengths(jax.random.fold_in(seeds[13], 71), 0),
        "cotangent": centred(seeds[2], (BATCH, SEQ, D), 1.0, 6.0, ((0, 8), (1, 16))),
        "query_weight": centred(seeds[3], (D, D), (16 * D) ** -0.5, 0.0546875, ((0, 128),), jnp.float32),
        "key_weight": centred(seeds[4], (D, D), D ** -0.5, 0.21875, ((0, 128),), jnp.float32),
        "value_weight": centred(seeds[5], (D, D), D ** -0.5, 0.21875, ((0, 128),), jnp.float32),
        "out_weight": centred(seeds[6], (D, D), (max(1, 16 * D // SEQ)) ** -0.5, 2.5, ((0, 128),), jnp.float32),
        "gate_weight": centred(seeds[7], (D, FF), D ** -0.5, 0.21875, ((0, 128),), jnp.float32),
        "up_weight": centred(seeds[8], (D, FF), D ** -0.5, 0.21875, ((0, 128),), jnp.float32),
        "down_weight": centred(seeds[9], (FF, D), FF ** -0.5, 0.125, ((0, 128),), jnp.float32),
        "first_gain": jnp.clip(1.0 + 0.15 * jax.random.normal(seeds[10], (D,), jnp.float32), 0.25, 1.75),
        "second_gain": jnp.clip(1.0 + 0.15 * jax.random.normal(seeds[11], (D,), jnp.float32), 0.25, 1.75),
        "bias_table": centred(seeds[12], (HEADS * BUCKETS,), 1.0, 3.0, ((0, 128),), jnp.float32),
    }


@jax.custom_vjp
def low(v):
    return lax.optimization_barrier(v.astype(jnp.bfloat16)).astype(jnp.float32)

@jax.custom_vjp
def low_back(v):
    return v

def low_keep(v):
    return (low(v), None)

def low_pass(kept, grad):
    return (grad,)

def back_keep(v):
    return (v, None)

def back_low(kept, grad):
    return (low(grad),)
low.defvjp(low_keep, low_pass)
low_back.defvjp(back_keep, back_low)
EPSILON = 1e-06
NEGATIVE = -1e+30
LIMITS = (1, 2, 3, 4, 5, 6, 7, 8, 12, 16, 23, 32, 46, 64, 91)

def rounded_both(values):
    return low_back(low(values))

def bucket_ids(offsets):
    distance = jnp.abs(offsets)
    bucket_sum = (offsets > 0).astype(jnp.int32) * (BUCKETS // 2)
    for threshold in LIMITS:
        bucket_sum = bucket_sum + (distance >= threshold).astype(jnp.int32)
    return bucket_sum

def rms_norm(values, gain_vector):
    mean_square = lax.optimization_barrier(jnp.mean(values * values, axis=-1, keepdims=True))
    return values * lax.rsqrt(mean_square + EPSILON) * gain_vector

def matmul_high(left, right):
    return jnp.dot(left, right, precision=lax.Precision.HIGHEST)

def row_forward(row_input, row_length, weights):
    query_w, key_w, value_w, out_w, gate_w, up_w, down_w, first_g, second_g, table = weights
    normed = low(rms_norm(row_input, first_g))
    queries = rounded_both(matmul_high(normed, query_w))
    keys_rows = rounded_both(matmul_high(normed, key_w))
    values_rows = rounded_both(matmul_high(normed, value_w))
    positions = jnp.arange(SEQ, dtype=jnp.int32)
    key_valid = positions < row_length
    head_keys = keys_rows.reshape(SEQ, HEADS, HEAD_DIM)
    head_values = values_rows.reshape(SEQ, HEADS, HEAD_DIM)
    block_rows = math.gcd(SEQ, 512)
    head_queries = queries.reshape(SEQ // block_rows, block_rows, HEADS, HEAD_DIM)
    block_starts = jnp.arange(SEQ // block_rows, dtype=jnp.int32) * block_rows

    @jax.checkpoint
    def attend(row_pair):
        query_block, block_start = row_pair
        query_pos = block_start + jnp.arange(block_rows, dtype=jnp.int32)
        bias_block = table[:, bucket_ids(positions[None, :] - query_pos[:, None])]
        products = low_back(jnp.einsum('qhd,khd->hqk', query_block, head_keys, precision=lax.Precision.HIGHEST))
        scores = products + bias_block
        scores = jnp.where(key_valid[None, None, :], scores, NEGATIVE)
        row_max = lax.optimization_barrier(jnp.max(scores, axis=-1, keepdims=True))
        log_total = row_max + jnp.log(lax.optimization_barrier(jnp.sum(jnp.exp(scores - row_max), axis=-1, keepdims=True)))
        probs_low = low(jnp.exp(scores - log_total))
        mixed_sum = jnp.einsum('hqk,khd->qhd', probs_low, head_values, precision=lax.Precision.HIGHEST)
        return mixed_sum.reshape(block_rows, HEADS * HEAD_DIM)
    attended = lax.map(attend, (head_queries, block_starts)).reshape(SEQ, D)
    attention_out = low_back(matmul_high(rounded_both(attended), out_w))
    middle = row_input + attention_out
    normed_two = low(rms_norm(middle, second_g))
    gate_act = low_back(matmul_high(normed_two, gate_w))
    up_act = low_back(matmul_high(normed_two, up_w))
    hidden = low(jax.nn.gelu(gate_act, approximate=True) * up_act)
    return middle + low_back(matmul_high(hidden, down_w))

def reference(tokens, lengths, cotangent, query_weight, key_weight, value_weight, out_weight, gate_weight, up_weight, down_weight, first_gain, second_gain, bias_table):
    inputs = tokens.astype(jnp.float32)
    params = (query_weight, key_weight, value_weight, out_weight, gate_weight, up_weight, down_weight, first_gain, second_gain, bias_table)

    def forward(layer_in, layer_params):
        rounded = jax.tree.map(low, layer_params)
        weights = rounded[:9] + (rounded[9].reshape(HEADS, BUCKETS),)
        return lax.map(lambda row_pair: row_forward(row_pair[0], row_pair[1], weights), (layer_in, lengths))
    output, pullback = jax.vjp(forward, inputs, params)
    input_grad, grads = pullback(cotangent.astype(jnp.float32))
    return (output.astype(jnp.bfloat16), input_grad, grads[0], grads[1], grads[2], grads[3], grads[4], grads[5], grads[6], grads[7], grads[8], grads[9])
```

```python
import math
import functools

import jax
import jax.numpy as jnp
from jax import lax
from jax.experimental import pallas as pl
from jax.experimental.pallas import tpu as pltpu
from jax.sharding import PartitionSpec as P

MESH = pl.DeviceIdType.MESH
BF = jnp.bfloat16
F32 = jnp.float32
D = 768
SEQ = 2048
EPSILON = 1e-06
NEGATIVE = -1e30
LIMITS = (1, 2, 3, 4, 5, 6, 7, 8, 12, 16, 23, 32, 46, 64, 91)
NSEM = 192
BQ = 256
STEPS = 12


def dev(x, y, z, c):
    return ((z % 2) * 4 + x, (y * 2 + z // 2) * 2 + c)


def first_head(t):
    return (3 * t) // 2


def iota(shape, dim):
    return lax.broadcasted_iota(jnp.int32, shape, dim)


def dot(a, b):
    return jnp.dot(a, b, preferred_element_type=F32)


def dot_nt(a, b):
    return lax.dot_general(a, b, (((1,), (1,)), ((), ())), preferred_element_type=F32)


class Comm:
    def __init__(self, x, y, z, c, send_sem, recv_sem):
        self.x, self.y, self.z, self.c = x, y, z, c
        self.ss, self.rs = send_sem, recv_sem
        self.next = 0
        self.pending = []

    def take(self, n=1):
        at = self.next
        self.next += n
        assert self.next <= NSEM
        return at

    def peer(self, axis, offset):
        x, y, z, c = self.x, self.y, self.z, self.c
        if axis == "x":
            return dev((x + offset) % 4, y, z, c)
        if axis == "y":
            return dev(x, (y + offset) % 4, z, c)
        if axis == "z":
            return dev(x, y, (z + offset) % 4, c)
        return dev(x, y, z, 1 - c)

    def place(self, axis, offset):
        at = {"x": self.x, "y": self.y, "z": self.z}[axis]
        return (at + offset) % 4

    def copy(self, src, dst, i, to, j=None):
        return pltpu.make_async_remote_copy(
            src_ref=src,
            dst_ref=dst,
            send_sem=self.ss.at[i],
            recv_sem=self.rs.at[i if j is None else j],
            device_id=to,
            device_id_type=MESH,
        )

    def send(self, src, dst, i, to):
        cp = self.copy(src, dst, i, to)
        cp.start()
        self.pending.append(cp)

    def recv(self, dst, i):
        self.copy(dst, dst, i, self.peer("c", 0)).wait_recv()

    def send_or_keep(self, src, dst, i, to, j, own):
        cp = self.copy(src, dst, i, to, j)
        keep = pltpu.make_async_copy(src, dst, self.rs.at[j])

        @pl.when(own)
        def _():
            keep.start()

        @pl.when(jnp.logical_not(own))
        def _():
            cp.start()

        self.pending.append((cp, own))

    def drain(self):
        for cp in self.pending:
            if isinstance(cp, tuple):
                cp, own = cp

                @pl.when(jnp.logical_not(own))
                def _():
                    cp.wait_send()
            else:
                cp.wait_send()
        self.pending = []


class Direct:
    def __init__(self, comm, axis, views):
        self.comm, self.axis, self.views = comm, axis, views
        self.count = len(views(comm.place(axis, 0)))
        self.base = comm.take(3 * self.count)

    def start(self):
        for k, off in enumerate((1, 3, 2)):
            for n, ref in enumerate(self.views(self.comm.place(self.axis, 0))):
                self.comm.send(ref, ref, self.base + k * self.count + n, self.comm.peer(self.axis, off))

    def wait(self):
        for k, off in enumerate((1, 3, 2)):
            for n, ref in enumerate(self.views(self.comm.place(self.axis, -off + 4))):
                self.comm.recv(ref, self.base + k * self.count + n)


class Ring:
    def __init__(self, comm, axis, views, halves):
        self.comm, self.axis, self.views, self.halves = comm, axis, views, halves
        self.count = len(views(comm.place(axis, 0)))
        self.base = comm.take(4 * self.count)

    def start(self, source=None):
        own = self.views(self.comm.place(self.axis, 0))
        for n, ref in enumerate(own):
            src = ref if source is None else source[n]
            for k, off in enumerate((1, 3)):
                self.comm.send(src, ref, self.base + k * self.count + n, self.comm.peer(self.axis, off))

    def forward(self):
        for k, off in enumerate((1, 3)):
            came = self.comm.place(self.axis, -off + 4)
            for n, ref in enumerate(self.views(came)):
                self.comm.recv(ref, self.base + k * self.count + n)
            for n, ref in enumerate(self.halves(came, k)):
                self.comm.send(ref, ref, self.base + (2 + k) * self.count + n, self.comm.peer(self.axis, off))

    def wait(self):
        far = self.comm.place(self.axis, 2)
        for k in range(2):
            for n, ref in enumerate(self.halves(far, k)):
                self.comm.recv(ref, self.base + (2 + k) * self.count + n)


def bucket_ids(offsets):
    distance = jnp.abs(offsets)
    bucket_sum = jnp.where(offsets > 0, 16, 0)
    for threshold in LIMITS:
        bucket_sum = bucket_sum + jnp.where(distance >= threshold, 1, 0)
    return bucket_sum


def rms_scale(values):
    return lax.rsqrt(jnp.mean(values * values, axis=-1, keepdims=True) + EPSILON)


def greet(comm):
    x, y, z, c = comm.x, comm.y, comm.z, comm.c
    zl, zh = z % 2, z // 2
    barrier = pltpu.get_barrier_semaphore()
    count = 0
    peers = []
    for dy in range(4):
        for dh in range(2):
            for dc in range(2):
                if dy or dh or dc:
                    peers.append(dev(x, (y + dy) % 4, ((zh + dh) % 2) * 2 + zl, (c + dc) % 2))
    for off in (1, 2, 3):
        peers.append(comm.peer("x", off))
    for off in (1, 3):
        peers.append(comm.peer("z", off))
    for peer in peers:
        pl.semaphore_signal(barrier, inc=1, device_id=peer, device_id_type=MESH)
        count += 1
    return barrier, count


def cast_up(v):
    return v.astype(F32)


def head_bias(tables, o):
    return tables[o : o + 1, 0:1], tables[o : o + 1, 1023:1024]


def mega(stop, *refs):
    names = [n for n, _ in INPUTS] + [n for n, _ in outputs_of(stop)] + [n for n, _ in SCRATCH]
    r = dict(zip(names, refs))
    rows, seq = lax.axis_index("rows"), lax.axis_index("seq")
    x, y, zl, zh, c = rows % 4, seq // 4, rows // 4, (seq // 2) % 2, seq % 2
    z = zh * 2 + zl
    flat = rows * 16 + seq
    t = c * 4 + y
    comm = Comm(x, y, z, c, r["send_sem"], r["recv_sem"])
    barrier, count = greet(comm)

    lanes = iota((1, 1024), 1)
    first_row = jnp.zeros((1, 1024), F32)
    second_row = jnp.zeros((1, 1024), F32)
    for i in range(6):
        first_row += jnp.where(lanes == 6 * flat + i, r["g1"][i], 0.0)
        second_row += jnp.where(lanes == 6 * flat + i, r["g2"][i], 0.0)
    for i in range(3):
        at = 768 + 3 * flat + i
        first_row += jnp.where(lanes == at, r["bt"][i], 0.0)
        second_row += jnp.where((lanes >= 768) & (lanes == at - 256), r["bt"][i], 0.0)
    first_row = cast_up(first_row.astype(BF))
    second_row = cast_up(second_row.astype(BF))
    wst, w0 = r["wst"], r["w0"]
    for cc in range(2):
        for yy in range(4):
            d, h0 = cc * 4 + yy, first_head(cc * 4 + yy)
            for i, name in enumerate(("wq", "wk", "wv")):
                wst[d, 0:6, 128 * i : 128 * (i + 1)] = r[name][:, 64 * h0 : 64 * h0 + 128]
            for i, name in enumerate(("wg", "wu")):
                for k in range(2):
                    tile = 2 * (2 * yy + k) + cc
                    at = 384 + 256 * i + 128 * k
                    wst[d, 0:6, at : at + 128] = r[name][:, 128 * tile : 128 * tile + 128]
            if yy < 3:
                at = (cc * 3 + yy) * 128
                wst[d, 0:6, 896:1024] = r["wo"][:, at : at + 128]
            else:
                wst[d, 0:6, 896:1024] = jnp.zeros((6, 128), F32)
            wst[d, 6:7, :] = first_row
            wst[d, 7:8, :] = second_row
    r["wdst"][...] = r["wd"][...].astype(BF)

    pl.semaphore_wait(barrier, count)

    W1, WD, WQ, G5 = r["W1"], r["WD"], r["WQ"], r["G5"]
    T5, TK, CT, tok, cot = r["T5"], r["TK"], r["CT"], r["tok"], r["cot"]
    slot = (y % 2) * 4 + zh * 2 + c
    base0 = comm.take(8)
    baser = comm.take(8)
    for cc in range(2):
        for yy in range(4):
            to = dev(x, yy, (y // 2) * 2 + zl, cc)
            own = (y == yy) & (c == cc) & (zh == y // 2)
            cp = comm.copy(wst.at[cc * 4 + yy], w0.at[slot], base0 + cc * 4 + yy, to, baser + slot)
            keep = pltpu.make_async_copy(wst.at[cc * 4 + yy], w0.at[slot], comm.rs.at[baser + slot])
            pl.when(own)(keep.start)
            pl.when(jnp.logical_not(own))(cp.start)
            comm.pending.append((cp, own))
    wd_to = (zh * 2 + c, y % 2, y // 2)
    own_wd = (wd_to[0] == y) & (wd_to[1] == zh) & (wd_to[2] == c)
    wdi = comm.take()
    wd_region = WD.at[zl, x, wd_to[1], pl.ds(16 * wd_to[0], 16)]
    comm.send_or_keep(
        r["wdst"], wd_region, wdi, dev(x, wd_to[0], wd_to[1] * 2 + zl, wd_to[2]), wdi, own_wd
    )

    other = comm.peer("z", 2)
    zi = comm.take()
    comm.send(tok.at[1 - zh], T5.at[y, zh, c], zi, other)
    own_tokens = Ring(
        comm,
        "y",
        lambda yy: [T5.at[yy, zh, c]],
        lambda yy, k: [T5.at[yy, zh, c, pl.ds(64 * k, 64)]],
    )
    own_tokens.start(source=[tok.at[zh]])
    local = comm.take(3)
    keep_tokens = pltpu.make_async_copy(tok.at[zh], T5.at[y, zh, c], comm.ss.at[local])
    keep_tokens.start()
    keep_tk = pltpu.make_async_copy(tok, TK.at[:, c], comm.ss.at[local + 1])
    keep_tk.start()
    keep_ct = pltpu.make_async_copy(cot, CT.at[:, c], comm.ss.at[local + 2])
    keep_ct.start()
    pair = comm.take(2)

    for j in range(8):
        comm.recv(w0.at[j], baser + j)
    asm = r["asm"]
    gsum = jnp.zeros((2, 1024), F32)
    for j in range(8):
        asm[6 * j : 6 * j + 6, :] = w0[j, 0:6, :]
        gsum += w0[j, 6:8, :]
    WQ[zl, x, zh] = asm[:, 0:384].astype(BF)
    G5[zl, x, zh] = jnp.concatenate([gsum, jnp.zeros((6, 1024), F32)], axis=0)
    W1[zl, x, zh, :, pl.ds(pl.multiple_of(640 * y, 128), 640)] = asm[:, 384:1024].astype(BF)
    qkv_a1 = Direct(comm, "x", lambda xx: [WQ.at[zl, xx, zh, :, pl.ds(0, 256)], G5.at[zl, xx, zh]])
    qkv_b1 = Direct(comm, "z", lambda zz: [WQ.at[zz % 2, x, zz // 2, :, pl.ds(256, 128)]])
    qkv_a1.start()
    qkv_b1.start()
    comm.recv(WD.at[zl, x, zh, pl.ds(16 * y, 16)], wdi)
    ff_y = Direct(
        comm,
        "y",
        lambda yy: [
            W1.at[zl, x, zh, :, pl.ds(pl.multiple_of(640 * yy, 128), 640)],
            WD.at[zl, x, zh, pl.ds(16 * yy, 16)],
        ],
    )
    ff_y.start()

    comm.recv(T5.at[y, 1 - zh, c], zi)
    far_tokens = Ring(
        comm,
        "y",
        lambda yy: [T5.at[yy, 1 - zh, c]],
        lambda yy, k: [T5.at[yy, 1 - zh, c, pl.ds(64 * k, 64)]],
    )
    far_tokens.start()
    keep_tokens.wait()
    sib = comm.peer("c", 0)
    across = comm.take(4)

    def cross(k):
        yy = (y + (0, 1, 3, 2)[k]) % 4
        comm.send(T5.at[yy, :, c], T5.at[yy, :, c], across + k, sib)

    def crossed(k):
        yy = (y + (0, 1, 3, 2)[k]) % 4
        comm.recv(T5.at[yy, :, 1 - c], across + k)

    cross(0)
    own_tokens.forward()
    qkv_a1.wait()
    qkv_b1.wait()
    qkv_a2 = Direct(
        comm,
        "z",
        lambda zz: [WQ.at[zz % 2, :, zz // 2, :, pl.ds(0, 256)], G5.at[zz % 2, :, zz // 2]],
    )
    qkv_b2 = Direct(comm, "x", lambda xx: [WQ.at[:, xx, :, :, pl.ds(256, 128)]])
    qkv_a2.start()
    qkv_b2.start()
    far_tokens.forward()
    cross(1)
    cross(2)
    ff_y.wait()
    ff_a1 = Direct(
        comm,
        "x",
        lambda xx: [WO_A(W1.at[zl, xx, zh]), WD.at[zl, xx, zh, :, pl.ds(0, 384)]],
    )
    ff_b1 = Direct(
        comm,
        "z",
        lambda zz: [
            W1.at[zz % 2, x, zz // 2, :, pl.ds(1280, 1280)],
            WD.at[zz % 2, x, zz // 2, :, pl.ds(384, 384)],
        ],
    )
    ff_a1.start()
    ff_b1.start()
    own_tokens.wait()
    far_tokens.wait()
    cross(3)
    keep_tk.wait()
    keep_ct.wait()
    comm.send(TK.at[:, c], TK.at[:, c], pair, sib)
    comm.send(CT.at[:, c], CT.at[:, c], pair + 1, sib)

    qkv_a2.wait()
    qkv_b2.wait()
    total = jnp.zeros((8, 1024), F32)
    for a in range(2):
        for b in range(4):
            for e in range(2):
                total += G5[a, b, e]
    r["GS"][...] = total
    h0 = first_head(t)
    table_row = jnp.concatenate([total[0:1, 768:1024], total[1:2, 768:896]], axis=1)
    table_row = jnp.broadcast_to(table_row, (8, 384))
    table_row = pltpu.roll(table_row, 384 - 32 * h0, 1)[:, 0:128]
    lane = iota((8, 128), 1)
    sub = iota((8, 128), 0)
    table_two = jnp.where((lane // 32) == sub, table_row, 0.0).astype(BF)
    r["OH"][...] = jnp.where(
        bucket_ids(iota((128, 1024), 1) - 512) == iota((128, 1024), 0) % 32, 1.0, 0.0
    ).astype(BF)
    by_offset = dot(table_two, r["OH"][...])
    r["BO"][...] = by_offset
    for h in range(2):
        for k in range(4):
            rolled = pltpu.roll(
                jnp.broadcast_to(by_offset[h : h + 1, :], (64, 1024)), 640 + 64 * k, 1, stride=1, stride_axis=0
            )
            r["BT"][h, 64 * k : 64 * k + 64, :] = rolled[:, 0:512]

    for k in range(4):
        crossed(k)
    N, QA, KT, KN, VN, VT = r["N"], r["QA"], r["KT"], r["KN"], r["VN"], r["VT"]
    row_len = r["lens"][zh]

    def project(i, carry):
        raw = cast_up(T5[i // 2, i % 2].reshape(256, D))
        normed = (raw * rms_scale(raw) * r["GS"][0:1, 0:768]).astype(BF)
        N[pl.ds(i * 256, 256), :] = normed
        res = dot(normed, WQ[...].reshape(D, 384))
        q, k_, v = res[:, 0:128], res[:, 128:256], res[:, 256:384]
        at = pl.ds(pl.multiple_of(i * 256, 256), 256)
        KN[at, :] = k_.astype(BF)
        VN[at, :] = v.astype(BF)
        VT[:, at] = v.T.astype(BF)
        kt = k_.T
        lane = iota((256, 128), 1)
        sub = iota((128, 256), 0)
        key_at = i * 256 + iota((128, 256), 1)
        for h in range(2):
            base = 64 * (1 - h)
            hot = jnp.where((lane == base + i) | (lane == base + 8), 1.0, 0.0)
            QA[h, at, :] = jnp.where(lane // 64 == h, q, hot).astype(BF)
            left, right = head_bias(r["BO"][...], h)
            start = 256 * (sub - base)
            extra = jnp.where(key_at < start - 128, left, 0.0) + jnp.where(
                key_at >= start + 384, right, 0.0
            )
            masked = jnp.where(key_at >= row_len, NEGATIVE, 0.0)
            extra = jnp.where(sub - base < 8, extra, jnp.where(sub - base == 8, masked, 0.0))
            KT[h, :, at] = jnp.where(sub // 64 == h, kt, extra).astype(BF)
        return carry

    lax.fori_loop(0, 8, project, 0)
    r["ON"][...] = jnp.zeros((SEQ, 128), BF)

    SC, PB, BT, ON, LI = r["SC"], r["PB"], r["BT"], r["ON"], r["LI"]

    def unit_of(step):
        ui = step // 4
        u = jnp.where(ui == 0, 1, jnp.where(ui == 1, 0, 2))
        number = 3 * t + u
        head = number // 2 - h0
        start = (number % 2) * 1024 + (step % 4) * 256
        return head, pl.multiple_of(start, 256)

    def attend(step, carry):
        head, q0 = unit_of(step)
        qa = QA[head, pl.ds(q0, BQ), :]
        for j in range(8):
            SC[:, 128 + 256 * j : 384 + 256 * j] = dot(qa, KT[head, :, 256 * j : 256 * j + 256])
        SC[:, pl.ds(q0, 512)] = SC[:, pl.ds(q0, 512)] + BT[head]
        top = SC[:, 128:256]
        for j in range(2, 17):
            top = jnp.maximum(top, SC[:, 128 * j : 128 * j + 128])
        top = jnp.max(top, axis=1, keepdims=True)
        sums = jnp.zeros((BQ, 128), F32)
        for j in range(16):
            p = jnp.exp(SC[:, 128 + 128 * j : 256 + 128 * j] - top)
            sums += p
            PB[step, :, 128 * j : 128 * j + 128] = p.astype(BF)
        inv = 1.0 / jnp.sum(sums, axis=1, keepdims=True)
        LI[step] = jnp.broadcast_to(inv, (BQ, 128))
        mixed = dot(PB[step], VN[...]) * inv
        lane = iota((BQ, 128), 1)
        ON[pl.ds(q0, BQ), :] = jnp.where(lane // 64 == head, mixed, cast_up(ON[pl.ds(q0, BQ), :])).astype(BF)
        return carry

    A = r["A"]
    base_o = comm.take(8)
    base_or = comm.take(8)

    def give(half, n):
        for i in range(4):
            yy, hh = 2 * half + i // 2, i % 2
            src = ON.at[pl.ds(pl.multiple_of(256 * (yy * 2 + hh), 256), 256)]
            dst = A.at[zh, :, pl.ds(pl.multiple_of(128 * y, 128), 128)]
            own = (yy == y) & (hh == zh)
            cp = comm.copy(src, dst, base_o + 4 * n + i, dev(x, yy, hh * 2 + zl, c), base_or + y * 2 + zh)
            keep = pltpu.make_async_copy(src, dst, comm.rs.at[base_or + y * 2 + zh])
            pl.when(own)(keep.start)
            pl.when(jnp.logical_not(own))(cp.start)
            comm.pending.append((cp, own))

    single = (3 * t + 1) % 2
    lax.fori_loop(0, 2, attend, 0)
    ff_a1.wait()
    ff_b1.wait()
    ff_a2 = Ring(
        comm,
        "z",
        lambda zz: [
            W1.at[zz % 2, :, zz // 2, :, pl.ds(0, 1280)],
            WD.at[zz % 2, :, zz // 2, :, pl.ds(0, 384)],
        ],
        lambda zz, k: [
            W1.at[zz % 2, pl.ds(2 * k, 2), zz // 2, :, pl.ds(0, 1280)],
            WD.at[zz % 2, pl.ds(2 * k, 2), zz // 2, :, pl.ds(0, 384)],
        ],
    )
    ff_b2 = Ring(
        comm,
        "x",
        lambda xx: [
            W1.at[:, xx, :, :, pl.ds(1280, 1280)],
            WD.at[:, xx, :, :, pl.ds(384, 384)],
        ],
        lambda xx, k: [
            W1.at[k, xx, :, :, pl.ds(1280, 1280)],
            WD.at[k, xx, :, :, pl.ds(384, 384)],
        ],
    )
    ff_a2.start()
    ff_b2.start()
    lax.fori_loop(2, 4, attend, 0)
    give(single, 0)
    lax.fori_loop(4, 9, attend, 0)
    ff_a2.forward()
    ff_b2.forward()
    lax.fori_loop(9, STEPS, attend, 0)
    give(1 - single, 1)
    ff_a2.wait()
    ff_b2.wait()
    for yy in range(4):
        for hh in range(2):
            comm.recv(A.at[hh, :, pl.ds(128 * yy, 128)], base_or + yy * 2 + hh)
    comm.recv(TK.at[:, 1 - c], pair)
    comm.recv(CT.at[:, 1 - c], pair + 1)
    if stop == "fwd":
        comm.drain()
        for name, _ in outputs_of(stop):
            r[name][...] = r[name[2:]][...]
        return


def WO_A(ref):
    return ref.at[:, pl.ds(0, 1280)]


INPUTS = [
    ("lens", "s"), ("g1", "s"), ("g2", "s"), ("bt", "s"),
    ("tok", "v"), ("cot", "v"), ("wq", "v"), ("wk", "v"), ("wv", "v"), ("wo", "v"),
    ("wg", "v"), ("wu", "v"), ("wd", "v"),
]
SCRATCH = [
    ("W1", ((2, 4, 2, 48, 2560), BF)),
    ("WD", ((2, 4, 2, 64, 768), BF)),
    ("WQ", ((2, 4, 2, 48, 384), BF)),
    ("G5", ((2, 4, 2, 8, 1024), F32)),
    ("T5", ((4, 2, 2, 128, 768), BF)),
    ("TK", ((2, 2, 128, 768), BF)),
    ("CT", ((2, 2, 128, 768), BF)),
    ("wst", ((8, 8, 1024), F32)),
    ("w0", ((8, 8, 1024), F32)),
    ("asm", ((48, 1024), F32)),
    ("wdst", ((16, 768), BF)),
    ("GS", ((8, 1024), F32)),
    ("OH", ((128, 1024), BF)),
    ("BO", ((8, 1024), F32)),
    ("BT", ((2, 256, 512), F32)),
    ("N", ((2048, 768), BF)),
    ("QA", ((2, 2048, 128), BF)),
    ("KT", ((2, 128, 2048), BF)),
    ("KN", ((2048, 128), BF)),
    ("VN", ((2048, 128), BF)),
    ("VT", ((128, 2048), BF)),
    ("SC", ((256, 2304), F32)),
    ("PB", ((12, 256, 2048), BF)),
    ("ON", ((2048, 128), BF)),
    ("LI", ((12, 256, 128), F32)),
    ("A", ((2, 256, 512), BF)),
    ("send_sem", None),
    ("recv_sem", None),
]


def outputs_of(stop):
    if stop == "fwd":
        shapes = dict((n, s) for n, s in SCRATCH if s is not None)
        return [("o_" + n, shapes[n]) for n in ("A", "ON", "N", "WQ", "GS", "KN")]
    return []


def call_mega(stop, *args):
    spec = {"s": pl.BlockSpec(memory_space=pltpu.SMEM), "v": pl.BlockSpec(memory_space=pltpu.VMEM)}
    outs = outputs_of(stop)
    scratch = []
    for _, s in SCRATCH:
        scratch.append(pltpu.SemaphoreType.DMA((NSEM,)) if s is None else pltpu.VMEM(s[0], s[1]))
    return pl.pallas_call(
        functools.partial(mega, stop),
        out_shape=[jax.ShapeDtypeStruct(s[0], s[1]) for _, s in outs],
        in_specs=[spec[k] for _, k in INPUTS],
        out_specs=[pl.BlockSpec(memory_space=pltpu.VMEM) for _ in outs],
        scratch_shapes=scratch,
        name="layer",
        compiler_params=pltpu.CompilerParams(
            collective_id=0, has_side_effects=True, vmem_limit_bytes=62 * 2**20
        ),
    )(*args)


HEADS = 12
HEAD_DIM = 64
BUCKETS = 32


EPSILON = 1e-06
NEGATIVE = -1e30
LIMITS = (1, 2, 3, 4, 5, 6, 7, 8, 12, 16, 23, 32, 46, 64, 91)


def laid_out(parts, dim):
    lengths = list(parts.shape[1:])
    lengths[dim] *= parts.shape[0]
    return jnp.moveaxis(parts, 0, dim).reshape(lengths)


def gather_together(arrays, axis, dims):
    vector = jnp.concatenate([a.reshape(-1) for a in arrays])
    lines, at, done = (lax.all_gather(vector, axis), 0, [])
    for a, dim in zip(arrays, dims):
        parts = lines[:, at : at + a.size].reshape(-1, *a.shape)
        done.append(laid_out(parts, dim))
        at += a.size
    return tuple(done)


def sent_together(arrays, axis, dim, along):
    widths = [a.shape[along] for a in arrays]
    both = jnp.concatenate(arrays, axis=along)
    whole = lax.all_gather(both, axis, axis=dim, tiled=True)
    return tuple(jnp.split(whole, [sum(widths[:k]) for k in range(1, len(widths))], axis=along))


def in_one_piece(arrays, axis, dim, along):
    both = jnp.concatenate(arrays, axis=along)
    whole, at, done = (lax.psum_scatter(both, axis, scatter_dimension=dim, tiled=True), 0, [])
    for a in arrays:
        done.append(lax.slice_in_dim(whole, at, at + a.shape[along], axis=along))
        at += a.shape[along]
    return tuple(done)


def cut_along(shard, dim, size):
    before, after = (shard.shape[:dim], shard.shape[dim + 1 :])
    return jnp.moveaxis(shard.reshape(*before, size, -1, *after), dim, 0)


def sum_packed(arrays, axis, dims):
    size = lax.axis_size(axis)
    parts = [cut_along(a, dim, size) for a, dim in zip(arrays, dims)]
    lines = jnp.concatenate([b.reshape(size, -1) for b in parts], axis=1)
    span = max(16, -(-lines.shape[1] // 1024) * 8)
    lines = jnp.pad(lines, ((0, 0), (0, span * 128 - lines.shape[1]))).reshape(-1, 128)
    vector, at, done = (lax.psum_scatter(lines, axis, tiled=True).reshape(-1), 0, [])
    for b in parts:
        part = b[0]
        done.append(vector[at : at + part.size].reshape(part.shape))
        at += part.size
    return tuple(done)


def rms_norm(values, gain_vector):
    mean_square = jnp.mean(values * values, axis=-1, keepdims=True)
    return values * lax.rsqrt(mean_square + EPSILON) * gain_vector


def block_scores(query_part, key_part, query_at, key_at, table_mat, lengths):
    bucket_of = bucket_ids(key_at[None, :] - query_at[:, None])
    onehot = (bucket_of[:, :, None] == jnp.arange(BUCKETS, dtype=jnp.int32)).astype(jnp.bfloat16)
    bias_block = jnp.einsum("qkb,hb->hqk", onehot, table_mat, preferred_element_type=jnp.float32)
    scores = (
        jnp.einsum("rqhd,rkhd->rhqk", query_part, key_part, preferred_element_type=jnp.float32)
        + bias_block[None]
    )
    key_valid = key_at[None, :] < lengths[:, None]
    return (jnp.where(key_valid[:, None, None, :], scores, NEGATIVE), bucket_of)


def table_term(score_grad, bucket_of):
    selector = (bucket_of[:, :, None] == jnp.arange(BUCKETS, dtype=jnp.int32)).astype(jnp.bfloat16)
    upper = score_grad.astype(jnp.bfloat16)
    lower = (score_grad - upper.astype(jnp.float32)).astype(jnp.bfloat16)
    total = jnp.einsum("rhqk,qkb->hb", upper, selector, preferred_element_type=jnp.float32)
    return total + jnp.einsum("rhqk,qkb->hb", lower, selector, preferred_element_type=jnp.float32)


def per_device(
    tokens,
    lengths,
    cotangent,
    query_weight,
    key_weight,
    value_weight,
    out_weight,
    gate_weight,
    up_weight,
    down_weight,
    first_gain,
    second_gain,
    bias_table,
):
    gathered = gather_together(
        (
            query_weight.astype(jnp.bfloat16),
            key_weight.astype(jnp.bfloat16),
            value_weight.astype(jnp.bfloat16),
            out_weight.astype(jnp.bfloat16),
            gate_weight.astype(jnp.bfloat16),
            up_weight.astype(jnp.bfloat16),
            down_weight.astype(jnp.bfloat16),
            first_gain.astype(jnp.bfloat16),
            second_gain.astype(jnp.bfloat16),
            bias_table.astype(jnp.bfloat16),
        ),
        ("rows", "seq"),
        (0, 0, 0, 0, 0, 0, 0, 0, 0, 0),
    )
    (
        query_full,
        key_full,
        value_full,
        out_full,
        gate_full,
        up_full,
        down_full,
        gain_one,
        gain_two,
        table_full,
    ) = gathered
    table_mat = table_full.reshape(HEADS, BUCKETS)
    row_count, local_len, model_width = tokens.shape
    total_len = local_len * lax.axis_size("seq")
    token_count = row_count * local_len
    head_shape = (row_count, local_len, HEADS, HEAD_DIM)
    block_len = math.gcd(total_len, 1024)
    block_count = total_len // block_len
    block_ids = jnp.arange(block_count, dtype=jnp.int32)
    inputs = tokens.reshape(token_count, model_width).astype(jnp.float32)
    normed, first_pull = jax.vjp(rms_norm, inputs, gain_one.astype(jnp.float32))
    normed_low = normed.astype(jnp.bfloat16)
    queries = jnp.dot(normed_low, query_full, preferred_element_type=jnp.float32).astype(
        jnp.bfloat16
    )
    keys_rows = jnp.dot(normed_low, key_full, preferred_element_type=jnp.float32).astype(
        jnp.bfloat16
    )
    values_rows = jnp.dot(normed_low, value_full, preferred_element_type=jnp.float32).astype(
        jnp.bfloat16
    )
    query_heads = queries.reshape(head_shape)
    keys_all, values_all = sent_together(
        (
            keys_rows.reshape(row_count, local_len, model_width),
            values_rows.reshape(row_count, local_len, model_width),
        ),
        "seq",
        1,
        0,
    )
    query_pos = lax.axis_index("seq") * local_len + jnp.arange(local_len, dtype=jnp.int32)

    def key_slice(source, block_start):
        part_rows = lax.dynamic_slice_in_dim(source, block_start, block_len, 1)
        return part_rows.reshape(row_count, block_len, HEADS, HEAD_DIM)

    def stats_step(state_in, block_index):
        running_max, running_sum = state_in
        block_start = block_index * block_len
        key_at = block_start + jnp.arange(block_len, dtype=jnp.int32)
        scores = block_scores(
            query_heads, key_slice(keys_all, block_start), query_pos, key_at, table_mat, lengths
        )[0]
        new_max = jnp.maximum(running_max, jnp.max(scores, axis=-1))
        new_sum = running_sum * jnp.exp(running_max - new_max) + jnp.sum(
            jnp.exp(scores - new_max[..., None]), axis=-1
        )
        return ((new_max, new_sum), None)

    start_max = jnp.full((row_count, HEADS, local_len), NEGATIVE, jnp.float32)
    start_sum = jnp.zeros((row_count, HEADS, local_len), jnp.float32)
    final_max, final_sum = lax.scan(stats_step, (start_max, start_sum), block_ids)[0]
    log_total = final_max + jnp.log(final_sum)

    pieces = call_mega(
        "fwd", lengths, first_gain, second_gain, bias_table, tokens, cotangent, query_weight,
        key_weight, value_weight, out_weight, gate_weight, up_weight, down_weight
    )[0]
    core = lax.axis_index("seq") % 2
    heads_c = jnp.zeros((2, 256, 384), jnp.bfloat16)
    for k, at in enumerate((0, 64, 192, 256)):
        heads_c = heads_c.at[:, :, at : at + 128].add(pieces[:, :, 128 * k : 128 * k + 128])
    mine = lax.dynamic_slice_in_dim(heads_c, core * 128, 128, 1)
    theirs = lax.dynamic_slice_in_dim(heads_c, (1 - core) * 128, 128, 1)
    came = lax.ppermute(theirs, "seq", [(i, i ^ 1) for i in range(16)])
    attended_low = jnp.concatenate(
        [jnp.where(core == 0, mine, came), jnp.where(core == 0, came, mine)], axis=-1
    ).reshape(token_count, model_width)
    middle = inputs + jnp.dot(attended_low, out_full, preferred_element_type=jnp.float32)
    normed_two, second_pull = jax.vjp(rms_norm, middle, gain_two.astype(jnp.float32))
    normed_two_low = normed_two.astype(jnp.bfloat16)
    gate_act = jnp.dot(normed_two_low, gate_full, preferred_element_type=jnp.float32)
    up_act = jnp.dot(normed_two_low, up_full, preferred_element_type=jnp.float32)
    product, gated_pull = jax.vjp(
        lambda gate_in, up_in: jax.nn.gelu(gate_in, approximate=True) * up_in, gate_act, up_act
    )
    hidden = product.astype(jnp.bfloat16)
    output = middle + jnp.dot(hidden, down_full, preferred_element_type=jnp.float32)
    output_low = output.astype(jnp.bfloat16).reshape(tokens.shape)
    upstream_low = cotangent.reshape(token_count, model_width)
    upstream = upstream_low.astype(jnp.float32)
    down_weight_grad = jnp.einsum(
        "nf,nd->fd", hidden, upstream_low, preferred_element_type=jnp.float32
    )
    hidden_grad = jnp.einsum(
        "nd,fd->nf", upstream_low, down_full, preferred_element_type=jnp.float32
    )
    gate_grad, up_grad = gated_pull(hidden_grad)
    gate_grad_low = gate_grad.astype(jnp.bfloat16)
    up_grad_low = up_grad.astype(jnp.bfloat16)
    gate_weight_grad = jnp.einsum(
        "nd,nf->df", normed_two_low, gate_grad_low, preferred_element_type=jnp.float32
    )
    up_weight_grad = jnp.einsum(
        "nd,nf->df", normed_two_low, up_grad_low, preferred_element_type=jnp.float32
    )
    normed_two_grad = jnp.einsum(
        "nf,df->nd", gate_grad_low, gate_full, preferred_element_type=jnp.float32
    ) + jnp.einsum("nf,df->nd", up_grad_low, up_full, preferred_element_type=jnp.float32)
    middle_norm_grad, second_gain_term = second_pull(normed_two_grad)
    middle_grad = upstream + middle_norm_grad
    middle_low = middle_grad.astype(jnp.bfloat16)
    out_weight_grad = jnp.einsum(
        "nd,ne->de", attended_low, middle_low, preferred_element_type=jnp.float32
    )
    grad_heads = (
        jnp.einsum("ne,de->nd", middle_low, out_full, preferred_element_type=jnp.float32)
        .astype(jnp.bfloat16)
        .reshape(head_shape)
    )
    row_delta = jnp.einsum(
        "rqhd,rqhd->rhq",
        grad_heads,
        attended_low.reshape(head_shape),
        preferred_element_type=jnp.float32,
    )
    full_shape = (row_count, total_len, HEADS, HEAD_DIM)
    table_zero = jnp.zeros((HEADS, BUCKETS), jnp.float32)
    keys_again, values_again = (keys_all, values_all)

    def key_step(state_in, block_index):
        query_acc, table_acc, key_terms, value_terms = state_in
        block_start = block_index * block_len
        key_at = block_start + jnp.arange(block_len, dtype=jnp.int32)
        key_part = key_slice(keys_again, block_start)
        value_part = key_slice(values_again, block_start)
        scores, bucket_of = block_scores(
            query_heads, key_part, query_pos, key_at, table_mat, lengths
        )
        probs = jnp.exp(scores - log_total[..., None])
        probs_low = probs.astype(jnp.bfloat16)
        value_term = jnp.einsum(
            "rhqk,rqhd->rkhd", probs_low, grad_heads, preferred_element_type=jnp.float32
        )
        prob_grad = jnp.einsum(
            "rqhd,rkhd->rhqk", grad_heads, value_part, preferred_element_type=jnp.float32
        )
        score_grad = probs * (prob_grad - row_delta[..., None])
        score_low = score_grad.astype(jnp.bfloat16)
        query_acc = query_acc + jnp.einsum(
            "rhqk,rkhd->rqhd", score_low, key_part, preferred_element_type=jnp.float32
        )
        key_term = jnp.einsum(
            "rhqk,rqhd->rkhd", score_low, query_heads, preferred_element_type=jnp.float32
        )
        table_acc = table_acc + table_term(score_grad, bucket_of)
        key_terms = lax.dynamic_update_slice_in_dim(key_terms, key_term, block_start, 1)
        value_terms = lax.dynamic_update_slice_in_dim(value_terms, value_term, block_start, 1)
        return ((query_acc, table_acc, key_terms, value_terms), None)

    start_state = (
        jnp.zeros(head_shape, jnp.float32),
        table_zero,
        jnp.zeros(full_shape, jnp.float32),
        jnp.zeros(full_shape, jnp.float32),
    )
    query_grad, table_grad, key_terms, value_terms = lax.scan(key_step, start_state, block_ids)[0]
    key_grad, value_grad = in_one_piece(
        (
            key_terms.reshape(row_count, total_len, model_width),
            value_terms.reshape(row_count, total_len, model_width),
        ),
        "seq",
        1,
        0,
    )
    query_low = query_grad.reshape(token_count, model_width).astype(jnp.bfloat16)
    key_low = key_grad.reshape(token_count, model_width).astype(jnp.bfloat16)
    value_low = value_grad.reshape(token_count, model_width).astype(jnp.bfloat16)
    query_weight_grad = jnp.einsum(
        "nd,ne->de", normed_low, query_low, preferred_element_type=jnp.float32
    )
    key_weight_grad = jnp.einsum(
        "nd,ne->de", normed_low, key_low, preferred_element_type=jnp.float32
    )
    value_weight_grad = jnp.einsum(
        "nd,ne->de", normed_low, value_low, preferred_element_type=jnp.float32
    )
    normed_grad = jnp.einsum("ne,de->nd", query_low, query_full, preferred_element_type=jnp.float32)
    normed_grad = normed_grad + jnp.einsum(
        "ne,de->nd", key_low, key_full, preferred_element_type=jnp.float32
    )
    normed_grad = normed_grad + jnp.einsum(
        "ne,de->nd", value_low, value_full, preferred_element_type=jnp.float32
    )
    input_norm_grad, first_gain_term = first_pull(normed_grad)
    input_grad = (middle_grad + input_norm_grad).reshape(tokens.shape)
    summed = sum_packed(
        (
            query_weight_grad,
            key_weight_grad,
            value_weight_grad,
            out_weight_grad,
            gate_weight_grad,
            up_weight_grad,
            down_weight_grad,
            first_gain_term,
            second_gain_term,
            table_grad.reshape(HEADS * BUCKETS),
        ),
        ("rows", "seq"),
        (0, 0, 0, 0, 0, 0, 0, 0, 0, 0),
    )
    return (
        output_low,
        input_grad,
        summed[0],
        summed[1],
        summed[2],
        summed[3],
        summed[4],
        summed[5],
        summed[6],
        summed[7],
        summed[8],
        summed[9],
    )


def solution(mesh):
    in_specs = (
        P("rows", "seq", None),
        P("rows"),
        P("rows", "seq", None),
        P(("rows", "seq"), None),
        P(("rows", "seq"), None),
        P(("rows", "seq"), None),
        P(("rows", "seq"), None),
        P(("rows", "seq"), None),
        P(("rows", "seq"), None),
        P(("rows", "seq"), None),
        P(("rows", "seq")),
        P(("rows", "seq")),
        P(("rows", "seq")),
    )
    out_specs = (
        P("rows", "seq", None),
        P("rows", "seq", None),
        P(("rows", "seq"), None),
        P(("rows", "seq"), None),
        P(("rows", "seq"), None),
        P(("rows", "seq"), None),
        P(("rows", "seq"), None),
        P(("rows", "seq"), None),
        P(("rows", "seq"), None),
        P(("rows", "seq")),
        P(("rows", "seq")),
        P(("rows", "seq")),
    )
    return jax.shard_map(
        per_device, mesh=mesh, in_specs=in_specs, out_specs=out_specs, check_vma=False
    )
```

```python
import functools

import jax
import jax.numpy as jnp
from jax import lax
from jax.experimental import pallas as pl
from jax.experimental.pallas import tpu as pltpu
from jax.sharding import PartitionSpec as P

MESH = pl.DeviceIdType.MESH
BF = jnp.bfloat16
F32 = jnp.float32
D = 768
SEQ = 2048
EPSILON = 1e-06
NEGATIVE = -1e30
LIMITS = (1, 2, 3, 4, 5, 6, 7, 8, 12, 16, 23, 32, 46, 64, 91)
NSEM = 400
BQ = 256
STEPS = 12


def dev(x, y, z, c):
    return ((z % 2) * 4 + x, (y * 2 + z // 2) * 2 + c)


def first_head(t):
    return (3 * t) // 2


def iota(shape, dim):
    return lax.broadcasted_iota(jnp.int32, shape, dim)


def dot(a, b):
    return jnp.dot(a, b, preferred_element_type=F32)


def dot_nt(a, b):
    return lax.dot_general(a, b, (((1,), (1,)), ((), ())), preferred_element_type=F32)


class Comm:
    def __init__(self, x, y, z, c, send_sem, recv_sem):
        self.x, self.y, self.z, self.c = x, y, z, c
        self.ss, self.rs = send_sem, recv_sem
        self.next = 0
        self.pending = []

    def take(self, n=1):
        at = self.next
        self.next += n
        assert self.next <= NSEM
        return at

    def peer(self, axis, offset):
        x, y, z, c = self.x, self.y, self.z, self.c
        if axis == "x":
            return dev((x + offset) % 4, y, z, c)
        if axis == "y":
            return dev(x, (y + offset) % 4, z, c)
        if axis == "z":
            return dev(x, y, (z + offset) % 4, c)
        return dev(x, y, z, 1 - c)

    def place(self, axis, offset):
        at = {"x": self.x, "y": self.y, "z": self.z}[axis]
        return (at + offset) % 4

    def copy(self, src, dst, i, to, j=None):
        return pltpu.make_async_remote_copy(
            src_ref=src,
            dst_ref=dst,
            send_sem=self.ss.at[i],
            recv_sem=self.rs.at[i if j is None else j],
            device_id=to,
            device_id_type=MESH,
        )

    def send(self, src, dst, i, to):
        cp = self.copy(src, dst, i, to)
        cp.start()
        self.pending.append(cp)

    def recv(self, dst, i):
        self.copy(dst, dst, i, self.peer("c", 0)).wait_recv()

    def send_or_keep(self, src, dst, i, to, j, own):
        cp = self.copy(src, dst, i, to, j)
        keep = pltpu.make_async_copy(src, dst, self.rs.at[j])

        @pl.when(own)
        def _():
            keep.start()

        @pl.when(jnp.logical_not(own))
        def _():
            cp.start()

        self.pending.append((cp, own))

    def drain(self):
        for cp in self.pending:
            if isinstance(cp, tuple):
                cp, own = cp

                @pl.when(jnp.logical_not(own))
                def _():
                    cp.wait_send()
            else:
                cp.wait_send()
        self.pending = []


class Direct:
    def __init__(self, comm, axis, views):
        self.comm, self.axis, self.views = comm, axis, views
        self.count = len(views(comm.place(axis, 0)))
        self.base = comm.take(3 * self.count)

    def start(self):
        for k, off in enumerate((1, 3, 2)):
            for n, ref in enumerate(self.views(self.comm.place(self.axis, 0))):
                self.comm.send(ref, ref, self.base + k * self.count + n, self.comm.peer(self.axis, off))

    def wait(self):
        for k, off in enumerate((1, 3, 2)):
            for n, ref in enumerate(self.views(self.comm.place(self.axis, -off + 4))):
                self.comm.recv(ref, self.base + k * self.count + n)


class Ring:
    def __init__(self, comm, axis, views, halves):
        self.comm, self.axis, self.views, self.halves = comm, axis, views, halves
        self.count = len(views(comm.place(axis, 0)))
        self.base = comm.take(4 * self.count)

    def start(self, source=None):
        own = self.views(self.comm.place(self.axis, 0))
        for n, ref in enumerate(own):
            src = ref if source is None else source[n]
            for k, off in enumerate((1, 3)):
                self.comm.send(src, ref, self.base + k * self.count + n, self.comm.peer(self.axis, off))

    def forward(self):
        for k, off in enumerate((1, 3)):
            came = self.comm.place(self.axis, -off + 4)
            for n, ref in enumerate(self.views(came)):
                self.comm.recv(ref, self.base + k * self.count + n)
            for n, ref in enumerate(self.halves(came, k)):
                self.comm.send(ref, ref, self.base + (2 + k) * self.count + n, self.comm.peer(self.axis, off))

    def wait(self):
        far = self.comm.place(self.axis, 2)
        for k in range(2):
            for n, ref in enumerate(self.halves(far, k)):
                self.comm.recv(ref, self.base + (2 + k) * self.count + n)


class Scatter:
    def __init__(self, comm, axis, views, bufs):
        self.comm, self.axis, self.views, self.bufs = comm, axis, views, bufs
        self.base = comm.take(3 * len(bufs))

    def start(self):
        for k, off in enumerate((1, 3, 2)):
            refs = self.views(self.comm.place(self.axis, off))
            for n, ref in enumerate(refs):
                self.comm.send(
                    ref, self.bufs[n].at[k], self.base + k * len(refs) + n, self.comm.peer(self.axis, off)
                )

    def wait(self):
        for k in range(3):
            for n, buf in enumerate(self.bufs):
                self.comm.recv(buf.at[k], self.base + k * len(self.bufs) + n)


def bucket_ids(offsets):
    distance = jnp.abs(offsets)
    bucket_sum = jnp.where(offsets > 0, 16, 0)
    for threshold in LIMITS:
        bucket_sum = bucket_sum + jnp.where(distance >= threshold, 1, 0)
    return bucket_sum


def rms_scale(values):
    return lax.rsqrt(jnp.mean(values * values, axis=-1, keepdims=True) + EPSILON)


def greet(comm):
    x, y, z, c = comm.x, comm.y, comm.z, comm.c
    zl, zh = z % 2, z // 2
    barrier = pltpu.get_barrier_semaphore()
    count = 0
    peers = []
    for dy in range(4):
        for dh in range(2):
            for dc in range(2):
                if dy or dh or dc:
                    peers.append(dev(x, (y + dy) % 4, ((zh + dh) % 2) * 2 + zl, (c + dc) % 2))
    for off in (1, 2, 3):
        peers.append(comm.peer("x", off))
    for off in (1, 3):
        peers.append(comm.peer("z", off))
    for peer in peers:
        pl.semaphore_signal(barrier, inc=1, device_id=peer, device_id_type=MESH)
        count += 1
    return barrier, count


def cast_up(v):
    return v.astype(F32)


def head_bias(tables, o):
    return tables[o : o + 1, 0:1], tables[o : o + 1, 1023:1024]


def mega(stop, *refs):
    names = [n for n, _ in INPUTS] + [n for n, _ in outputs_of(stop)] + [n for n, _ in SCRATCH]
    r = dict(zip(names, refs))
    rows, seq = lax.axis_index("rows"), lax.axis_index("seq")
    x, y, zl, zh, c = rows % 4, seq // 4, rows // 4, (seq // 2) % 2, seq % 2
    z = zh * 2 + zl
    flat = rows * 16 + seq
    t = c * 4 + y
    comm = Comm(x, y, z, c, r["send_sem"], r["recv_sem"])
    barrier, count = greet(comm)

    lanes = iota((1, 1024), 1)
    first_row = jnp.zeros((1, 1024), F32)
    second_row = jnp.zeros((1, 1024), F32)
    for i in range(6):
        first_row += jnp.where(lanes == 6 * flat + i, r["g1"][i], 0.0)
        second_row += jnp.where(lanes == 6 * flat + i, r["g2"][i], 0.0)
    for i in range(3):
        at = 768 + 3 * flat + i
        first_row += jnp.where(lanes == at, r["bt"][i], 0.0)
        second_row += jnp.where((lanes >= 768) & (lanes == at - 256), r["bt"][i], 0.0)
    first_row = cast_up(first_row.astype(BF))
    second_row = cast_up(second_row.astype(BF))
    wst, w0 = r["wst"], r["w0"]
    for cc in range(2):
        for yy in range(4):
            d, h0 = cc * 4 + yy, first_head(cc * 4 + yy)
            for i, name in enumerate(("wq", "wk", "wv")):
                wst[d, 0:6, 128 * i : 128 * (i + 1)] = r[name][:, 64 * h0 : 64 * h0 + 128]
            for i, name in enumerate(("wg", "wu")):
                for k in range(2):
                    tile = 2 * (2 * yy + k) + cc
                    at = 384 + 256 * i + 128 * k
                    wst[d, 0:6, at : at + 128] = r[name][:, 128 * tile : 128 * tile + 128]
            if yy < 3:
                at = (cc * 3 + yy) * 128
                wst[d, 0:6, 896:1024] = r["wo"][:, at : at + 128]
            else:
                wst[d, 0:6, 896:1024] = jnp.zeros((6, 128), F32)
            wst[d, 6:7, :] = first_row
            wst[d, 7:8, :] = second_row
    r["wdst"][...] = r["wd"][...].astype(BF)

    pl.semaphore_wait(barrier, count)

    W1, WD, WQ, G5 = r["W1"], r["WD"], r["WQ"], r["G5"]
    T5, TK, CT, tok, cot = r["T5"], r["TK"], r["CT"], r["tok"], r["cot"]
    slot = (y % 2) * 4 + zh * 2 + c
    base0 = comm.take(8)
    baser = comm.take(8)
    for cc in range(2):
        for yy in range(4):
            to = dev(x, yy, (y // 2) * 2 + zl, cc)
            own = (y == yy) & (c == cc) & (zh == y // 2)
            cp = comm.copy(wst.at[cc * 4 + yy], w0.at[slot], base0 + cc * 4 + yy, to, baser + slot)
            keep = pltpu.make_async_copy(wst.at[cc * 4 + yy], w0.at[slot], comm.rs.at[baser + slot])
            pl.when(own)(keep.start)
            pl.when(jnp.logical_not(own))(cp.start)
            comm.pending.append((cp, own))
    wd_to = (zh * 2 + c, y % 2, y // 2)
    own_wd = (wd_to[0] == y) & (wd_to[1] == zh) & (wd_to[2] == c)
    wdi = comm.take()
    wd_region = WD.at[zl, x, wd_to[1], pl.ds(16 * wd_to[0], 16)]
    comm.send_or_keep(
        r["wdst"], wd_region, wdi, dev(x, wd_to[0], wd_to[1] * 2 + zl, wd_to[2]), wdi, own_wd
    )

    other = comm.peer("z", 2)
    zi = comm.take()
    comm.send(tok.at[1 - zh], T5.at[y, zh, c], zi, other)
    own_tokens = Ring(
        comm,
        "y",
        lambda yy: [T5.at[yy, zh, c]],
        lambda yy, k: [T5.at[yy, zh, c, pl.ds(64 * k, 64)]],
    )
    own_tokens.start(source=[tok.at[zh]])
    local = comm.take(3)
    keep_tokens = pltpu.make_async_copy(tok.at[zh], T5.at[y, zh, c], comm.ss.at[local])
    keep_tokens.start()
    keep_tk = pltpu.make_async_copy(tok, TK.at[:, c], comm.ss.at[local + 1])
    keep_tk.start()
    keep_ct = pltpu.make_async_copy(cot, CT.at[:, c], comm.ss.at[local + 2])
    keep_ct.start()
    pair = comm.take(2)

    for j in range(8):
        comm.recv(w0.at[j], baser + j)
    asm = r["asm"]
    gsum = jnp.zeros((2, 1024), F32)
    for j in range(8):
        asm[6 * j : 6 * j + 6, :] = w0[j, 0:6, :]
        gsum += w0[j, 6:8, :]
    WQ[zl, x, zh] = asm[:, 0:384].astype(BF)
    G5[zl, x, zh] = jnp.concatenate([gsum, jnp.zeros((6, 1024), F32)], axis=0)
    W1[zl, x, zh, :, pl.ds(pl.multiple_of(640 * y, 128), 640)] = asm[:, 384:1024].astype(BF)
    qkv_a1 = Direct(comm, "x", lambda xx: [WQ.at[zl, xx, zh, :, pl.ds(0, 256)], G5.at[zl, xx, zh]])
    qkv_b1 = Direct(comm, "z", lambda zz: [WQ.at[zz % 2, x, zz // 2, :, pl.ds(256, 128)]])
    qkv_a1.start()
    qkv_b1.start()
    comm.recv(WD.at[zl, x, zh, pl.ds(16 * y, 16)], wdi)
    ff_y = Direct(
        comm,
        "y",
        lambda yy: [
            W1.at[zl, x, zh, :, pl.ds(pl.multiple_of(640 * yy, 128), 640)],
            WD.at[zl, x, zh, pl.ds(16 * yy, 16)],
        ],
    )
    ff_y.start()

    comm.recv(T5.at[y, 1 - zh, c], zi)
    far_tokens = Ring(
        comm,
        "y",
        lambda yy: [T5.at[yy, 1 - zh, c]],
        lambda yy, k: [T5.at[yy, 1 - zh, c, pl.ds(64 * k, 64)]],
    )
    far_tokens.start()
    keep_tokens.wait()
    sib = comm.peer("c", 0)
    across = comm.take(4)

    def cross(k):
        yy = (y + (0, 1, 3, 2)[k]) % 4
        comm.send(T5.at[yy, :, c], T5.at[yy, :, c], across + k, sib)

    def crossed(k):
        yy = (y + (0, 1, 3, 2)[k]) % 4
        comm.recv(T5.at[yy, :, 1 - c], across + k)

    cross(0)
    own_tokens.forward()
    qkv_a1.wait()
    qkv_b1.wait()
    qkv_a2 = Direct(
        comm,
        "z",
        lambda zz: [WQ.at[zz % 2, :, zz // 2, :, pl.ds(0, 256)], G5.at[zz % 2, :, zz // 2]],
    )
    qkv_b2 = Direct(comm, "x", lambda xx: [WQ.at[:, xx, :, :, pl.ds(256, 128)]])
    qkv_a2.start()
    qkv_b2.start()
    far_tokens.forward()
    cross(1)
    cross(2)
    ff_y.wait()
    ff_a1 = Direct(
        comm,
        "x",
        lambda xx: [WO_A(W1.at[zl, xx, zh]), WD.at[zl, xx, zh, :, pl.ds(0, 384)]],
    )
    ff_b1 = Direct(
        comm,
        "z",
        lambda zz: [
            W1.at[zz % 2, x, zz // 2, :, pl.ds(1280, 1280)],
            WD.at[zz % 2, x, zz // 2, :, pl.ds(384, 384)],
        ],
    )
    ff_a1.start()
    ff_b1.start()
    own_tokens.wait()
    far_tokens.wait()
    cross(3)
    keep_tk.wait()
    keep_ct.wait()
    comm.send(TK.at[:, c], TK.at[:, c], pair, sib)
    comm.send(CT.at[:, c], CT.at[:, c], pair + 1, sib)

    qkv_a2.wait()
    qkv_b2.wait()
    total = jnp.zeros((8, 1024), F32)
    for a in range(2):
        for b in range(4):
            for e in range(2):
                total += G5[a, b, e]
    r["GS"][...] = total
    h0 = first_head(t)
    table_row = jnp.concatenate([total[0:1, 768:1024], total[1:2, 768:896]], axis=1)
    table_row = jnp.broadcast_to(table_row, (8, 384))
    table_row = pltpu.roll(table_row, 384 - 32 * h0, 1)[:, 0:128]
    lane = iota((8, 128), 1)
    sub = iota((8, 128), 0)
    table_two = jnp.where((lane // 32) == sub, table_row, 0.0).astype(BF)
    r["OH"][...] = jnp.where(
        bucket_ids(iota((128, 1024), 1) - 512) == iota((128, 1024), 0) % 32, 1.0, 0.0
    ).astype(BF)
    by_offset = dot(table_two, r["OH"][...])
    r["BO"][...] = by_offset
    for h in range(2):
        for k in range(4):
            rolled = pltpu.roll(
                jnp.broadcast_to(by_offset[h : h + 1, :], (64, 1024)), 640 + 64 * k, 1, stride=1, stride_axis=0
            )
            r["BT"][h, 64 * k : 64 * k + 64, :] = rolled[:, 0:512]

    for k in range(4):
        crossed(k)
    QA, KT, KN, VN, VT = r["QA"], r["KT"], r["KN"], r["VN"], r["VT"]
    row_len = r["lens"][zh]

    def project(i, carry):
        raw = cast_up(T5[i // 2, i % 2].reshape(256, D))
        normed = (raw * rms_scale(raw) * r["GS"][0:1, 0:768]).astype(BF)
        res = dot(normed, WQ[...].reshape(D, 384))
        q, k_, v = res[:, 0:128], res[:, 128:256], res[:, 256:384]
        at = pl.ds(pl.multiple_of(i * 256, 256), 256)
        KN[at, :] = k_.astype(BF)
        VN[at, :] = v.astype(BF)
        VT[:, at] = v.T.astype(BF)
        kt = k_.T
        lane = iota((256, 128), 1)
        sub = iota((128, 256), 0)
        key_at = i * 256 + iota((128, 256), 1)
        for h in range(2):
            base = 64 * (1 - h)
            hot = jnp.where((lane == base + i) | (lane == base + 8), 1.0, 0.0)
            QA[h, at, :] = jnp.where(lane // 64 == h, q, hot).astype(BF)
            left, right = head_bias(r["BO"][...], h)
            start = 256 * (sub - base)
            extra = jnp.where(key_at < start - 128, left, 0.0) + jnp.where(
                key_at >= start + 384, right, 0.0
            )
            masked = jnp.where(key_at >= row_len, NEGATIVE, 0.0)
            extra = jnp.where(sub - base < 8, extra, jnp.where(sub - base == 8, masked, 0.0))
            KT[h, :, at] = jnp.where(sub // 64 == h, kt, extra).astype(BF)
        return carry

    lax.fori_loop(0, 8, project, 0)
    r["ON"][...] = jnp.zeros((SEQ, 128), BF)
    r["LI"][...] = jnp.zeros((BQ, 128), F32)

    SC, PB, BT, ON, LI = r["SC"], r["PB"], r["BT"], r["ON"], r["LI"]

    def unit_of(step):
        ui = step // 4
        u = jnp.where(ui == 0, 1, jnp.where(ui == 1, 0, 2))
        number = 3 * t + u
        head = number // 2 - h0
        start = (number % 2) * 1024 + (step % 4) * 256
        return head, pl.multiple_of(start, 256)

    def attend(step, carry):
        head, q0 = unit_of(step)
        qa = QA[head, pl.ds(q0, BQ), :]
        for j in range(8):
            SC[:, 128 + 256 * j : 384 + 256 * j] = dot(qa, KT[head, :, 256 * j : 256 * j + 256])
        SC[:, pl.ds(q0, 512)] = SC[:, pl.ds(q0, 512)] + BT[head]
        top = SC[:, 128:256]
        for j in range(2, 17):
            top = jnp.maximum(top, SC[:, 128 * j : 128 * j + 128])
        top = jnp.max(top, axis=1, keepdims=True)
        sums = jnp.zeros((BQ, 128), F32)
        for j in range(16):
            p = jnp.exp(SC[:, 128 + 128 * j : 256 + 128 * j] - top)
            sums += p
            PB[step, :, 128 * j : 128 * j + 128] = p.astype(BF)
        inv = 1.0 / jnp.sum(sums, axis=1, keepdims=True)
        lane = iota((BQ, 128), 1)
        LI[...] = jnp.where(lane == step, inv, LI[...])
        mixed = dot(PB[step], VN[...]) * inv
        ON[pl.ds(q0, BQ), :] = jnp.where(lane // 64 == head, mixed, cast_up(ON[pl.ds(q0, BQ), :])).astype(BF)
        return carry

    A = r["A"]
    base_o = comm.take(8)
    base_or = comm.take(8)

    def give(half, n):
        for i in range(4):
            yy, hh = 2 * half + i // 2, i % 2
            src = ON.at[pl.ds(pl.multiple_of(256 * (yy * 2 + hh), 256), 256)]
            dst = A.at[zh, :, pl.ds(pl.multiple_of(128 * y, 128), 128)]
            own = (yy == y) & (hh == zh)
            cp = comm.copy(src, dst, base_o + 4 * n + i, dev(x, yy, hh * 2 + zl, c), base_or + y * 2 + zh)
            keep = pltpu.make_async_copy(src, dst, comm.rs.at[base_or + y * 2 + zh])
            pl.when(own)(keep.start)
            pl.when(jnp.logical_not(own))(cp.start)
            comm.pending.append((cp, own))

    single = (3 * t + 1) % 2
    lax.fori_loop(0, 2, attend, 0)
    ff_a1.wait()
    ff_b1.wait()
    ff_a2 = Ring(
        comm,
        "z",
        lambda zz: [
            W1.at[zz % 2, :, zz // 2, :, pl.ds(0, 1280)],
            WD.at[zz % 2, :, zz // 2, :, pl.ds(0, 384)],
        ],
        lambda zz, k: [
            W1.at[zz % 2, pl.ds(2 * k, 2), zz // 2, :, pl.ds(0, 1280)],
            WD.at[zz % 2, pl.ds(2 * k, 2), zz // 2, :, pl.ds(0, 384)],
        ],
    )
    ff_b2 = Ring(
        comm,
        "x",
        lambda xx: [
            W1.at[:, xx, :, :, pl.ds(1280, 1280)],
            WD.at[:, xx, :, :, pl.ds(384, 384)],
        ],
        lambda xx, k: [
            W1.at[k, xx, :, :, pl.ds(1280, 1280)],
            WD.at[k, xx, :, :, pl.ds(384, 384)],
        ],
    )
    ff_a2.start()
    ff_b2.start()
    lax.fori_loop(2, 4, attend, 0)
    give(single, 0)
    lax.fori_loop(4, 9, attend, 0)
    ff_a2.forward()
    ff_b2.forward()
    lax.fori_loop(9, STEPS, attend, 0)
    give(1 - single, 1)
    ff_a2.wait()
    ff_b2.wait()
    for yy in range(4):
        for hh in range(2):
            comm.recv(A.at[hh, :, pl.ds(128 * yy, 128)], base_or + yy * 2 + hh)
    comm.recv(TK.at[:, 1 - c], pair)
    comm.recv(CT.at[:, 1 - c], pair + 1)
    comm.drain()

    WOF = r["WOF"]
    base_w = comm.take(3)
    keeps = []
    for yy in range(3):
        cols = pl.ds(pl.multiple_of((c * 3 + yy) * 128, 128), 128)
        piece = pl.ds(640 * yy + 512, 128)
        comm.send(W1.at[1 - c, :, :, :, piece], WOF.at[:, :, :, cols], base_w + yy, sib)
        keep = pltpu.make_async_copy(
            W1.at[c, :, :, :, piece], WOF.at[:, :, :, cols], comm.ss.at[comm.take()]
        )
        keep.start()
        keeps.append(keep)
    lane = iota((256, 128), 1)
    for hh in range(2):
        p0, p1, p2, p3 = [cast_up(A[hh, :, 128 * k : 128 * k + 128]) for k in range(4)]
        p1, p2 = pltpu.roll(p1, 64, 1), pltpu.roll(p2, 64, 1)
        A[hh, :, 0:128] = (p0 + jnp.where(lane >= 64, p1, 0.0)).astype(BF)
        A[hh, :, 128:256] = jnp.where(lane < 64, p1, p2).astype(BF)
        A[hh, :, 256:384] = (p3 + jnp.where(lane < 64, p2, 0.0)).astype(BF)
    for keep in keeps:
        keep.wait()
    for yy in range(3):
        cols = pl.ds(pl.multiple_of(((1 - c) * 3 + yy) * 128, 128), 128)
        comm.recv(WOF.at[:, :, :, cols], base_w + yy)

    POS, POR, MID, N2, N2T = r["POS"], r["POR"], r["MID"], r["N2"], r["N2T"]
    base_p = comm.take(2)
    for hh in range(2):
        term = dot(A[hh, :, 0:384], WOF[...].reshape(384, D))
        POS[hh] = term.astype(BF).reshape(2, 128, D)
        comm.send(POS.at[hh], POR.at[hh], base_p + hh, sib)
    second_gain = r["GS"][1:2, 0:768]
    for hh in range(2):
        comm.recv(POR.at[hh], base_p + hh)
        for k in range(2):
            middle = cast_up(TK[hh, k]) + (cast_up(POS[hh, k]) + cast_up(POR[hh, k]))
            MID[2 * hh + k] = middle
            normed = middle * rms_scale(middle) * second_gain
            N2[128 * k : 128 * k + 128, 768 * hh : 768 * hh + 768] = normed.astype(BF)
            at = 256 * hh + 128 * k
            N2T[:, at : at + 128] = normed.T.astype(BF)

    HX, HIDT, GU = r["HX"], r["HIDT"], r["GU"]

    def gated(k, carry):
        at = pl.multiple_of(640 * k, 128)
        gate_w = W1[:, :, :, :, pl.ds(at, 256)].reshape(D, 256)
        up_w = W1[:, :, :, :, pl.ds(at + 256, 256)].reshape(D, 256)
        down_w = WD[k // 2, pl.ds((2 * k) % 4, 2)].reshape(256, D)
        for hh in range(2):
            gate = dot(N2[:, 768 * hh : 768 * hh + 768], gate_w)
            up = dot(N2[:, 768 * hh : 768 * hh + 768], up_w)
            back = dot_nt(CT[hh].reshape(256, D), down_w)
            square = gate * gate
            th = jnp.tanh(0.7978845608028654 * (gate + 0.044715 * (square * gate)))
            half = 0.5 * (1.0 + th)
            gelu = gate * half
            slope = half + (0.5 * gate) * (1.0 - th * th) * (
                0.7978845608028654 * (1.0 + 3 * 0.044715 * square)
            )
            hidden = gelu * up
            cols = pl.ds(pl.multiple_of(256 * k, 256), 256)
            HX[:, pl.ds(pl.multiple_of(1024 * hh + 256 * k, 256), 256)] = hidden.astype(BF)
            HIDT[cols, 256 * hh : 256 * hh + 256] = hidden.T.astype(BF)
            both = pl.multiple_of(512 * k, 512)
            GU[hh, :, :, pl.ds(both, 256)] = (back * up * slope).astype(BF).reshape(2, 128, 256)
            GU[hh, :, :, pl.ds(both + 256, 256)] = (back * gelu).astype(BF).reshape(2, 128, 256)
        return carry

    lax.fori_loop(0, 4, gated, 0)
    PNR, SC = r["PNR"], r["SC"]
    base_n = comm.take(2)
    comm.drain()
    for hh in range(2):
        term = dot_nt(GU[hh, :, :, 0:512].reshape(256, 512), W1[:, :, :, :, 0:512].reshape(D, 512))
        for k in range(1, 4):
            term += dot_nt(
                GU[hh, :, :, 512 * k : 512 * k + 512].reshape(256, 512),
                W1[:, :, :, :, 640 * k : 640 * k + 512].reshape(D, 512),
            )
        POS[hh] = term.astype(BF).reshape(2, 128, D)
        comm.send(POS.at[hh], PNR.at[hh], base_n + hh, sib)
    PYS, PYR = r["PYS"], r["PYR"]
    yi = comm.take()
    down_all = WD[...].reshape(1024, D)
    for hh in range(2):
        PYS[hh] = dot(HX[pl.ds(pl.multiple_of(128 * (1 - c), 128), 128), 1024 * hh : 1024 * hh + 1024], down_all).astype(BF)
    comm.send(PYS, PYR, yi, sib)
    for hh in range(2):
        SC[128 * hh : 128 * hh + 128, 0:768] = dot(HX[pl.ds(pl.multiple_of(128 * c, 128), 128), 1024 * hh : 1024 * hh + 1024], down_all)

    ML, DOS, DO, VEC = r["ML"], r["DOS"], r["DO"], r["VEC"]
    VEC[...] = jnp.zeros((8, 1024), F32)
    base_d = comm.take(8)
    base_dr = comm.take(8)
    m = y * 2 + zh
    for hh in range(2):
        comm.recv(PNR.at[hh], base_n + hh)
        for k in range(2):
            grad = cast_up(POS[hh, k]) + cast_up(PNR[hh, k])
            middle = MID[2 * hh + k]
            scale = rms_scale(middle)
            gained = grad * second_gain
            mean = jnp.mean(middle * gained, axis=-1, keepdims=True)
            full = cast_up(CT[hh, k]) + scale * gained - middle * (scale * scale * scale * mean)
            ML[hh, k] = full.astype(BF)

            @pl.when(c == k)
            def _():
                r["din"][hh] = full
                VEC[1:2, 0:768] += jnp.sum(grad * middle * scale, axis=0, keepdims=True)

        given = dot_nt(ML[hh].reshape(256, D), WOF[...].reshape(384, D))
        g0, g1, g2 = given[:, 0:128], given[:, 128:256], given[:, 256:384]
        r0, r1, r2 = pltpu.roll(g0, 64, 1), pltpu.roll(g1, 64, 1), pltpu.roll(g2, 64, 1)
        DOS[0, hh] = g0.astype(BF)
        DOS[1, hh] = jnp.where(lane < 64, r0, r1).astype(BF)
        DOS[2, hh] = jnp.where(lane < 64, r1, r2).astype(BF)
        DOS[3, hh] = g2.astype(BF)
        for yy in range(4):
            dst = DO.at[pl.ds(pl.multiple_of(256 * m, 256), 256)]
            own = (yy == y) & (hh == zh)
            cp = comm.copy(DOS.at[yy, hh], dst, base_d + 4 * hh + yy, dev(x, yy, hh * 2 + zl, c), base_dr + m)
            keep = pltpu.make_async_copy(DOS.at[yy, hh], dst, comm.rs.at[base_dr + m])
            pl.when(own)(keep.start)
            pl.when(jnp.logical_not(own))(cp.start)
            comm.pending.append((cp, own))

    def down_term(k, carry):
        res = dot(HIDT[pl.ds(pl.multiple_of(256 * k, 256), 256), :], CT[...].reshape(512, D))
        WD[k // 2, pl.ds((2 * k) % 4, 2)] = res.astype(BF).reshape(2, 2, 64, D)
        return carry

    lax.fori_loop(0, 4, down_term, 0)

    def gated_term(k, carry):
        res = dot(N2T[...], GU[:, :, :, pl.ds(pl.multiple_of(512 * k, 512), 512)].reshape(512, 512))
        at = pl.multiple_of(640 * k, 128)
        W1[:, :, :, :, pl.ds(at, 512)] = res.astype(BF).reshape(2, 4, 2, 48, 512)
        return carry

    lax.fori_loop(0, 4, gated_term, 0)
    attended_t = jnp.concatenate(
        [cast_up(A[hh, :, 0:384]).T.astype(BF) for hh in range(2)], axis=1
    )
    WOF[...] = dot(attended_t, ML[...].reshape(512, D)).astype(BF).reshape(4, 2, 48, D)
    base_g = comm.take(3)
    keeps = []
    for yy in range(3):
        piece = pl.ds(640 * yy + 512, 128)
        own_cols = pl.ds(pl.multiple_of((c * 3 + yy) * 128, 128), 128)
        sib_cols = pl.ds(pl.multiple_of(((1 - c) * 3 + yy) * 128, 128), 128)
        comm.send(WOF.at[:, :, :, sib_cols], W1.at[c, :, :, :, piece], base_g + yy, sib)
        keep = pltpu.make_async_copy(
            WOF.at[:, :, :, own_cols], W1.at[c, :, :, :, piece], comm.ss.at[comm.take()]
        )
        keep.start()
        keeps.append(keep)
    for keep in keeps:
        keep.wait()
    for yy in range(3):
        comm.recv(W1.at[1 - c, :, :, :, pl.ds(640 * yy + 512, 128)], base_g + yy)
    low, high = pl.ds(0, 1280), pl.ds(1280, 1280)
    low_d, high_d = pl.ds(0, 384), pl.ds(384, 384)
    ff_ra = Scatter(
        comm,
        "z",
        lambda zz: [W1.at[zz % 2, :, zz // 2, :, low], WD.at[zz % 2, :, zz // 2, :, low_d]],
        [r["RA1"], r["RA2"]],
    )
    ff_rb = Scatter(
        comm,
        "x",
        lambda xx: [W1.at[:, xx, :, :, high], WD.at[:, xx, :, :, high_d]],
        [r["RB1"], r["RB2"]],
    )
    ff_ra.start()
    ff_rb.start()
    comm.recv(PYR, yi)
    for hh in range(2):
        middle = MID[pl.ds(2 * hh + c, 1)].reshape(128, D)
        r["out"][hh] = (middle + SC[128 * hh : 128 * hh + 128, 0:768] + cast_up(PYR[hh])).astype(BF)

    DS, DVT = r["HX"], r["DVT"]
    DS[...] = jnp.zeros((BQ, 2304), BF)
    SC[:, 0:2048] = jnp.zeros((256, SEQ), F32)
    DVT[...] = jnp.zeros((128, SEQ), F32)
    N2[:, 0:1024] = jnp.zeros((BQ, 1024), BF)
    BT[...] = jnp.zeros((2, 256, 512), F32)
    for yy in range(4):
        for hh in range(2):
            comm.recv(DO.at[pl.ds(256 * (yy * 2 + hh), 256)], base_dr + yy * 2 + hh)

    def retreat(step, carry):
        head, q0 = unit_of(step)
        lane = iota((BQ, 128), 1)
        inv = jnp.sum(jnp.where(lane == step, LI[...], 0.0), axis=1, keepdims=True)
        given = jnp.where(lane // 64 == head, cast_up(DO[pl.ds(q0, BQ), :]) * inv, 0.0)
        given_low = given.astype(BF)
        delta = jnp.sum(cast_up(given_low) * cast_up(ON[pl.ds(q0, BQ), :]), axis=1, keepdims=True)
        given_t = given.T.astype(BF)
        query_t = cast_up(QA[head, pl.ds(q0, BQ), :]).T.astype(BF)
        for j in range(8):
            cols = slice(256 * j, 256 * j + 256)
            probs = PB[step, :, cols]
            grad = dot(given_low, VT[:, cols])
            DS[:, 128 + 256 * j : 384 + 256 * j] = (cast_up(probs) * (grad - delta)).astype(BF)
            DVT[:, cols] += dot(given_t, probs)
        key_rows = pl.ds(pl.multiple_of(128 * head, 128), 128)
        for j in range(8):
            cols = slice(256 * j, 256 * j + 256)
            SC[key_rows, cols] += dot(query_t, DS[:, 128 + 256 * j : 384 + 256 * j])
        moved = dot(DS[:, 128:2176], KN[...])
        block = pl.ds(pl.multiple_of(q0 // 2, 128), 128)
        N2[:, block] = jnp.where(lane // 64 == head, moved, cast_up(N2[:, block])).astype(BF)
        BT[head] += cast_up(DS[:, pl.ds(q0, 512)])
        return carry

    def add_low(refs, bufs):
        for ref, buf in zip(refs, bufs):
            total = cast_up(ref[...])
            for k in range(3):
                total += cast_up(buf[k])
            ref[...] = total.astype(BF)

    lax.fori_loop(0, 9, retreat, 0)
    ff_ra.wait()
    ff_rb.wait()

    def add_a(i, carry):
        add_low(
            [W1.at[zl, i, zh, :, low], WD.at[zl, i, zh, :, low_d]],
            [r["RA1"].at[:, i], r["RA2"].at[:, i]],
        )
        return carry

    def add_b(i, carry):
        add_low(
            [W1.at[i // 2, x, i % 2, :, high], WD.at[i // 2, x, i % 2, :, high_d]],
            [r["RB1"].at[:, i // 2, i % 2], r["RB2"].at[:, i // 2, i % 2]],
        )
        return carry

    lax.fori_loop(0, 4, add_a, 0)
    lax.fori_loop(0, 4, add_b, 0)
    ff_ra2 = Scatter(
        comm,
        "x",
        lambda xx: [W1.at[zl, xx, zh, :, low], WD.at[zl, xx, zh, :, low_d]],
        [r["SA1"], r["SA2"]],
    )
    ff_rb2 = Scatter(
        comm,
        "z",
        lambda zz: [W1.at[zz % 2, x, zz // 2, :, high], WD.at[zz % 2, x, zz // 2, :, high_d]],
        [r["SB1"], r["SB2"]],
    )
    ff_ra2.start()
    ff_rb2.start()
    lax.fori_loop(9, STEPS, retreat, 0)

    lane = iota((8, 128), 1)
    sub = iota((8, 128), 0)
    diagonals = []
    flip = jnp.where(iota((256, 256), 0) + iota((256, 256), 1) == 255, 1.0, 0.0).astype(BF)
    table_grad = jnp.zeros((1, 128), F32)
    one = iota((1, 128), 1)
    for h in range(2):
        near = jnp.zeros((1, 1024), F32)
        whole = BT[h]
        upper = whole.astype(BF)
        lower = (whole - cast_up(upper)).astype(BF)
        flipped = dot(flip, upper) + dot(flip, lower)
        for k in range(4):
            part = jnp.concatenate([flipped[64 * k : 64 * k + 64], jnp.zeros((64, 512), F32)], axis=1)
            part = pltpu.roll(part, 129 + 64 * k, 1, stride=1, stride_axis=0)
            near += jnp.sum(part, axis=0, keepdims=True)
        diagonals.append(near)
        base = 64 * (1 - h)
        rows_far = SC[128 * h + base : 128 * h + base + 8, 0:2048]
        key_at = iota((8, SEQ), 1)
        start = 256 * iota((8, SEQ), 0)
        left = jnp.sum(jnp.where(key_at < start - 128, rows_far, 0.0), axis=(0, 1), keepdims=True)
        right = jnp.sum(jnp.where(key_at >= start + 384, rows_far, 0.0), axis=(0, 1), keepdims=True)
        table_grad += jnp.where(one == 32 * h + 15, left, 0.0) + jnp.where(one == 32 * h + 31, right, 0.0)
    near = jnp.concatenate(diagonals + [jnp.zeros((6, 1024), F32)], axis=0)
    upper = near.astype(BF)
    lower = (near - cast_up(upper)).astype(BF)
    sums = dot_nt(upper, r["OH"][...]) + dot_nt(lower, r["OH"][...])
    table_grad += jnp.sum(jnp.where(lane // 32 == sub, sums, 0.0), axis=0, keepdims=True)
    spread = jnp.concatenate([table_grad, jnp.zeros((1, 256), F32)], axis=1)
    spread = pltpu.roll(jnp.broadcast_to(spread, (8, 384)), 32 * h0, 1)
    VEC[0:1, 768:1024] = spread[0:1, 0:256]
    VEC[1:2, 768:896] = spread[0:1, 256:384]

    YR, DWQ = r["YR"], r["DWQ"]
    first_gain = r["GS"][0:1, 0:768]
    base_s = comm.take(4)
    MID[...] = jnp.zeros((4, 128, D), F32)

    def sib_at(yy):
        return GU.at[yy // 2, :, :, pl.ds(pl.multiple_of((yy % 2) * 1024, 128), 768)]

    def place_of(k):
        return (y + jnp.where(k == 0, 2, jnp.where(k == 1, 1, jnp.where(k == 2, 3, 0)))) % 4

    def spread_back(k, carry):
        yy = place_of(k)

        def half(hh, inner):
            at = pl.ds(pl.multiple_of(512 * yy + 256 * hh, 256), 256)
            raw = cast_up(T5[yy, hh].reshape(256, D))
            scale = rms_scale(raw)
            normed = (raw * scale * first_gain).astype(BF)
            dq = N2[:, pl.ds(pl.multiple_of(256 * yy + 128 * hh, 128), 128)]
            sub = iota((128, 256), 0)
            dkt = jnp.where(sub < 64, SC[0:128, at], SC[128:256, at])
            dvt = DVT[:, at]
            dk, dv = dkt.T.astype(BF), dvt.T.astype(BF)
            dqt = cast_up(dq).T.astype(BF)
            grad = dot_nt(jnp.concatenate([dq, dk, dv], axis=1), WQ[...].reshape(D, 384))
            VEC[0:1, 0:768] += jnp.sum(grad * raw * scale, axis=0, keepdims=True)
            MID[0] += dot(dqt, normed)
            MID[1] += dot(dkt.astype(BF), normed)
            MID[2] += dot(dvt.astype(BF), normed)
            T5[yy, hh] = grad.astype(BF).reshape(2, 128, D)
            return inner

        lax.fori_loop(0, 2, half, 0)
        comm.copy(T5.at[yy, :, 1 - c], sib_at(yy), base_s + k, sib).start()
        return carry

    lax.fori_loop(0, 4, spread_back, 0)
    for i in range(3):
        DWQ[:, :, :, :, 128 * i : 128 * i + 128] = MID[i].T.astype(BF).reshape(2, 4, 2, 48, 128)
    qa, qb = pl.ds(0, 256), pl.ds(256, 128)
    q_ra = Scatter(comm, "z", lambda zz: [DWQ.at[zz % 2, :, zz // 2, :, qa]], [r["QA1"]])
    q_rb = Scatter(comm, "x", lambda xx: [DWQ.at[:, xx, :, :, qb]], [r["QB1"]])
    v_z = Scatter(comm, "z", lambda zz: [VEC], [r["V1"]])
    base_y = comm.take(3)
    for k in range(4):
        yy = (y + (2, 1, 3, 0)[k]) % 4
        comm.recv(sib_at(yy), base_s + k)
        for hh in range(2):
            T5[yy, hh, c] = (cast_up(T5[yy, hh, c]) + cast_up(sib_at(yy)[hh])).astype(BF)
        if k < 3:
            comm.send(T5.at[yy, :, c], YR.at[k], base_y + k, comm.peer("y", (2, 1, 3)[k]))
        if k == 0:
            q_ra.start()
            q_rb.start()
            v_z.start()

    ff_ra2.wait()
    ff_rb2.wait()
    add_low([W1.at[zl, x, zh, :, low], WD.at[zl, x, zh, :, low_d]], [r["SA1"], r["SA2"]])
    add_low([W1.at[zl, x, zh, :, high], WD.at[zl, x, zh, :, high_d]], [r["SB1"], r["SB2"]])
    ff_ry = Scatter(
        comm,
        "y",
        lambda yy: [
            W1.at[zl, x, zh, :, pl.ds(pl.multiple_of(640 * yy, 128), 640)],
            WD.at[zl, x, zh, pl.ds(16 * yy, 16)],
        ],
        [r["SY1"], r["SY2"]],
    )
    ff_ry.start()
    q_ra.wait()
    q_rb.wait()
    v_z.wait()
    for i in range(4):
        add_low([DWQ.at[zl, i, zh, :, qa]], [r["QA1"].at[:, i]])
        add_low([DWQ.at[i // 2, x, i % 2, :, qb]], [r["QB1"].at[:, i // 2, i % 2]])
    VE2 = r["VE2"]
    VE2[...] = VEC[...] + r["V1"][0] + r["V1"][1] + r["V1"][2]
    q_ra2 = Scatter(comm, "x", lambda xx: [DWQ.at[zl, xx, zh, :, qa]], [r["QA2"]])
    q_rb2 = Scatter(comm, "z", lambda zz: [DWQ.at[zz % 2, x, zz // 2, :, qb]], [r["QB2"]])
    v_x = Scatter(comm, "x", lambda xx: [VE2], [r["V2"]])
    q_ra2.start()
    q_rb2.start()
    v_x.start()

    for k in range(3):
        comm.recv(YR.at[k], base_y + k)
    zri = comm.take()
    ZS, ZR = r["ZS"], r["ZR"]

    def summed(hh):
        total = cast_up(T5[y, hh, c])
        for k in range(3):
            total += cast_up(YR[k, hh])
        return total

    ZS[...] = summed(1 - zh).astype(BF)
    comm.send(ZS, ZR, zri, other)

    def finish(hh, grad):
        raw = cast_up(tok[hh])
        scale = rms_scale(raw)
        gained = grad * first_gain
        mean = jnp.mean(raw * gained, axis=-1, keepdims=True)
        r["din"][hh] = r["din"][hh] + scale * gained - raw * (scale * scale * scale * mean)

    finish(zh, summed(zh))

    ff_ry.wait()
    here = pl.ds(pl.multiple_of(640 * y, 128), 640)
    total = cast_up(W1[zl, x, zh, :, here])
    for k in range(3):
        total += cast_up(r["SY1"][k])
    asm[:, 384:1024] = total
    total = cast_up(WD[zl, x, zh, pl.ds(16 * y, 16)])
    for k in range(3):
        total += cast_up(r["SY2"][k])
    r["WDG"][...] = total
    home = (2 * c + zh, y // 2, y % 2)
    own_home = (home[0] == y) & (home[1] == zh) & (home[2] == c)
    dwi = comm.take()
    comm.send_or_keep(
        r["WDG"], r["dwd_in"], dwi, dev(x, home[0], home[1] * 2 + zl, home[2]), dwi, own_home
    )
    q_ra2.wait()
    q_rb2.wait()
    v_x.wait()
    for cols, ref, buf in ((slice(0, 256), qa, r["QA2"]), (slice(256, 384), qb, r["QB2"])):
        total = cast_up(DWQ[zl, x, zh, :, ref])
        for k in range(3):
            total += cast_up(buf[k])
        asm[:, cols] = total
    sums = VE2[...] + r["V2"][0] + r["V2"][1] + r["V2"][2]
    W2R = r["W2R"]
    base_h = comm.take(8)
    base_hr = comm.take(8)
    mine = c * 4 + y
    for j in range(8):
        wst[j, 0:6, :] = asm[6 * j : 6 * j + 6, :]
        wst[j, 6:8, :] = sums[0:2]
        ys, hs, cs = 2 * zh + j // 4, (j // 2) % 2, j % 2
        own = (ys == y) & (hs == zh) & (cs == c)
        cp = comm.copy(wst.at[j], W2R.at[mine], base_h + j, dev(x, ys, hs * 2 + zl, cs), base_hr + mine)
        keep = pltpu.make_async_copy(wst.at[j], W2R.at[mine], comm.rs.at[base_hr + mine])
        pl.when(own)(keep.start)
        pl.when(jnp.logical_not(own))(cp.start)
        comm.pending.append((cp, own))
    comm.recv(ZR, zri)
    finish(1 - zh, cast_up(ZR[...]))
    for d in range(8):
        comm.recv(W2R.at[d], base_hr + d)
    for name in ("dwq", "dwk", "dwv"):
        r[name][...] = jnp.zeros((6, D), F32)
    rows_sum = jnp.zeros((2, 1024), F32)
    for cc in range(2):
        for yy in range(4):
            d, first = cc * 4 + yy, 64 * first_head(cc * 4 + yy)
            for i, name in enumerate(("dwq", "dwk", "dwv")):
                r[name][:, first : first + 128] += W2R[d, 0:6, 128 * i : 128 * i + 128]
            for i, name in enumerate(("dwg", "dwu")):
                for k in range(2):
                    tile = 2 * (2 * yy + k) + cc
                    at = 384 + 256 * i + 128 * k
                    r[name][:, 128 * tile : 128 * tile + 128] = W2R[d, 0:6, at : at + 128]
            if yy < 3:
                at = (cc * 3 + yy) * 128
                r["dwo"][:, at : at + 128] = W2R[d, 0:6, 896:1024]
            rows_sum += W2R[d, 6:8, :]
    r["dvec"][0:2, :] = rows_sum
    r["dvec"][2:8, :] = jnp.zeros((6, 1024), F32)
    comm.recv(r["dwd_in"], dwi)
    r["dwd"][...] = r["dwd_in"][...]
    for k in range(4):
        yy = (y + (2, 1, 3, 0)[k]) % 4
        comm.copy(T5.at[yy, :, 1 - c], sib_at(yy), base_s + k, sib).wait_send()
    comm.drain()
    if stop != "all":
        for n in DEBUG:
            r["o_" + n][...] = r[n][...]


def WO_A(ref):
    return ref.at[:, pl.ds(0, 1280)]


INPUTS = [
    ("lens", "s"), ("g1", "s"), ("g2", "s"), ("bt", "s"),
    ("tok", "v"), ("cot", "v"), ("wq", "v"), ("wk", "v"), ("wv", "v"), ("wo", "v"),
    ("wg", "v"), ("wu", "v"), ("wd", "v"),
]
SCRATCH = [
    ("W1", ((2, 4, 2, 48, 2560), BF)),
    ("WD", ((2, 4, 2, 64, 768), BF)),
    ("WQ", ((2, 4, 2, 48, 384), BF)),
    ("G5", ((2, 4, 2, 8, 1024), F32)),
    ("T5", ((4, 2, 2, 128, 768), BF)),
    ("TK", ((2, 2, 128, 768), BF)),
    ("CT", ((2, 2, 128, 768), BF)),
    ("wst", ((8, 8, 1024), F32)),
    ("w0", ((8, 8, 1024), F32)),
    ("asm", ((48, 1024), F32)),
    ("wdst", ((16, 768), BF)),
    ("GS", ((8, 1024), F32)),
    ("OH", ((128, 1024), BF)),
    ("BO", ((8, 1024), F32)),
    ("BT", ((2, 256, 512), F32)),
    ("QA", ((2, 2048, 128), BF)),
    ("KT", ((2, 128, 2048), BF)),
    ("KN", ((2048, 128), BF)),
    ("VN", ((2048, 128), BF)),
    ("VT", ((128, 2048), BF)),
    ("SC", ((256, 2304), F32)),
    ("PB", ((12, 256, 2048), BF)),
    ("ON", ((2048, 128), BF)),
    ("LI", ((256, 128), F32)),
    ("A", ((2, 256, 512), BF)),
    ("WOF", ((4, 2, 48, 768), BF)),
    ("POS", ((2, 2, 128, 768), BF)),
    ("POR", ((2, 2, 128, 768), BF)),
    ("MID", ((4, 128, 768), F32)),
    ("N2", ((256, 1536), BF)),
    ("N2T", ((768, 512), BF)),
    ("HIDT", ((1024, 512), BF)),
    ("GU", ((2, 2, 128, 2048), BF)),
    ("PNR", ((2, 2, 128, 768), BF)),
    ("PYS", ((2, 128, 768), BF)),
    ("PYR", ((2, 128, 768), BF)),
    ("ML", ((2, 2, 128, 768), BF)),
    ("DOS", ((4, 2, 256, 128), BF)),
    ("DO", ((2048, 128), BF)),
    ("RA1", ((3, 4, 48, 1280), BF)),
    ("RA2", ((3, 4, 64, 384), BF)),
    ("RB1", ((3, 2, 2, 48, 1280), BF)),
    ("RB2", ((3, 2, 2, 64, 384), BF)),
    ("SA1", ((3, 48, 1280), BF)),
    ("SA2", ((3, 64, 384), BF)),
    ("SB1", ((3, 48, 1280), BF)),
    ("SB2", ((3, 64, 384), BF)),
    ("SY1", ((3, 48, 640), BF)),
    ("SY2", ((3, 16, 768), BF)),
    ("HX", ((256, 2304), BF)),
    ("DVT", ((128, 2048), F32)),
    ("YR", ((3, 2, 128, 768), BF)),
    ("ZS", ((128, 768), BF)),
    ("ZR", ((128, 768), BF)),
    ("DWQ", ((2, 4, 2, 48, 384), BF)),
    ("QA1", ((3, 4, 48, 256), BF)),
    ("QA2", ((3, 48, 256), BF)),
    ("QB1", ((3, 2, 2, 48, 128), BF)),
    ("QB2", ((3, 48, 128), BF)),
    ("VEC", ((8, 1024), F32)),
    ("V1", ((3, 8, 1024), F32)),
    ("V2", ((3, 8, 1024), F32)),
    ("VE2", ((8, 1024), F32)),
    ("W2R", ((8, 8, 1024), F32)),
    ("WDG", ((16, 768), F32)),
    ("dwd_in", ((16, 768), F32)),
    ("send_sem", None),
    ("recv_sem", None),
]


OUTPUTS = [
    ("out", ((2, 128, 768), BF)),
    ("din", ((2, 128, 768), F32)),
    ("dwq", ((6, 768), F32)),
    ("dwk", ((6, 768), F32)),
    ("dwv", ((6, 768), F32)),
    ("dwo", ((6, 768), F32)),
    ("dwg", ((6, 2048), F32)),
    ("dwu", ((6, 2048), F32)),
    ("dwd", ((16, 768), F32)),
    ("dvec", ((8, 1024), F32)),
]
DEBUG = []


def outputs_of(stop):
    if stop == "all":
        return OUTPUTS
    shapes = dict((n, s) for n, s in SCRATCH if s is not None)
    return OUTPUTS + [("o_" + n, shapes[n]) for n in DEBUG]


def call_mega(stop, *args):
    spec = {"s": pl.BlockSpec(memory_space=pltpu.SMEM), "v": pl.BlockSpec(memory_space=pltpu.VMEM)}
    outs = outputs_of(stop)
    scratch = []
    for _, s in SCRATCH:
        scratch.append(pltpu.SemaphoreType.DMA((NSEM,)) if s is None else pltpu.VMEM(s[0], s[1]))
    return pl.pallas_call(
        functools.partial(mega, stop),
        out_shape=[jax.ShapeDtypeStruct(s[0], s[1]) for _, s in outs],
        in_specs=[spec[k] for _, k in INPUTS],
        out_specs=[pl.BlockSpec(memory_space=pltpu.VMEM) for _ in outs],
        scratch_shapes=scratch,
        name="layer",
        compiler_params=pltpu.CompilerParams(
            collective_id=0, has_side_effects=True, vmem_limit_bytes=62 * 2**20
        ),
    )(*args)


def per_device(
    tokens,
    lengths,
    cotangent,
    query_weight,
    key_weight,
    value_weight,
    out_weight,
    gate_weight,
    up_weight,
    down_weight,
    first_gain,
    second_gain,
    bias_table,
):
    done = call_mega(
        "all",
        lengths,
        first_gain,
        second_gain,
        bias_table,
        tokens,
        cotangent,
        query_weight,
        key_weight,
        value_weight,
        out_weight,
        gate_weight,
        up_weight,
        down_weight,
    )
    flat = lax.axis_index("rows") * 16 + lax.axis_index("seq")
    vectors = done[9]
    table = jnp.concatenate([vectors[0, 768:1024], vectors[1, 768:896]])
    return (
        *done[:9],
        lax.dynamic_slice(vectors, (0, 6 * flat), (1, 6))[0],
        lax.dynamic_slice(vectors, (1, 6 * flat), (1, 6))[0],
        lax.dynamic_slice(table, (3 * flat,), (3,)),
    )


def solution(mesh):
    tokens = P("rows", "seq", None)
    matrix = P(("rows", "seq"), None)
    vector = P(("rows", "seq"))
    return jax.shard_map(
        per_device,
        mesh=mesh,
        in_specs=(tokens, P("rows"), tokens, *([matrix] * 7), *([vector] * 3)),
        out_specs=(tokens, tokens, *([matrix] * 7), *([vector] * 3)),
        check_vma=False,
    )
```

```python
import jax
import jax.numpy as jnp
from jax import lax
from jax.experimental import pallas as pl
from jax.experimental.pallas import tpu as pltpu
from jax.sharding import PartitionSpec as P

MESH = pl.DeviceIdType.MESH
BF = jnp.bfloat16
F32 = jnp.float32
D = 768
SEQ = 2048
EPSILON = 1e-06
NEGATIVE = -1e30
LIMITS = (1, 2, 3, 4, 5, 6, 7, 8, 12, 16, 23, 32, 46, 64, 91)
NSEM = 240
BQ = 256
STEPS = 12


def dev(x, y, z, c):
    return ((z % 2) * 4 + x, (y * 2 + z // 2) * 2 + c)


def first_head(t):
    return (3 * t) // 2


def iota(shape, dim):
    return lax.broadcasted_iota(jnp.int32, shape, dim)


def dot(a, b):
    return jnp.dot(a, b, preferred_element_type=F32)


def dot_nt(a, b):
    return lax.dot_general(a, b, (((1,), (1,)), ((), ())), preferred_element_type=F32)


class Comm:
    def __init__(self, x, y, z, c, send_sem, recv_sem):
        self.x, self.y, self.z, self.c = x, y, z, c
        self.ss, self.rs = send_sem, recv_sem
        self.next = 0
        self.pending = []

    def take(self, n=1):
        at = self.next
        self.next += n
        assert self.next <= NSEM
        return at

    def peer(self, axis, offset):
        x, y, z, c = self.x, self.y, self.z, self.c
        if axis == "x":
            return dev((x + offset) % 4, y, z, c)
        if axis == "y":
            return dev(x, (y + offset) % 4, z, c)
        if axis == "z":
            return dev(x, y, (z + offset) % 4, c)
        return dev(x, y, z, 1 - c)

    def place(self, axis, offset):
        at = {"x": self.x, "y": self.y, "z": self.z}[axis]
        return (at + offset) % 4

    def copy(self, src, dst, i, to, j=None):
        return pltpu.make_async_remote_copy(
            src_ref=src,
            dst_ref=dst,
            send_sem=self.ss.at[i],
            recv_sem=self.rs.at[i if j is None else j],
            device_id=to,
            device_id_type=MESH,
        )

    def send(self, src, dst, i, to):
        cp = self.copy(src, dst, i, to)
        cp.start()
        self.pending.append(cp)

    def recv(self, dst, i):
        self.copy(dst, dst, i, self.peer("c", 0)).wait_recv()

    def send_or_keep(self, src, dst, i, to, j, own):
        cp = self.copy(src, dst, i, to, j)
        keep = pltpu.make_async_copy(src, dst, self.rs.at[j])

        @pl.when(own)
        def _():
            keep.start()

        @pl.when(jnp.logical_not(own))
        def _():
            cp.start()

        self.pending.append((cp, own))

    def drain(self):
        for cp in self.pending:
            if isinstance(cp, tuple):
                cp, own = cp

                @pl.when(jnp.logical_not(own))
                def _():
                    cp.wait_send()
            else:
                cp.wait_send()
        self.pending = []


class Direct:
    def __init__(self, comm, axis, views):
        self.comm, self.axis, self.views = comm, axis, views
        self.count = len(views(comm.place(axis, 0)))
        self.base = comm.take(3 * self.count)

    def start(self):
        for k, off in enumerate((1, 3, 2)):
            for n, ref in enumerate(self.views(self.comm.place(self.axis, 0))):
                self.comm.send(ref, ref, self.base + k * self.count + n, self.comm.peer(self.axis, off))

    def wait(self):
        for k, off in enumerate((1, 3, 2)):
            for n, ref in enumerate(self.views(self.comm.place(self.axis, -off + 4))):
                self.comm.recv(ref, self.base + k * self.count + n)


class Ring:
    def __init__(self, comm, axis, views, halves):
        self.comm, self.axis, self.views, self.halves = comm, axis, views, halves
        self.count = len(views(comm.place(axis, 0)))
        self.base = comm.take(4 * self.count)

    def start(self, source=None):
        own = self.views(self.comm.place(self.axis, 0))
        for n, ref in enumerate(own):
            src = ref if source is None else source[n]
            for k, off in enumerate((1, 3)):
                self.comm.send(src, ref, self.base + k * self.count + n, self.comm.peer(self.axis, off))

    def forward(self):
        for k, off in enumerate((1, 3)):
            came = self.comm.place(self.axis, -off + 4)
            for n, ref in enumerate(self.views(came)):
                self.comm.recv(ref, self.base + k * self.count + n)
            for n, ref in enumerate(self.halves(came, k)):
                self.comm.send(ref, ref, self.base + (2 + k) * self.count + n, self.comm.peer(self.axis, off))

    def wait(self):
        far = self.comm.place(self.axis, 2)
        for k in range(2):
            for n, ref in enumerate(self.halves(far, k)):
                self.comm.recv(ref, self.base + (2 + k) * self.count + n)


class Scatter:
    def __init__(self, comm, axis, views, bufs):
        self.comm, self.axis, self.views, self.bufs = comm, axis, views, bufs
        self.base = comm.take(3 * len(bufs))

    def start(self):
        for k, off in enumerate((1, 3, 2)):
            refs = self.views(self.comm.place(self.axis, off))
            for n, ref in enumerate(refs):
                self.comm.send(
                    ref, self.bufs[n].at[k], self.base + k * len(refs) + n, self.comm.peer(self.axis, off)
                )

    def wait(self):
        for k in range(3):
            for n, buf in enumerate(self.bufs):
                self.comm.recv(buf.at[k], self.base + k * len(self.bufs) + n)


def bucket_ids(offsets):
    distance = jnp.abs(offsets)
    bucket_sum = jnp.where(offsets > 0, 16, 0)
    for threshold in LIMITS:
        bucket_sum = bucket_sum + jnp.where(distance >= threshold, 1, 0)
    return bucket_sum


def rms_scale(values):
    return lax.rsqrt(jnp.mean(values * values, axis=-1, keepdims=True) + EPSILON)


def greet(comm):
    x, y, z, c = comm.x, comm.y, comm.z, comm.c
    zl, zh = z % 2, z // 2
    barrier = pltpu.get_barrier_semaphore()
    count = 0
    peers = []
    for dy in range(4):
        for dh in range(2):
            for dc in range(2):
                if dy or dh or dc:
                    peers.append(dev(x, (y + dy) % 4, ((zh + dh) % 2) * 2 + zl, (c + dc) % 2))
    for off in (1, 2, 3):
        peers.append(comm.peer("x", off))
    for off in (1, 3):
        peers.append(comm.peer("z", off))
    for peer in peers:
        pl.semaphore_signal(barrier, inc=1, device_id=peer, device_id_type=MESH)
        count += 1
    return barrier, count


def cast_up(v):
    return v.astype(F32)


def head_bias(tables, o):
    return tables[o : o + 1, 0:1], tables[o : o + 1, 1023:1024]


def mega(*refs):
    names = [n for n, _ in INPUTS] + [n for n, _ in OUTPUTS] + [n for n, _ in SCRATCH]
    r = dict(zip(names, refs))
    rows, seq = lax.axis_index("rows"), lax.axis_index("seq")
    x, y, zl, zh, c = rows % 4, seq // 4, rows // 4, (seq // 2) % 2, seq % 2
    z = zh * 2 + zl
    flat = rows * 16 + seq
    t = c * 4 + y
    comm = Comm(x, y, z, c, r["send_sem"], r["recv_sem"])
    local_sem = r["local_sem"]
    TK, CT, T5, tok, cot = r["TK"], r["CT"], r["T5"], r["tok"], r["cot"]
    loads = []
    for i, name in enumerate(("wq", "wk", "wv", "wo", "wg", "wu", "wd")):
        loads.append(pltpu.make_async_copy(r["h_" + name], r[name], local_sem.at[i]))
        loads[-1].start()
    keep_tokens = pltpu.make_async_copy(tok.at[zh], T5.at[y, zh, c], local_sem.at[7])
    keep_tk = pltpu.make_async_copy(tok, TK.at[:, c], local_sem.at[8])
    keep_ct = pltpu.make_async_copy(cot, CT.at[:, c], local_sem.at[9])
    keep_tokens.start()
    keep_tk.start()
    keep_ct.start()
    barrier, count = greet(comm)

    lanes = iota((1, 1024), 1)
    first_row = jnp.zeros((1, 1024), F32)
    second_row = jnp.zeros((1, 1024), F32)
    for i in range(6):
        first_row += jnp.where(lanes == 6 * flat + i, r["g1"][i], 0.0)
        second_row += jnp.where(lanes == 6 * flat + i, r["g2"][i], 0.0)
    for i in range(3):
        at = 768 + 3 * flat + i
        first_row += jnp.where(lanes == at, r["bt"][i], 0.0)
        second_row += jnp.where((lanes >= 768) & (lanes == at - 256), r["bt"][i], 0.0)
    first_row = cast_up(first_row.astype(BF))
    second_row = cast_up(second_row.astype(BF))
    wst, w0 = r["wst"], r["w0"]
    for load in loads:
        load.wait()
    for cc in range(2):
        for yy in range(4):
            d, h0 = cc * 4 + yy, first_head(cc * 4 + yy)
            for i, name in enumerate(("wq", "wk", "wv")):
                wst[d, 0:6, 128 * i : 128 * (i + 1)] = r[name][:, 64 * h0 : 64 * h0 + 128]
            for i, name in enumerate(("wg", "wu")):
                for k in range(2):
                    tile = 2 * (2 * yy + k) + cc
                    at = 512 + 256 * i + 128 * k
                    wst[d, 0:6, at : at + 128] = r[name][:, 128 * tile : 128 * tile + 128]
            if yy < 3:
                at = (cc * 3 + yy) * 128
                wst[d, 0:6, 384:512] = r["wo"][:, at : at + 128]
            else:
                wst[d, 0:6, 384:512] = jnp.zeros((6, 128), F32)
            wst[d, 6:7, :] = first_row
            wst[d, 7:8, :] = second_row
    r["wdst"][...] = r["wd"][...].astype(BF)

    pl.semaphore_wait(barrier, count)

    W1, WD, WQ, G5 = r["W1"], r["WD"], r["WQ"], r["G5"]
    other = comm.peer("z", 2)
    zi = comm.take()
    comm.send(tok.at[1 - zh], T5.at[y, zh, c], zi, other)
    own_tokens = Ring(
        comm,
        "y",
        lambda yy: [T5.at[yy, zh, c]],
        lambda yy, k: [T5.at[yy, zh, c, pl.ds(64 * k, 64)]],
    )
    own_tokens.start(source=[tok.at[zh]])
    slot = (y % 2) * 4 + zh * 2 + c
    base0 = comm.take(8)
    baser = comm.take(8)
    for cc in range(2):
        for yy in range(4):
            to = dev(x, yy, (y // 2) * 2 + zl, cc)
            own = (y == yy) & (c == cc) & (zh == y // 2)
            cp = comm.copy(wst.at[cc * 4 + yy], w0.at[slot], base0 + cc * 4 + yy, to, baser + slot)
            keep = pltpu.make_async_copy(wst.at[cc * 4 + yy], w0.at[slot], comm.rs.at[baser + slot])
            pl.when(own)(keep.start)
            pl.when(jnp.logical_not(own))(cp.start)
            comm.pending.append((cp, own))
    wd_to = (zh * 2 + c, y % 2, y // 2)
    own_wd = (wd_to[0] == y) & (wd_to[1] == zh) & (wd_to[2] == c)
    wdi = comm.take()
    wd_region = WD.at[zl, x, wd_to[1], wd_to[0]]
    comm.send_or_keep(
        r["wdst"], wd_region, wdi, dev(x, wd_to[0], wd_to[1] * 2 + zl, wd_to[2]), wdi, own_wd
    )

    pair = comm.take(2)

    for j in range(8):
        comm.recv(w0.at[j], baser + j)
    asm = r["asm"]
    gsum = jnp.zeros((2, 1024), F32)
    for j in range(8):
        asm[6 * j : 6 * j + 6, :] = w0[j, 0:6, :]
        gsum += w0[j, 6:8, :]
    WQ[zl, x, zh] = asm[:, 0:512].astype(BF)
    G5[zl, x, zh] = jnp.concatenate([gsum, jnp.zeros((6, 1024), F32)], axis=0)
    W1[zl, x, zh, y] = asm[:, 512:1024].astype(BF)
    qkv_a1 = Direct(comm, "x", lambda xx: [WQ.at[zl, xx, zh, :, pl.ds(0, 256)], G5.at[zl, xx, zh]])
    qkv_b1 = Direct(comm, "z", lambda zz: [WQ.at[zz % 2, x, zz // 2, :, pl.ds(256, 256)]])
    qkv_a1.start()
    qkv_b1.start()
    comm.recv(WD.at[zl, x, zh, y], wdi)
    ff_y = Direct(comm, "y", lambda yy: [W1.at[zl, x, zh, yy], WD.at[zl, x, zh, yy]])
    ff_y.start()

    comm.recv(T5.at[y, 1 - zh, c], zi)
    far_tokens = Ring(
        comm,
        "y",
        lambda yy: [T5.at[yy, 1 - zh, c]],
        lambda yy, k: [T5.at[yy, 1 - zh, c, pl.ds(64 * k, 64)]],
    )
    far_tokens.start()
    keep_tokens.wait()
    sib = comm.peer("c", 0)
    across = comm.take(4)

    def cross(k):
        yy = (y + (0, 1, 3, 2)[k]) % 4
        comm.send(T5.at[yy, :, c], T5.at[yy, :, c], across + k, sib)

    def crossed(k):
        yy = (y + (0, 1, 3, 2)[k]) % 4
        comm.recv(T5.at[yy, :, 1 - c], across + k)

    cross(0)
    own_tokens.forward()
    qkv_a1.wait()
    qkv_b1.wait()
    qkv_a2 = Direct(
        comm,
        "z",
        lambda zz: [WQ.at[zz % 2, :, zz // 2, :, pl.ds(0, 256)], G5.at[zz % 2, :, zz // 2]],
    )
    qkv_b2 = Direct(comm, "x", lambda xx: [WQ.at[:, xx, :, :, pl.ds(256, 256)]])
    qkv_a2.start()
    qkv_b2.start()
    ff_y.wait()
    low, high = pl.ds(0, 256), pl.ds(256, 256)
    low_d, high_d = pl.ds(0, 384), pl.ds(384, 384)
    ff_a1 = Direct(
        comm, "x", lambda xx: [W1.at[zl, xx, zh, :, :, low], WD.at[zl, xx, zh, :, :, low_d]]
    )
    ff_b1 = Direct(
        comm,
        "z",
        lambda zz: [
            W1.at[zz % 2, x, zz // 2, :, :, high],
            WD.at[zz % 2, x, zz // 2, :, :, high_d],
        ],
    )
    ff_a1.start()
    ff_b1.start()
    far_tokens.forward()
    cross(1)
    cross(2)
    keep_tk.wait()
    keep_ct.wait()
    comm.send(TK.at[:, c], TK.at[:, c], pair, sib)
    comm.send(CT.at[:, c], CT.at[:, c], pair + 1, sib)

    qkv_a2.wait()
    qkv_b2.wait()
    WOF = r["WOF"]
    base_w = comm.take(8)
    base_wr = comm.take(8)
    for cc in range(2):
        for yy in range(4):
            src = WQ.at[cc, :, :, :, pl.ds(384, 128)]
            dst = WOF.at[:, :, :, pl.ds(pl.multiple_of((c * 3 + y % 3) * 128, 128), 128)]
            cp = comm.copy(src, dst, base_w + cc * 4 + yy, dev(x, yy, z, cc), base_wr + c * 4 + y)
            keep = pltpu.make_async_copy(src, dst, comm.rs.at[base_wr + c * 4 + y])
            here = (yy == y) & (cc == c)
            pl.when(here & (y < 3))(keep.start)
            pl.when(jnp.logical_not(here) & (y < 3))(cp.start)
            comm.pending.append((cp, here | (y == 3)))
    total = jnp.zeros((8, 1024), F32)
    for a in range(2):
        for b in range(4):
            for e in range(2):
                total += G5[a, b, e]
    r["GS"][...] = total
    h0 = first_head(t)
    table_row = jnp.concatenate([total[0:1, 768:1024], total[1:2, 768:896]], axis=1)
    table_row = jnp.broadcast_to(table_row, (8, 384))
    table_row = pltpu.roll(table_row, 384 - 32 * h0, 1)[:, 0:128]
    lane = iota((8, 128), 1)
    sub = iota((8, 128), 0)
    table_two = jnp.where((lane // 32) == sub, table_row, 0.0).astype(BF)
    r["OH"][...] = jnp.where(
        bucket_ids(iota((128, 1024), 1) - 512) == iota((128, 1024), 0) % 32, 1.0, 0.0
    ).astype(BF)
    by_offset = dot(table_two, r["OH"][...])
    r["BO"][...] = by_offset
    for h in range(2):
        for k in range(4):
            rolled = pltpu.roll(
                jnp.broadcast_to(by_offset[h : h + 1, :], (64, 1024)), 640 + 64 * k, 1, stride=1, stride_axis=0
            )
            r["BT"][h, 64 * k : 64 * k + 64, :] = rolled[:, 0:512]

    ff_a1.wait()
    ff_b1.wait()
    ff_a2 = Ring(
        comm,
        "z",
        lambda zz: [
            W1.at[zz % 2, :, zz // 2, :, :, low],
            WD.at[zz % 2, :, zz // 2, :, :, low_d],
        ],
        lambda zz, k: [
            W1.at[zz % 2, pl.ds(2 * k, 2), zz // 2, :, :, low],
            WD.at[zz % 2, pl.ds(2 * k, 2), zz // 2, :, :, low_d],
        ],
    )
    ff_b2 = Ring(
        comm,
        "x",
        lambda xx: [W1.at[:, xx, :, :, :, high], WD.at[:, xx, :, :, :, high_d]],
        lambda xx, k: [W1.at[k, xx, :, :, :, high], WD.at[k, xx, :, :, :, high_d]],
    )
    ff_a2.start()
    ff_b2.start()

    QA, KT, KN, VN, VT = r["QA"], r["KT"], r["KN"], r["VN"], r["VT"]
    row_len = r["lens"][zh]

    def project(i, carry):
        raw = cast_up(T5[i // 2, i % 2].reshape(256, D))
        normed = (raw * rms_scale(raw) * r["GS"][0:1, 0:768]).astype(BF)
        res = dot(normed, WQ[:, :, :, :, 0:384].reshape(D, 384))
        q, k_, v = res[:, 0:128], res[:, 128:256], res[:, 256:384]
        at = pl.ds(pl.multiple_of(i * 256, 256), 256)
        KN[at, :] = k_.astype(BF)
        VN[at, :] = jnp.concatenate([v, jnp.ones((256, 128), F32)], axis=1).astype(BF)
        VT[:, at] = v.T.astype(BF)
        kt = k_.T
        lane = iota((256, 128), 1)
        sub = iota((128, 256), 0)
        key_at = i * 256 + iota((128, 256), 1)
        for h in range(2):
            base = 64 * (1 - h)
            hot = jnp.where((lane == base + i) | (lane == base + 8), 1.0, 0.0)
            QA[h, at, :] = jnp.where(lane // 64 == h, q, hot).astype(BF)
            left, right = head_bias(r["BO"][...], h)
            start = 256 * (sub - base)
            extra = jnp.where(key_at < start - 128, left, 0.0) + jnp.where(
                key_at >= start + 384, right, 0.0
            )
            masked = jnp.where(key_at >= row_len, NEGATIVE, 0.0)
            extra = jnp.where(sub - base < 8, extra, jnp.where(sub - base == 8, masked, 0.0))
            KT[h, :, at] = jnp.where(sub // 64 == h, kt, extra).astype(BF)
        return carry

    for k in range(4):
        if k == 3:
            own_tokens.wait()
            far_tokens.wait()
            cross(3)
        crossed(k)
        first = 2 * ((y + (0, 1, 3, 2)[k]) % 4)
        lax.fori_loop(first, first + 2, project, 0)
    r["ON"][...] = jnp.zeros((SEQ, 128), BF)
    r["LI"][...] = jnp.zeros((1024, 128), F32)
    r["PB"][:, :, 0:128] = jnp.zeros((3, 1024, 128), BF)
    r["PB"][:, :, 2176:2304] = jnp.zeros((3, 1024, 128), BF)

    SC, PB, BT, ON, LI = r["SC"], r["PB"], r["BT"], r["ON"], r["LI"]

    def unit_of(step):
        ui = step // 4
        u = jnp.where(ui == 0, 1, jnp.where(ui == 1, 0, 2))
        number = 3 * t + u
        head = number // 2 - h0
        start = (number % 2) * 1024 + (step % 4) * 256
        return head, pl.multiple_of(start, 256)

    S2 = r["S2"]

    def score_part(step, buf, j, top):
        head, q0 = unit_of(step)
        s = dot(QA[head, pl.ds(q0, BQ), :], KT[head, :, 256 * j : 256 * j + 256])
        buf[:, 128 + 256 * j : 384 + 256 * j] = s
        most = jnp.maximum(s[:, 0:128], s[:, 128:256])
        return most if top is None else jnp.maximum(top, most)

    def score_end(step, buf, top):
        head, q0 = unit_of(step)
        buf[:, pl.ds(q0, 512)] = buf[:, pl.ds(q0, 512)] + BT[head]
        return jnp.max(top, axis=1, keepdims=True)

    def block_of(step):
        return pl.ds(pl.multiple_of((step % 4) * 256, 256), BQ)

    def prob_part(step, buf, j, top):
        for k in (2 * j + 1, 2 * j + 2):
            p = jnp.exp(buf[:, 128 * k : 128 * k + 128] - top)
            PB[step // 4, block_of(step), 128 * k : 128 * k + 128] = p.astype(BF)

    def mix(step):
        head, q0 = unit_of(step)
        mixed = dot(PB[step // 4, block_of(step), 128:2176], VN[...])
        inv = 1.0 / mixed[:, 128:129]
        lane = iota((BQ, 128), 1)
        LI[block_of(step), :] = jnp.where(lane == step // 4, inv, LI[block_of(step), :])
        mixed = mixed[:, 0:128] * inv
        ON[pl.ds(q0, BQ), :] = jnp.where(lane // 64 == head, mixed, cast_up(ON[pl.ds(q0, BQ), :])).astype(BF)

    def first_scores(step):
        top = None
        for j in range(8):
            top = score_part(step, SC, j, top)
        return score_end(step, SC, top)

    def attend(pair, top_a):
        one, two = 2 * pair, 2 * pair + 1
        top_b = None
        for j in range(8):
            top_b = score_part(two, S2, j, top_b)
            prob_part(one, SC, j, top_a)
        top_b = score_end(two, S2, top_b)
        mix(one)
        then = jnp.minimum(two + 1, STEPS - 1)
        top_a = None
        for j in range(8):
            prob_part(two, S2, j, top_b)
            top_a = score_part(then, SC, j, top_a)
        top_a = score_end(then, SC, top_a)
        mix(two)
        return top_a

    A = r["A"]
    base_o = comm.take(8)
    base_or = comm.take(8)

    def give(half, n):
        for i in range(4):
            yy, hh = 2 * half + i // 2, i % 2
            src = ON.at[pl.ds(pl.multiple_of(256 * (yy * 2 + hh), 256), 256)]
            dst = A.at[zh, :, pl.ds(pl.multiple_of(128 * y, 128), 128)]
            own = (yy == y) & (hh == zh)
            cp = comm.copy(src, dst, base_o + 4 * n + i, dev(x, yy, hh * 2 + zl, c), base_or + y * 2 + zh)
            keep = pltpu.make_async_copy(src, dst, comm.rs.at[base_or + y * 2 + zh])
            pl.when(own)(keep.start)
            pl.when(jnp.logical_not(own))(cp.start)
            comm.pending.append((cp, own))

    single = (3 * t + 1) % 2
    top_now = lax.fori_loop(0, 2, attend, first_scores(0))
    give(single, 0)
    top_now = lax.fori_loop(2, 3, attend, top_now)
    ff_a2.forward()
    ff_b2.forward()
    lax.fori_loop(3, STEPS // 2, attend, top_now)
    give(1 - single, 1)
    ff_a2.wait()
    ff_b2.wait()
    for yy in range(4):
        for hh in range(2):
            comm.recv(A.at[hh, :, pl.ds(128 * yy, 128)], base_or + yy * 2 + hh)
    comm.recv(TK.at[:, 1 - c], pair)
    comm.recv(CT.at[:, 1 - c], pair + 1)
    comm.drain()

    lane = iota((256, 128), 1)
    for hh in range(2):
        p0, p1, p2, p3 = [cast_up(A[hh, :, 128 * k : 128 * k + 128]) for k in range(4)]
        p1, p2 = pltpu.roll(p1, 64, 1), pltpu.roll(p2, 64, 1)
        A[hh, :, 0:128] = (p0 + jnp.where(lane >= 64, p1, 0.0)).astype(BF)
        A[hh, :, 128:256] = jnp.where(lane < 64, p1, p2).astype(BF)
        A[hh, :, 256:384] = (p3 + jnp.where(lane < 64, p2, 0.0)).astype(BF)
    for cc in range(2):
        for yy in range(3):
            comm.recv(WOF.at[:, :, :, pl.ds(128 * (cc * 3 + yy), 128)], base_wr + cc * 4 + yy)

    POS, POR, N2, N2T = r["POS"], r["POR"], r["N2"], r["N2T"]
    base_p = comm.take(2)
    for hh in range(2):
        term = dot(A[hh, :, 0:384], WOF[...].reshape(384, D))
        POS[hh] = term.astype(BF).reshape(2, 128, D)
        comm.send(POS.at[hh], POR.at[hh], base_p + hh, sib)
    second_gain = r["GS"][1:2, 0:768]
    for hh in range(2):
        comm.recv(POR.at[hh], base_p + hh)
        for k in range(2):
            middle = cast_up(TK[hh, k]) + (cast_up(POS[hh, k]) + cast_up(POR[hh, k]))
            S2[128 * hh : 128 * hh + 128, 768 * k : 768 * k + 768] = middle
            normed = middle * rms_scale(middle) * second_gain
            N2[128 * k : 128 * k + 128, 768 * hh : 768 * hh + 768] = normed.astype(BF)
            at = 256 * hh + 128 * k
            N2T[:, at : at + 128] = normed.T.astype(BF)

    HX, HIDT, GU = r["HX"], r["HIDT"], r["GU"]

    def gated(k, carry):
        gate_w = W1[:, :, :, k, :, 0:256].reshape(D, 256)
        up_w = W1[:, :, :, k, :, 256:512].reshape(D, 256)
        down_w = WD[k // 2, pl.ds((2 * k) % 4, 2)].reshape(256, D)
        for hh in range(2):
            gate = dot(N2[:, 768 * hh : 768 * hh + 768], gate_w)
            up = dot(N2[:, 768 * hh : 768 * hh + 768], up_w)
            back = dot_nt(CT[hh].reshape(256, D), down_w)
            square = gate * gate
            th = jnp.tanh(0.7978845608028654 * (gate + 0.044715 * (square * gate)))
            half = 0.5 * (1.0 + th)
            gelu = gate * half
            slope = half + (0.5 * gate) * (1.0 - th * th) * (
                0.7978845608028654 * (1.0 + 3 * 0.044715 * square)
            )
            hidden = gelu * up
            cols = pl.ds(pl.multiple_of(256 * k, 256), 256)
            HX[:, pl.ds(pl.multiple_of(1024 * hh + 256 * k, 256), 256)] = hidden.astype(BF)
            HIDT[cols, 256 * hh : 256 * hh + 256] = hidden.T.astype(BF)
            both = pl.multiple_of(512 * k, 512)
            GU[hh, :, :, pl.ds(both, 256)] = (back * up * slope).astype(BF).reshape(2, 128, 256)
            GU[hh, :, :, pl.ds(both + 256, 256)] = (back * gelu).astype(BF).reshape(2, 128, 256)
        return carry

    lax.fori_loop(0, 4, gated, 0)
    PNR, SC = r["PNR"], r["SC"]
    base_n = comm.take(2)
    comm.drain()
    for hh in range(2):
        term = dot_nt(GU[hh, :, :, 0:512].reshape(256, 512), W1[:, :, :, 0].reshape(D, 512))
        for k in range(1, 4):
            term += dot_nt(
                GU[hh, :, :, 512 * k : 512 * k + 512].reshape(256, 512), W1[:, :, :, k].reshape(D, 512)
            )
        POS[hh] = term.astype(BF).reshape(2, 128, D)
        comm.send(POS.at[hh], PNR.at[hh], base_n + hh, sib)
    PYS, PYR = r["PYS"], r["PYR"]
    yi = comm.take()
    down_all = WD[...].reshape(1024, D)
    for hh in range(2):
        PYS[hh] = dot(HX[pl.ds(pl.multiple_of(128 * (1 - c), 128), 128), 1024 * hh : 1024 * hh + 1024], down_all).astype(BF)
    comm.send(PYS, PYR, yi, sib)
    for hh in range(2):
        SC[128 * hh : 128 * hh + 128, 0:768] = dot(HX[pl.ds(pl.multiple_of(128 * c, 128), 128), 1024 * hh : 1024 * hh + 1024], down_all)

    def down_term(k, carry):
        res = dot(HIDT[pl.ds(pl.multiple_of(256 * k, 256), 256), :], CT[...].reshape(512, D))
        WD[k // 2, pl.ds((2 * k) % 4, 2)] = res.astype(BF).reshape(2, 2, 4, 16, D)
        return carry

    lax.fori_loop(0, 4, down_term, 0)
    wd_ra = Scatter(
        comm, "z", lambda zz: [WD.at[zz % 2, :, zz // 2, :, :, low_d]], [r["RA2"]]
    )
    wd_rb = Scatter(comm, "x", lambda xx: [WD.at[:, xx, :, :, :, high_d]], [r["RB2"]])
    wd_rb.start()

    ML, DOS, DO, VEC = r["ML"], r["DOS"], r["DO"], r["VEC"]
    VEC[...] = jnp.zeros((8, 1024), F32)
    base_d = comm.take(8)
    base_dr = comm.take(8)
    m = y * 2 + zh
    for hh in range(2):
        comm.recv(PNR.at[hh], base_n + hh)
        for k in range(2):
            grad = cast_up(POS[hh, k]) + cast_up(PNR[hh, k])
            middle = S2[128 * hh : 128 * hh + 128, 768 * k : 768 * k + 768]
            scale = rms_scale(middle)
            gained = grad * second_gain
            mean = jnp.mean(middle * gained, axis=-1, keepdims=True)
            full = cast_up(CT[hh, k]) + scale * gained - middle * (scale * scale * scale * mean)
            ML[hh, k] = full.astype(BF)

            @pl.when(c == k)
            def _():
                r["din"][hh] = full
                VEC[1:2, 0:768] += jnp.sum(grad * middle * scale, axis=0, keepdims=True)

        given = dot_nt(ML[hh].reshape(256, D), WOF[...].reshape(384, D))
        g0, g1, g2 = given[:, 0:128], given[:, 128:256], given[:, 256:384]
        r0, r1, r2 = pltpu.roll(g0, 64, 1), pltpu.roll(g1, 64, 1), pltpu.roll(g2, 64, 1)
        DOS[0, hh] = g0.astype(BF)
        DOS[1, hh] = jnp.where(lane < 64, r0, r1).astype(BF)
        DOS[2, hh] = jnp.where(lane < 64, r1, r2).astype(BF)
        DOS[3, hh] = g2.astype(BF)
        for yy in range(4):
            dst = DO.at[pl.ds(pl.multiple_of(256 * m, 256), 256)]
            own = (yy == y) & (hh == zh)
            cp = comm.copy(DOS.at[yy, hh], dst, base_d + 4 * hh + yy, dev(x, yy, hh * 2 + zl, c), base_dr + m)
            keep = pltpu.make_async_copy(DOS.at[yy, hh], dst, comm.rs.at[base_dr + m])
            pl.when(own)(keep.start)
            pl.when(jnp.logical_not(own))(cp.start)
            comm.pending.append((cp, own))


    def gated_term(k, carry):
        res = dot(N2T[...], GU[:, :, :, pl.ds(pl.multiple_of(512 * k, 512), 512)].reshape(512, 512))
        W1[:, :, :, k] = res.astype(BF).reshape(2, 4, 2, 48, 512)
        return carry

    lax.fori_loop(0, 4, gated_term, 0)
    pl.semaphore_signal(r["free_sem"], inc=1, device_id=sib, device_id_type=MESH)
    ff_ra = Scatter(comm, "z", lambda zz: [W1.at[zz % 2, :, zz // 2, :, :, low]], [r["RA1"]])
    ff_rb = Scatter(comm, "x", lambda xx: [W1.at[:, xx, :, :, :, high]], [r["RB1"]])
    ff_rb.start()
    attended_t = jnp.concatenate(
        [cast_up(A[hh, :, 0:384]).T.astype(BF) for hh in range(2)], axis=1
    )
    WOF[...] = dot(attended_t, ML[...].reshape(512, D)).astype(BF).reshape(4, 2, 48, D)
    base_g = comm.take(6)
    base_gr = comm.take(8)
    WOR = r["WOR"]
    for cc in range(2):
        for yy in range(3):
            src = WOF.at[:, :, :, pl.ds(128 * (cc * 3 + yy), 128)]
            cp = comm.copy(src, WOR.at[y, c], base_g + cc * 3 + yy, dev(x, yy, z, cc), base_gr + c * 4 + y)
            keep = pltpu.make_async_copy(src, WOR.at[y, c], comm.rs.at[base_gr + c * 4 + y])
            here = (yy == y) & (cc == c)
            pl.when(here)(keep.start)
            pl.when(jnp.logical_not(here))(cp.start)
            comm.pending.append((cp, here))
    comm.recv(PYR, yi)
    for hh in range(2):
        middle = S2[128 * hh : 128 * hh + 128, pl.ds(pl.multiple_of(768 * c, 128), 768)]
        r["out"][hh] = (middle + SC[128 * hh : 128 * hh + 128, 0:768] + cast_up(PYR[hh])).astype(BF)
    stores = [pltpu.make_async_copy(r["out"], r["h_out"], local_sem.at[10])]
    stores[0].start()

    SC[:, 0:2048] = jnp.zeros((256, SEQ), F32)
    S2[0:128, 0:2048] = jnp.zeros((128, SEQ), F32)
    N2[:, 0:1024] = jnp.zeros((BQ, 1024), BF)
    BT[...] = jnp.zeros((2, 256, 512), F32)
    for yy in range(4):
        for hh in range(2):
            comm.recv(DO.at[pl.ds(256 * (yy * 2 + hh), 256)], base_dr + yy * 2 + hh)
    wd_ra.start()
    ff_ra.start()

    GL, DL = r["GL"], r["DL"]

    def retreat(ui, carry):
        head, q0 = unit_of(4 * ui)
        rows = pl.ds(pl.multiple_of(q0, 1024), 1024)
        lane = iota((1024, 128), 1)
        inv = jnp.sum(jnp.where(lane == ui, LI[...], 0.0), axis=1, keepdims=True)
        given = jnp.where(lane // 64 == head, cast_up(DO[rows, :]) * inv, 0.0)
        GL[...] = given.astype(BF)
        delta = jnp.sum(cast_up(GL[...]) * cast_up(ON[rows, :]), axis=1, keepdims=True)
        DL[...] = jnp.broadcast_to(delta, (1024, 128))
        given_t = given.T.astype(BF)
        for j in range(8):
            S2[0:128, 256 * j : 256 * j + 256] += dot(given_t, PB[ui, :, 128 + 256 * j : 384 + 256 * j])

        def inner(b, more):
            block = pl.ds(pl.multiple_of(256 * b, 256), 256)
            low_rows = GL[block, :]
            shift = DL[block, 0:1]
            for j in range(8):
                cols = slice(128 + 256 * j, 384 + 256 * j)
                grad = dot(low_rows, VT[:, 256 * j : 256 * j + 256])
                PB[ui, block, cols] = (cast_up(PB[ui, block, cols]) * (grad - shift)).astype(BF)
            moved = dot(PB[ui, block, 128:2176], KN[...])
            at = q0 + 256 * b
            lane = iota((BQ, 128), 1)
            spot = pl.ds(pl.multiple_of(at // 2, 128), 128)
            N2[:, spot] = jnp.where(lane // 64 == head, moved, cast_up(N2[:, spot])).astype(BF)
            BT[head] += cast_up(PB[ui, block, pl.ds(pl.multiple_of(at, 256), 512)])
            return more

        lax.fori_loop(0, 4, inner, 0)
        query_t = cast_up(QA[head, rows, :]).T.astype(BF)
        key_rows = pl.ds(pl.multiple_of(128 * head, 128), 128)
        for j in range(8):
            SC[key_rows, 256 * j : 256 * j + 256] += dot(query_t, PB[ui, :, 128 + 256 * j : 384 + 256 * j])
        return carry

    def add_low(refs, bufs):
        for ref, buf in zip(refs, bufs):
            total = cast_up(ref[...])
            for k in range(3):
                total += cast_up(buf[k])
            ref[...] = total.astype(BF)

    lax.fori_loop(0, 3, retreat, 0)

    YR, DWQ = r["YR"], r["DWQ"]
    first_gain = r["GS"][0:1, 0:768]
    base_s = comm.take(4)
    S2[128:256, :] = jnp.zeros((128, 2304), F32)

    def sib_at(yy):
        return GU.at[yy // 2, :, :, pl.ds(pl.multiple_of((yy % 2) * 1024, 128), 768)]

    def place_of(k):
        return (y + jnp.where(k == 0, 2, jnp.where(k == 1, 1, jnp.where(k == 2, 3, 0)))) % 4

    def spread_back(k, carry):
        yy = place_of(k)

        def half(hh, inner):
            at = pl.ds(pl.multiple_of(512 * yy + 256 * hh, 256), 256)
            raw = cast_up(T5[yy, hh].reshape(256, D))
            scale = rms_scale(raw)
            normed = (raw * scale * first_gain).astype(BF)
            dq = N2[:, pl.ds(pl.multiple_of(256 * yy + 128 * hh, 128), 128)]
            sub = iota((128, 256), 0)
            dkt = jnp.where(sub < 64, SC[0:128, at], SC[128:256, at])
            dvt = S2[0:128, at]
            dk, dv = dkt.T.astype(BF), dvt.T.astype(BF)
            dqt = cast_up(dq).T.astype(BF)
            grad = dot_nt(jnp.concatenate([dq, dk, dv], axis=1), WQ[:, :, :, :, 0:384].reshape(D, 384))
            VEC[0:1, 0:768] += jnp.sum(grad * raw * scale, axis=0, keepdims=True)
            S2[128:256, 0:768] += dot(dqt, normed)
            S2[128:256, 768:1536] += dot(dkt.astype(BF), normed)
            S2[128:256, 1536:2304] += dot(dvt.astype(BF), normed)
            T5[yy, hh] = grad.astype(BF).reshape(2, 128, D)
            return inner

        lax.fori_loop(0, 2, half, 0)
        comm.copy(T5.at[yy, :, 1 - c], sib_at(yy), base_s + k, sib).start()
        return carry

    base_y = comm.take(3)

    def pass_on(k):
        yy = (y + (2, 1, 3, 0)[k]) % 4
        comm.recv(sib_at(yy), base_s + k)
        for hh in range(2):
            T5[yy, hh, c] = (cast_up(T5[yy, hh, c]) + cast_up(sib_at(yy)[hh])).astype(BF)
        if k < 3:
            comm.send(T5.at[yy, :, c], YR.at[k], base_y + k, comm.peer("y", (2, 1, 3)[k]))

    pl.semaphore_wait(r["free_sem"], 1)
    for k in range(4):
        spread_back(k, 0)
        if k:
            pass_on(k - 1)
    for i in range(3):
        DWQ[:, :, :, :, 128 * i : 128 * i + 128] = S2[128:256, 768 * i : 768 * i + 768].T.astype(BF).reshape(2, 4, 2, 48, 128)

    @pl.when(y == 3)
    def _():
        DWQ[:, :, :, :, 384:512] = jnp.zeros((2, 4, 2, 48, 128), BF)

    @pl.when(y < 3)
    def _():
        for k in range(4):
            for cc in range(2):
                comm.recv(WOR.at[k, cc], base_gr + cc * 4 + k)
        for cc in range(2):
            total = cast_up(WOR[0, cc])
            for k in range(1, 4):
                total += cast_up(WOR[k, cc])
            DWQ[cc, :, :, :, 384:512] = total.astype(BF)

    q_ra = Scatter(
        comm,
        "z",
        lambda zz: [DWQ.at[zz % 2, :, zz // 2, :, low]],
        [r["QA1"]],
    )
    q_rb = Scatter(
        comm,
        "x",
        lambda xx: [DWQ.at[:, xx, :, :, high]],
        [r["QB1"]],
    )
    lane = iota((8, 128), 1)
    sub = iota((8, 128), 0)
    diagonals = []
    flip = jnp.where(iota((256, 256), 0) + iota((256, 256), 1) == 255, 1.0, 0.0).astype(BF)
    table_grad = jnp.zeros((1, 128), F32)
    one = iota((1, 128), 1)
    for h in range(2):
        near = jnp.zeros((1, 1024), F32)
        whole = BT[h]
        upper = whole.astype(BF)
        lower = (whole - cast_up(upper)).astype(BF)
        flipped = dot(flip, upper) + dot(flip, lower)
        for k in range(4):
            part = jnp.concatenate([flipped[64 * k : 64 * k + 64], jnp.zeros((64, 512), F32)], axis=1)
            part = pltpu.roll(part, 129 + 64 * k, 1, stride=1, stride_axis=0)
            near += jnp.sum(part, axis=0, keepdims=True)
        diagonals.append(near)
        base = 64 * (1 - h)
        rows_far = SC[128 * h + base : 128 * h + base + 8, 0:2048]
        key_at = iota((8, SEQ), 1)
        start = 256 * iota((8, SEQ), 0)
        left = jnp.sum(jnp.where(key_at < start - 128, rows_far, 0.0), axis=(0, 1), keepdims=True)
        right = jnp.sum(jnp.where(key_at >= start + 384, rows_far, 0.0), axis=(0, 1), keepdims=True)
        table_grad += jnp.where(one == 32 * h + 15, left, 0.0) + jnp.where(one == 32 * h + 31, right, 0.0)
    near = jnp.concatenate(diagonals + [jnp.zeros((6, 1024), F32)], axis=0)
    upper = near.astype(BF)
    lower = (near - cast_up(upper)).astype(BF)
    sums = dot_nt(upper, r["OH"][...]) + dot_nt(lower, r["OH"][...])
    table_grad += jnp.sum(jnp.where(lane // 32 == sub, sums, 0.0), axis=0, keepdims=True)
    spread = jnp.concatenate([table_grad, jnp.zeros((1, 256), F32)], axis=1)
    spread = pltpu.roll(jnp.broadcast_to(spread, (8, 384)), 32 * h0, 1)
    VEC[0:1, 768:1024] = spread[0:1, 0:256]
    VEC[1:2, 768:896] = spread[0:1, 256:384]

    v_z = Scatter(comm, "z", lambda zz: [VEC], [r["V1"]])
    q_ra.start()
    q_rb.start()
    v_z.start()
    pass_on(3)
    wd_ra.wait()
    wd_rb.wait()
    ff_ra.wait()
    ff_rb.wait()

    def add_a(i, carry):
        add_low(
            [W1.at[zl, i, zh, :, :, low], WD.at[zl, i, zh, :, :, low_d]],
            [r["RA1"].at[:, i], r["RA2"].at[:, i]],
        )
        add_low(
            [W1.at[i // 2, x, i % 2, :, :, high], WD.at[i // 2, x, i % 2, :, :, high_d]],
            [r["RB1"].at[:, i // 2, i % 2], r["RB2"].at[:, i // 2, i % 2]],
        )
        return carry

    lax.fori_loop(0, 4, add_a, 0)
    ff_ra2 = Scatter(
        comm,
        "x",
        lambda xx: [W1.at[zl, xx, zh, :, :, low], WD.at[zl, xx, zh, :, :, low_d]],
        [r["SA1"], r["SA2"]],
    )
    ff_rb2 = Scatter(
        comm,
        "z",
        lambda zz: [
            W1.at[zz % 2, x, zz // 2, :, :, high],
            WD.at[zz % 2, x, zz // 2, :, :, high_d],
        ],
        [r["SB1"], r["SB2"]],
    )
    ff_ra2.start()
    ff_rb2.start()
    q_ra.wait()
    q_rb.wait()
    v_z.wait()
    for i in range(4):
        add_low([DWQ.at[zl, i, zh, :, low]], [r["QA1"].at[:, i]])
        add_low([DWQ.at[i // 2, x, i % 2, :, high]], [r["QB1"].at[:, i // 2, i % 2]])
    VE2 = r["VE2"]
    VE2[...] = VEC[...] + r["V1"][0] + r["V1"][1] + r["V1"][2]
    q_ra2 = Scatter(comm, "x", lambda xx: [DWQ.at[zl, xx, zh, :, low]], [r["QA2"]])
    q_rb2 = Scatter(comm, "z", lambda zz: [DWQ.at[zz % 2, x, zz // 2, :, high]], [r["QB2"]])
    v_x = Scatter(comm, "x", lambda xx: [VE2], [r["V2"]])
    q_ra2.start()
    q_rb2.start()
    v_x.start()
    ff_ra2.wait()
    ff_rb2.wait()
    add_low([W1.at[zl, x, zh, :, :, low], WD.at[zl, x, zh, :, :, low_d]], [r["SA1"], r["SA2"]])
    add_low([W1.at[zl, x, zh, :, :, high], WD.at[zl, x, zh, :, :, high_d]], [r["SB1"], r["SB2"]])
    ff_ry = Scatter(
        comm, "y", lambda yy: [W1.at[zl, x, zh, yy], WD.at[zl, x, zh, yy]], [r["SY1"], r["SY2"]]
    )
    ff_ry.start()

    for k in range(3):
        comm.recv(YR.at[k], base_y + k)
    zri = comm.take()
    ZS, ZR = r["ZS"], r["ZR"]

    def summed(hh):
        total = cast_up(T5[y, hh, c])
        for k in range(3):
            total += cast_up(YR[k, hh])
        return total

    ZS[...] = summed(1 - zh).astype(BF)
    comm.send(ZS, ZR, zri, other)

    def finish(hh, grad):
        raw = cast_up(TK[hh, c])
        scale = rms_scale(raw)
        gained = grad * first_gain
        mean = jnp.mean(raw * gained, axis=-1, keepdims=True)
        r["din"][hh] = r["din"][hh] + scale * gained - raw * (scale * scale * scale * mean)

    finish(zh, summed(zh))

    ff_ry.wait()
    total = cast_up(W1[zl, x, zh, y])
    for k in range(3):
        total += cast_up(r["SY1"][k])
    asm[:, 512:1024] = total
    q_ra2.wait()
    q_rb2.wait()
    v_x.wait()
    total = cast_up(WD[zl, x, zh, y])
    for k in range(3):
        total += cast_up(r["SY2"][k])
    r["WDG"][...] = total
    home = (2 * c + zh, y // 2, y % 2)
    own_home = (home[0] == y) & (home[1] == zh) & (home[2] == c)
    dwi = comm.take()
    comm.send_or_keep(
        r["WDG"], r["dwd_in"], dwi, dev(x, home[0], home[1] * 2 + zl, home[2]), dwi, own_home
    )
    for cols, buf in ((low, r["QA2"]), (high, r["QB2"])):
        total = cast_up(DWQ[zl, x, zh, :, cols])
        for k in range(3):
            total += cast_up(buf[k])
        asm[:, cols] = total
    sums = VE2[...] + r["V2"][0] + r["V2"][1] + r["V2"][2]
    W2R = r["W2R"]
    base_h = comm.take(8)
    base_hr = comm.take(8)
    mine = c * 4 + y
    for j in range(8):
        wst[j, 0:6, :] = asm[6 * j : 6 * j + 6, :]
        wst[j, 6:8, :] = sums[0:2]
        ys, hs, cs = 2 * zh + j // 4, (j // 2) % 2, j % 2
        own = (ys == y) & (hs == zh) & (cs == c)
        cp = comm.copy(wst.at[j], W2R.at[mine], base_h + j, dev(x, ys, hs * 2 + zl, cs), base_hr + mine)
        keep = pltpu.make_async_copy(wst.at[j], W2R.at[mine], comm.rs.at[base_hr + mine])
        pl.when(own)(keep.start)
        pl.when(jnp.logical_not(own))(cp.start)
        comm.pending.append((cp, own))
    comm.recv(ZR, zri)
    finish(1 - zh, cast_up(ZR[...]))
    for d in range(8):
        comm.recv(W2R.at[d], base_hr + d)
    for name in ("dwq", "dwk", "dwv"):
        r[name][...] = jnp.zeros((6, D), F32)
    rows_sum = jnp.zeros((2, 1024), F32)
    for cc in range(2):
        for yy in range(4):
            d, first = cc * 4 + yy, 64 * first_head(cc * 4 + yy)
            for i, name in enumerate(("dwq", "dwk", "dwv")):
                r[name][:, first : first + 128] += W2R[d, 0:6, 128 * i : 128 * i + 128]
            for i, name in enumerate(("dwg", "dwu")):
                for k in range(2):
                    tile = 2 * (2 * yy + k) + cc
                    at = 512 + 256 * i + 128 * k
                    r[name][:, 128 * tile : 128 * tile + 128] = W2R[d, 0:6, at : at + 128]
            if yy < 3:
                at = (cc * 3 + yy) * 128
                r["dwo"][:, at : at + 128] = W2R[d, 0:6, 384:512]
            rows_sum += W2R[d, 6:8, :]
    table = jnp.concatenate([rows_sum[0:1, 768:1024], rows_sum[1:2, 768:1024], rows_sum[0:1, 0:512]], axis=1)
    gains = jnp.broadcast_to(jnp.concatenate([rows_sum, jnp.zeros((6, 1024), F32)], axis=0), (8, 1024))
    gains = pltpu.roll(gains, 1024 - 6 * flat, 1)[0:2, 0:128]
    table = pltpu.roll(jnp.broadcast_to(table, (8, 1024)), 1024 - 3 * flat, 1)[0:1, 0:128]
    r["dvec"][...] = jnp.concatenate([gains, table, jnp.zeros((5, 128), F32)], axis=0)
    comm.recv(r["dwd_in"], dwi)
    names = ("din", "dwq", "dwk", "dwv", "dwo", "dwg", "dwu", "dwd", "dvec")
    for i, name in enumerate(names):
        src = r["dwd_in"] if name == "dwd" else r[name]
        stores.append(pltpu.make_async_copy(src, r["h_" + name], local_sem.at[11 + i]))
        stores[-1].start()
    for k in range(4):
        yy = (y + (2, 1, 3, 0)[k]) % 4
        comm.copy(T5.at[yy, :, 1 - c], sib_at(yy), base_s + k, sib).wait_send()
    comm.drain()
    for store in stores:
        store.wait()


INPUTS = [
    ("lens", "s"), ("g1", "s"), ("g2", "s"), ("bt", "s"),
    ("tok", "a"), ("cot", "a"), ("h_wq", "a"), ("h_wk", "a"), ("h_wv", "a"), ("h_wo", "a"),
    ("h_wg", "a"), ("h_wu", "a"), ("h_wd", "a"),
]
SCRATCH = [
    ("W1", ((2, 4, 2, 4, 48, 512), BF)),
    ("WD", ((2, 4, 2, 4, 16, 768), BF)),
    ("WQ", ((2, 4, 2, 48, 512), BF)),
    ("G5", ((2, 4, 2, 8, 1024), F32)),
    ("T5", ((4, 2, 2, 128, 768), BF)),
    ("TK", ((2, 2, 128, 768), BF)),
    ("CT", ((2, 2, 128, 768), BF)),
    ("wst", ((8, 8, 1024), F32)),
    ("w0", ((8, 8, 1024), F32)),
    ("asm", ((48, 1024), F32)),
    ("wdst", ((16, 768), BF)),
    ("GS", ((8, 1024), F32)),
    ("OH", ((128, 1024), BF)),
    ("BO", ((8, 1024), F32)),
    ("BT", ((2, 256, 512), F32)),
    ("QA", ((2, 2048, 128), BF)),
    ("KT", ((2, 128, 2048), BF)),
    ("KN", ((2048, 128), BF)),
    ("VN", ((2048, 256), BF)),
    ("VT", ((128, 2048), BF)),
    ("SC", ((256, 2304), F32)),
    ("S2", ((256, 2304), F32)),
    ("PB", ((3, 1024, 2304), BF)),
    ("ON", ((2048, 128), BF)),
    ("LI", ((1024, 128), F32)),
    ("GL", ((1024, 128), BF)),
    ("DL", ((1024, 128), F32)),
    ("A", ((2, 256, 512), BF)),
    ("WOF", ((4, 2, 48, 768), BF)),
    ("POS", ((2, 2, 128, 768), BF)),
    ("POR", ((2, 2, 128, 768), BF)),
    ("N2", ((256, 1536), BF)),
    ("N2T", ((768, 512), BF)),
    ("HIDT", ((1024, 512), BF)),
    ("GU", ((2, 2, 128, 2048), BF)),
    ("PNR", ((2, 2, 128, 768), BF)),
    ("PYS", ((2, 128, 768), BF)),
    ("PYR", ((2, 128, 768), BF)),
    ("ML", ((2, 2, 128, 768), BF)),
    ("DOS", ((4, 2, 256, 128), BF)),
    ("DO", ((2048, 128), BF)),
    ("RA1", ((3, 4, 4, 48, 256), BF)),
    ("RA2", ((3, 4, 4, 16, 384), BF)),
    ("RB1", ((3, 2, 2, 4, 48, 256), BF)),
    ("RB2", ((3, 2, 2, 4, 16, 384), BF)),
    ("SA1", ((3, 4, 48, 256), BF)),
    ("SA2", ((3, 4, 16, 384), BF)),
    ("SB1", ((3, 4, 48, 256), BF)),
    ("SB2", ((3, 4, 16, 384), BF)),
    ("SY1", ((3, 48, 512), BF)),
    ("SY2", ((3, 16, 768), BF)),
    ("WOR", ((4, 2, 4, 2, 48, 128), BF)),
    ("HX", ((256, 2304), BF)),
    ("YR", ((3, 2, 128, 768), BF)),
    ("ZS", ((128, 768), BF)),
    ("ZR", ((128, 768), BF)),
    ("DWQ", ((2, 4, 2, 48, 512), BF)),
    ("QA1", ((3, 4, 48, 256), BF)),
    ("QA2", ((3, 48, 256), BF)),
    ("QB1", ((3, 2, 2, 48, 256), BF)),
    ("QB2", ((3, 48, 256), BF)),
    ("VEC", ((8, 1024), F32)),
    ("V1", ((3, 8, 1024), F32)),
    ("V2", ((3, 8, 1024), F32)),
    ("VE2", ((8, 1024), F32)),
    ("W2R", ((8, 8, 1024), F32)),
    ("WDG", ((16, 768), F32)),
    ("dwd_in", ((16, 768), F32)),
    ("out", ((2, 128, 768), BF)),
    ("din", ((2, 128, 768), F32)),
    ("dwq", ((6, 768), F32)),
    ("dwk", ((6, 768), F32)),
    ("dwv", ((6, 768), F32)),
    ("dwo", ((6, 768), F32)),
    ("dwg", ((6, 2048), F32)),
    ("dwu", ((6, 2048), F32)),
    ("dvec", ((8, 128), F32)),
    ("wq", ((6, 768), F32)),
    ("wk", ((6, 768), F32)),
    ("wv", ((6, 768), F32)),
    ("wo", ((6, 768), F32)),
    ("wg", ((6, 2048), F32)),
    ("wu", ((6, 2048), F32)),
    ("wd", ((16, 768), F32)),
    ("free_sem", 0),
    ("local_sem", 32),
    ("send_sem", None),
    ("recv_sem", None),
]


OUTPUTS = [
    ("h_out", ((2, 128, 768), BF)),
    ("h_din", ((2, 128, 768), F32)),
    ("h_dwq", ((6, 768), F32)),
    ("h_dwk", ((6, 768), F32)),
    ("h_dwv", ((6, 768), F32)),
    ("h_dwo", ((6, 768), F32)),
    ("h_dwg", ((6, 2048), F32)),
    ("h_dwu", ((6, 2048), F32)),
    ("h_dwd", ((16, 768), F32)),
    ("h_dvec", ((8, 128), F32)),
]


def call_mega(*args):
    spec = {"s": pl.BlockSpec(memory_space=pltpu.SMEM), "a": pl.BlockSpec(memory_space=pl.ANY)}
    outs = OUTPUTS
    scratch = []
    for _, s in SCRATCH:
        if s == 0:
            scratch.append(pltpu.SemaphoreType.REGULAR)
        elif s is None or isinstance(s, int):
            scratch.append(pltpu.SemaphoreType.DMA((s or NSEM,)))
        else:
            scratch.append(pltpu.VMEM(s[0], s[1]))
    return pl.pallas_call(
        mega,
        out_shape=[jax.ShapeDtypeStruct(s[0], s[1]) for _, s in outs],
        in_specs=[spec[k] for _, k in INPUTS],
        out_specs=[pl.BlockSpec(memory_space=pl.ANY) for _ in outs],
        scratch_shapes=scratch,
        name="layer",
        compiler_params=pltpu.CompilerParams(
            collective_id=0, has_side_effects=True, vmem_limit_bytes=62 * 2**20
        ),
    )(*args)


def per_device(
    tokens,
    lengths,
    cotangent,
    query_weight,
    key_weight,
    value_weight,
    out_weight,
    gate_weight,
    up_weight,
    down_weight,
    first_gain,
    second_gain,
    bias_table,
):
    done = call_mega(
        lengths,
        first_gain,
        second_gain,
        bias_table,
        tokens,
        cotangent,
        query_weight,
        key_weight,
        value_weight,
        out_weight,
        gate_weight,
        up_weight,
        down_weight,
    )
    return hand_out(*done)


def hand_out_kernel(*refs):
    n = len(OUTPUTS)
    vectors, ins, outs, held, sem = refs[0], refs[1:n], refs[n : 2 * n + 2], refs[2 * n + 2 : -1], refs[-1]
    loads = [pltpu.make_async_copy(a, b, sem.at[i]) for i, (a, b) in enumerate(zip(ins, held))]
    copies = [pltpu.make_async_copy(a, b, sem.at[i]) for i, (a, b) in enumerate(zip(held, outs))]
    for load in loads:
        load.start()
    for load, copy in zip(loads, copies):
        load.wait()
        copy.start()
    for row, (ref, width) in enumerate(zip(outs[n - 1 :], (6, 6, 3))):
        for i in range(width):
            ref[i] = vectors[row, i]
    for copy in copies:
        copy.wait()


def hand_out(*done):
    shapes = [jax.ShapeDtypeStruct(s[0], s[1]) for _, s in OUTPUTS[:-1]]
    shapes += [jax.ShapeDtypeStruct((n,), F32) for n in (6, 6, 3)]
    smem, hbm = pl.BlockSpec(memory_space=pltpu.SMEM), pl.BlockSpec(memory_space=pl.ANY)
    n = len(done) - 1
    return tuple(
        pl.pallas_call(
            hand_out_kernel,
            out_shape=shapes,
            in_specs=[smem] + [hbm] * n,
            out_specs=[hbm] * n + [smem] * 3,
            scratch_shapes=[pltpu.VMEM(s[0], s[1]) for _, s in OUTPUTS[:-1]]
            + [pltpu.SemaphoreType.DMA((n,))],
            name="hand_out",
        )(done[-1], *done[:-1])
    )


def solution(mesh):
    tokens = P("rows", "seq", None)
    matrix = P(("rows", "seq"), None)
    vector = P(("rows", "seq"))
    return jax.shard_map(
        per_device,
        mesh=mesh,
        in_specs=(tokens, P("rows"), tokens, *([matrix] * 7), *([vector] * 3)),
        out_specs=(tokens, tokens, *([matrix] * 7), *([vector] * 3)),
        check_vma=False,
    )
```

```python
import jax
import jax.numpy as jnp
from jax import lax
from jax.experimental import pallas as pl
from jax.experimental.pallas import tpu as pltpu
from jax.sharding import PartitionSpec as P

MESH = pl.DeviceIdType.MESH
BF = jnp.bfloat16
F32 = jnp.float32
D = 768
SEQ = 2048
EPSILON = 1e-06
NEGATIVE = -1e30
LIMITS = (1, 2, 3, 4, 5, 6, 7, 8, 12, 16, 23, 32, 46, 64, 91)
NSEM = 240
BQ = 256
STEPS = 12


def dev(x, y, z, c):
    return ((z % 2) * 4 + x, (y * 2 + z // 2) * 2 + c)


def first_head(t):
    return (3 * t) // 2


def iota(shape, dim):
    return lax.broadcasted_iota(jnp.int32, shape, dim)


def dot(a, b):
    return jnp.dot(a, b, preferred_element_type=F32)


def dot_nt(a, b):
    return lax.dot_general(a, b, (((1,), (1,)), ((), ())), preferred_element_type=F32)


class Comm:
    def __init__(self, x, y, z, c, send_sem, recv_sem):
        self.x, self.y, self.z, self.c = x, y, z, c
        self.ss, self.rs = send_sem, recv_sem
        self.next = 0
        self.pending = []

    def take(self, n=1):
        at = self.next
        self.next += n
        assert self.next <= NSEM
        return at

    def peer(self, axis, offset):
        x, y, z, c = self.x, self.y, self.z, self.c
        if axis == "x":
            return dev((x + offset) % 4, y, z, c)
        if axis == "y":
            return dev(x, (y + offset) % 4, z, c)
        if axis == "z":
            return dev(x, y, (z + offset) % 4, c)
        return dev(x, y, z, 1 - c)

    def place(self, axis, offset):
        at = {"x": self.x, "y": self.y, "z": self.z}[axis]
        return (at + offset) % 4

    def copy(self, src, dst, i, to, j=None):
        return pltpu.make_async_remote_copy(
            src_ref=src,
            dst_ref=dst,
            send_sem=self.ss.at[i],
            recv_sem=self.rs.at[i if j is None else j],
            device_id=to,
            device_id_type=MESH,
        )

    def send(self, src, dst, i, to):
        cp = self.copy(src, dst, i, to)
        cp.start()
        self.pending.append(cp)

    def recv(self, dst, i):
        self.copy(dst, dst, i, self.peer("c", 0)).wait_recv()

    def send_or_keep(self, src, dst, i, to, j, own):
        cp = self.copy(src, dst, i, to, j)
        keep = pltpu.make_async_copy(src, dst, self.rs.at[j])

        @pl.when(own)
        def _():
            keep.start()

        @pl.when(jnp.logical_not(own))
        def _():
            cp.start()

        self.pending.append((cp, own))

    def drain(self):
        for cp in self.pending:
            if isinstance(cp, tuple):
                cp, own = cp

                @pl.when(jnp.logical_not(own))
                def _():
                    cp.wait_send()
            else:
                cp.wait_send()
        self.pending = []


class Direct:
    def __init__(self, comm, axis, views):
        self.comm, self.axis, self.views = comm, axis, views
        self.count = len(views(comm.place(axis, 0)))
        self.base = comm.take(3 * self.count)

    def start(self):
        for k, off in enumerate((1, 3, 2)):
            for n, ref in enumerate(self.views(self.comm.place(self.axis, 0))):
                self.comm.send(ref, ref, self.base + k * self.count + n, self.comm.peer(self.axis, off))

    def wait(self):
        for k, off in enumerate((1, 3, 2)):
            for n, ref in enumerate(self.views(self.comm.place(self.axis, -off + 4))):
                self.comm.recv(ref, self.base + k * self.count + n)


class Ring:
    def __init__(self, comm, axis, views, halves):
        self.comm, self.axis, self.views, self.halves = comm, axis, views, halves
        self.count = len(views(comm.place(axis, 0)))
        self.base = comm.take(4 * self.count)

    def start(self, source=None):
        own = self.views(self.comm.place(self.axis, 0))
        for n, ref in enumerate(own):
            src = ref if source is None else source[n]
            for k, off in enumerate((1, 3)):
                self.comm.send(src, ref, self.base + k * self.count + n, self.comm.peer(self.axis, off))

    def forward(self):
        for k, off in enumerate((1, 3)):
            came = self.comm.place(self.axis, -off + 4)
            for n, ref in enumerate(self.views(came)):
                self.comm.recv(ref, self.base + k * self.count + n)
            for n, ref in enumerate(self.halves(came, k)):
                self.comm.send(ref, ref, self.base + (2 + k) * self.count + n, self.comm.peer(self.axis, off))

    def wait(self):
        far = self.comm.place(self.axis, 2)
        for k in range(2):
            for n, ref in enumerate(self.halves(far, k)):
                self.comm.recv(ref, self.base + (2 + k) * self.count + n)


class Scatter:
    def __init__(self, comm, axis, views, bufs):
        self.comm, self.axis, self.views, self.bufs = comm, axis, views, bufs
        self.base = comm.take(3 * len(bufs))

    def start(self):
        for k, off in enumerate((1, 3, 2)):
            refs = self.views(self.comm.place(self.axis, off))
            for n, ref in enumerate(refs):
                self.comm.send(
                    ref, self.bufs[n].at[k], self.base + k * len(refs) + n, self.comm.peer(self.axis, off)
                )

    def wait(self):
        for k in range(3):
            for n, buf in enumerate(self.bufs):
                self.comm.recv(buf.at[k], self.base + k * len(self.bufs) + n)


def bucket_ids(offsets):
    distance = jnp.abs(offsets)
    bucket_sum = jnp.where(offsets > 0, 16, 0)
    for threshold in LIMITS:
        bucket_sum = bucket_sum + jnp.where(distance >= threshold, 1, 0)
    return bucket_sum


def rms_scale(values):
    return lax.rsqrt(jnp.mean(values * values, axis=-1, keepdims=True) + EPSILON)


def greet(comm):
    x, y, z, c = comm.x, comm.y, comm.z, comm.c
    zl, zh = z % 2, z // 2
    barrier = pltpu.get_barrier_semaphore()
    count = 0
    peers = []
    for dy in range(4):
        for dh in range(2):
            for dc in range(2):
                if dy or dh or dc:
                    peers.append(dev(x, (y + dy) % 4, ((zh + dh) % 2) * 2 + zl, (c + dc) % 2))
    for off in (1, 2, 3):
        peers.append(comm.peer("x", off))
    for off in (1, 3):
        peers.append(comm.peer("z", off))
    for peer in peers:
        pl.semaphore_signal(barrier, inc=1, device_id=peer, device_id_type=MESH)
        count += 1
    return barrier, count


def cast_up(v):
    return v.astype(F32)


def head_bias(tables, o):
    return tables[o : o + 1, 0:1], tables[o : o + 1, 1023:1024]


def mega(*refs):
    names = [n for n, _ in INPUTS] + [n for n, _ in OUTPUTS] + [n for n, _ in SCRATCH]
    r = dict(zip(names, refs))
    rows, seq = lax.axis_index("rows"), lax.axis_index("seq")
    x, y, zl, zh, c = rows % 4, seq // 4, rows // 4, (seq // 2) % 2, seq % 2
    z = zh * 2 + zl
    flat = rows * 16 + seq
    t = c * 4 + y
    comm = Comm(x, y, z, c, r["send_sem"], r["recv_sem"])
    local_sem = r["local_sem"]
    TK, CT, T5, tok, cot = r["TK"], r["CT"], r["T5"], r["tok"], r["cot"]
    loads = []
    for i, name in enumerate(("wq", "wk", "wv", "wo", "wg", "wu", "wd")):
        loads.append(pltpu.make_async_copy(r["h_" + name], r[name], local_sem.at[i]))
        loads[-1].start()
    keep_tokens = pltpu.make_async_copy(tok.at[zh], T5.at[y, zh, c], local_sem.at[7])
    keep_tk = pltpu.make_async_copy(tok, TK.at[:, c], local_sem.at[8])
    keep_ct = pltpu.make_async_copy(cot, CT.at[:, c], local_sem.at[9])
    keep_tokens.start()
    keep_tk.start()
    keep_ct.start()
    barrier, count = greet(comm)

    lanes = iota((1, 1024), 1)
    first_row = jnp.zeros((1, 1024), F32)
    second_row = jnp.zeros((1, 1024), F32)
    for i in range(6):
        first_row += jnp.where(lanes == 6 * flat + i, r["g1"][i], 0.0)
        second_row += jnp.where(lanes == 6 * flat + i, r["g2"][i], 0.0)
    for i in range(3):
        at = 768 + 3 * flat + i
        first_row += jnp.where(lanes == at, r["bt"][i], 0.0)
        second_row += jnp.where((lanes >= 768) & (lanes == at - 256), r["bt"][i], 0.0)
    first_row = cast_up(first_row.astype(BF))
    second_row = cast_up(second_row.astype(BF))
    wst, w0 = r["wst"], r["w0"]
    for load in loads:
        load.wait()
    for cc in range(2):
        for yy in range(4):
            d, h0 = cc * 4 + yy, first_head(cc * 4 + yy)
            for i, name in enumerate(("wq", "wk", "wv")):
                wst[d, 0:6, 128 * i : 128 * (i + 1)] = r[name][:, 64 * h0 : 64 * h0 + 128]
            for i, name in enumerate(("wg", "wu")):
                for k in range(2):
                    tile = 2 * (2 * yy + k) + cc
                    at = 512 + 256 * i + 128 * k
                    wst[d, 0:6, at : at + 128] = r[name][:, 128 * tile : 128 * tile + 128]
            if yy < 3:
                at = (cc * 3 + yy) * 128
                wst[d, 0:6, 384:512] = r["wo"][:, at : at + 128]
            else:
                wst[d, 0:6, 384:512] = jnp.zeros((6, 128), F32)
            wst[d, 6:7, :] = first_row
            wst[d, 7:8, :] = second_row
    r["wdst"][...] = r["wd"][...].astype(BF)

    pl.semaphore_wait(barrier, count)

    W1, WD, WQ, G5 = r["W1"], r["WD"], r["WQ"], r["G5"]
    slot = (y % 2) * 4 + zh * 2 + c
    base0 = comm.take(8)
    baser = comm.take(8)
    for cc in range(2):
        for yy in range(4):
            to = dev(x, yy, (y // 2) * 2 + zl, cc)
            own = (y == yy) & (c == cc) & (zh == y // 2)
            cp = comm.copy(wst.at[cc * 4 + yy], w0.at[slot], base0 + cc * 4 + yy, to, baser + slot)
            keep = pltpu.make_async_copy(wst.at[cc * 4 + yy], w0.at[slot], comm.rs.at[baser + slot])
            pl.when(own)(keep.start)
            pl.when(jnp.logical_not(own))(cp.start)
            comm.pending.append((cp, own))
    wd_to = (zh * 2 + c, y % 2, y // 2)
    own_wd = (wd_to[0] == y) & (wd_to[1] == zh) & (wd_to[2] == c)
    wdi = comm.take()
    wd_region = WD.at[zl, x, wd_to[1], wd_to[0]]
    comm.send_or_keep(
        r["wdst"], wd_region, wdi, dev(x, wd_to[0], wd_to[1] * 2 + zl, wd_to[2]), wdi, own_wd
    )

    other = comm.peer("z", 2)
    zi = comm.take()
    comm.send(tok.at[1 - zh], T5.at[y, zh, c], zi, other)
    own_tokens = Ring(
        comm,
        "y",
        lambda yy: [T5.at[yy, zh, c]],
        lambda yy, k: [T5.at[yy, zh, c, pl.ds(64 * k, 64)]],
    )
    own_tokens.start(source=[tok.at[zh]])
    pair = comm.take(2)

    for j in range(8):
        comm.recv(w0.at[j], baser + j)
    asm = r["asm"]
    gsum = jnp.zeros((2, 1024), F32)
    for j in range(8):
        asm[6 * j : 6 * j + 6, :] = w0[j, 0:6, :]
        gsum += w0[j, 6:8, :]
    WQ[zl, x, zh] = asm[:, 0:512].astype(BF)
    G5[zl, x, zh] = jnp.concatenate([gsum, jnp.zeros((6, 1024), F32)], axis=0)
    W1[zl, x, zh, y] = asm[:, 512:1024].astype(BF)
    qkv_a1 = Direct(comm, "x", lambda xx: [WQ.at[zl, xx, zh, :, pl.ds(0, 256)], G5.at[zl, xx, zh]])
    qkv_b1 = Direct(comm, "z", lambda zz: [WQ.at[zz % 2, x, zz // 2, :, pl.ds(256, 256)]])
    qkv_a1.start()
    qkv_b1.start()
    comm.recv(WD.at[zl, x, zh, y], wdi)
    ff_y = Direct(comm, "y", lambda yy: [W1.at[zl, x, zh, yy], WD.at[zl, x, zh, yy]])
    ff_y.start()

    comm.recv(T5.at[y, 1 - zh, c], zi)
    far_tokens = Ring(
        comm,
        "y",
        lambda yy: [T5.at[yy, 1 - zh, c]],
        lambda yy, k: [T5.at[yy, 1 - zh, c, pl.ds(64 * k, 64)]],
    )
    far_tokens.start()
    keep_tokens.wait()
    sib = comm.peer("c", 0)
    across = comm.take(4)

    def cross(k):
        yy = (y + (0, 1, 3, 2)[k]) % 4
        comm.send(T5.at[yy, :, c], T5.at[yy, :, c], across + k, sib)

    def crossed(k):
        yy = (y + (0, 1, 3, 2)[k]) % 4
        comm.recv(T5.at[yy, :, 1 - c], across + k)

    cross(0)
    qkv_a1.wait()
    qkv_b1.wait()
    qkv_a2 = Direct(
        comm,
        "z",
        lambda zz: [WQ.at[zz % 2, :, zz // 2, :, pl.ds(0, 256)], G5.at[zz % 2, :, zz // 2]],
    )
    qkv_b2 = Direct(comm, "x", lambda xx: [WQ.at[:, xx, :, :, pl.ds(256, 256)]])
    qkv_a2.start()
    qkv_b2.start()
    own_tokens.forward()
    ff_y.wait()
    low, high = pl.ds(0, 256), pl.ds(256, 256)
    low_d, high_d = pl.ds(0, 384), pl.ds(384, 384)
    ff_a1 = Direct(
        comm, "x", lambda xx: [W1.at[zl, xx, zh, :, :, low], WD.at[zl, xx, zh, :, :, low_d]]
    )
    ff_b1 = Direct(
        comm,
        "z",
        lambda zz: [
            W1.at[zz % 2, x, zz // 2, :, :, high],
            WD.at[zz % 2, x, zz // 2, :, :, high_d],
        ],
    )
    ff_a1.start()
    ff_b1.start()
    far_tokens.forward()
    cross(1)
    cross(2)
    keep_tk.wait()
    keep_ct.wait()
    comm.send(TK.at[:, c], TK.at[:, c], pair, sib)
    comm.send(CT.at[:, c], CT.at[:, c], pair + 1, sib)

    qkv_a2.wait()
    qkv_b2.wait()
    WOF = r["WOF"]
    base_w = comm.take(8)
    base_wr = comm.take(8)
    for cc in range(2):
        for yy in range(4):
            src = WQ.at[cc, :, :, :, pl.ds(384, 128)]
            dst = WOF.at[:, :, :, pl.ds(pl.multiple_of((c * 3 + y % 3) * 128, 128), 128)]
            cp = comm.copy(src, dst, base_w + cc * 4 + yy, dev(x, yy, z, cc), base_wr + c * 4 + y)
            keep = pltpu.make_async_copy(src, dst, comm.rs.at[base_wr + c * 4 + y])
            here = (yy == y) & (cc == c)
            pl.when(here & (y < 3))(keep.start)
            pl.when(jnp.logical_not(here) & (y < 3))(cp.start)
            comm.pending.append((cp, here | (y == 3)))
    total = jnp.zeros((8, 1024), F32)
    for a in range(2):
        for b in range(4):
            for e in range(2):
                total += G5[a, b, e]
    r["GS"][...] = total
    h0 = first_head(t)
    table_row = jnp.concatenate([total[0:1, 768:1024], total[1:2, 768:896]], axis=1)
    table_row = jnp.broadcast_to(table_row, (8, 384))
    table_row = pltpu.roll(table_row, 384 - 32 * h0, 1)[:, 0:128]
    lane = iota((8, 128), 1)
    sub = iota((8, 128), 0)
    table_two = jnp.where((lane // 32) == sub, table_row, 0.0).astype(BF)
    r["OH"][...] = jnp.where(
        bucket_ids(iota((128, 1024), 1) - 512) == iota((128, 1024), 0) % 32, 1.0, 0.0
    ).astype(BF)
    by_offset = dot(table_two, r["OH"][...])
    r["BO"][...] = by_offset
    for h in range(2):
        for k in range(4):
            rolled = pltpu.roll(
                jnp.broadcast_to(by_offset[h : h + 1, :], (64, 1024)), 640 + 64 * k, 1, stride=1, stride_axis=0
            )
            r["BT"][h, 64 * k : 64 * k + 64, :] = rolled[:, 0:512]

    ff_a1.wait()
    ff_b1.wait()
    ff_a2 = Ring(
        comm,
        "z",
        lambda zz: [
            W1.at[zz % 2, :, zz // 2, :, :, low],
            WD.at[zz % 2, :, zz // 2, :, :, low_d],
        ],
        lambda zz, k: [
            W1.at[zz % 2, pl.ds(2 * k, 2), zz // 2, :, :, low],
            WD.at[zz % 2, pl.ds(2 * k, 2), zz // 2, :, :, low_d],
        ],
    )
    ff_b2 = Ring(
        comm,
        "x",
        lambda xx: [W1.at[:, xx, :, :, :, high], WD.at[:, xx, :, :, :, high_d]],
        lambda xx, k: [W1.at[k, xx, :, :, :, high], WD.at[k, xx, :, :, :, high_d]],
    )
    ff_a2.start()
    ff_b2.start()

    QA, KT, KN, VN, VT = r["QA"], r["KT"], r["KN"], r["VN"], r["VT"]
    row_len = r["lens"][zh]

    def project(i, carry):
        raw = cast_up(T5[i // 2, i % 2].reshape(256, D))
        normed = (raw * rms_scale(raw) * r["GS"][0:1, 0:768]).astype(BF)
        res = dot(normed, WQ[:, :, :, :, 0:384].reshape(D, 384))
        q, k_, v = res[:, 0:128], res[:, 128:256], res[:, 256:384]
        at = pl.ds(pl.multiple_of(i * 256, 256), 256)
        KN[at, :] = k_.astype(BF)
        VN[at, :] = jnp.concatenate([v, jnp.ones((256, 128), F32)], axis=1).astype(BF)
        VT[:, at] = v.T.astype(BF)
        kt = k_.T
        lane = iota((256, 128), 1)
        sub = iota((128, 256), 0)
        key_at = i * 256 + iota((128, 256), 1)
        for h in range(2):
            base = 64 * (1 - h)
            hot = jnp.where((lane == base + i) | (lane == base + 8), 1.0, 0.0)
            QA[h, at, :] = jnp.where(lane // 64 == h, q, hot).astype(BF)
            left, right = head_bias(r["BO"][...], h)
            start = 256 * (sub - base)
            extra = jnp.where(key_at < start - 128, left, 0.0) + jnp.where(
                key_at >= start + 384, right, 0.0
            )
            masked = jnp.where(key_at >= row_len, NEGATIVE, 0.0)
            extra = jnp.where(sub - base < 8, extra, jnp.where(sub - base == 8, masked, 0.0))
            KT[h, :, at] = jnp.where(sub // 64 == h, kt, extra).astype(BF)
        return carry

    for k in range(4):
        if k == 3:
            own_tokens.wait()
            far_tokens.wait()
            cross(3)
        crossed(k)
        first = 2 * ((y + (0, 1, 3, 2)[k]) % 4)
        lax.fori_loop(first, first + 2, project, 0)
    r["ON"][...] = jnp.zeros((SEQ, 128), BF)
    r["LI"][...] = jnp.zeros((1024, 128), F32)
    r["PB"][:, :, 0:128] = jnp.zeros((3, 1024, 128), BF)
    r["PB"][:, :, 2176:2304] = jnp.zeros((3, 1024, 128), BF)

    SC, PB, BT, ON, LI = r["SC"], r["PB"], r["BT"], r["ON"], r["LI"]

    def unit_of(step):
        ui = step // 4
        u = jnp.where(ui == 0, 1, jnp.where(ui == 1, 0, 2))
        number = 3 * t + u
        head = number // 2 - h0
        start = (number % 2) * 1024 + (step % 4) * 256
        return head, pl.multiple_of(start, 256)

    S2 = r["S2"]

    def score_part(step, buf, j, top):
        head, q0 = unit_of(step)
        s = dot(QA[head, pl.ds(q0, BQ), :], KT[head, :, 256 * j : 256 * j + 256])
        buf[:, 128 + 256 * j : 384 + 256 * j] = s
        most = jnp.maximum(s[:, 0:128], s[:, 128:256])
        return most if top is None else jnp.maximum(top, most)

    def score_end(step, buf, top):
        head, q0 = unit_of(step)
        buf[:, pl.ds(q0, 512)] = buf[:, pl.ds(q0, 512)] + BT[head]
        return jnp.max(top, axis=1, keepdims=True)

    def block_of(step):
        return pl.ds(pl.multiple_of((step % 4) * 256, 256), BQ)

    def prob_part(step, buf, j, top):
        for k in (2 * j + 1, 2 * j + 2):
            p = jnp.exp(buf[:, 128 * k : 128 * k + 128] - top)
            PB[step // 4, block_of(step), 128 * k : 128 * k + 128] = p.astype(BF)

    def mix(step):
        head, q0 = unit_of(step)
        mixed = dot(PB[step // 4, block_of(step), 128:2176], VN[...])
        inv = 1.0 / mixed[:, 128:129]
        lane = iota((BQ, 128), 1)
        LI[block_of(step), :] = jnp.where(lane == step // 4, inv, LI[block_of(step), :])
        mixed = mixed[:, 0:128] * inv
        ON[pl.ds(q0, BQ), :] = jnp.where(lane // 64 == head, mixed, cast_up(ON[pl.ds(q0, BQ), :])).astype(BF)

    def first_scores(step):
        top = None
        for j in range(8):
            top = score_part(step, SC, j, top)
        return score_end(step, SC, top)

    def attend(pair, top_a):
        one, two = 2 * pair, 2 * pair + 1
        top_b = None
        for j in range(8):
            top_b = score_part(two, S2, j, top_b)
            prob_part(one, SC, j, top_a)
        top_b = score_end(two, S2, top_b)
        mix(one)
        then = jnp.minimum(two + 1, STEPS - 1)
        top_a = None
        for j in range(8):
            prob_part(two, S2, j, top_b)
            top_a = score_part(then, SC, j, top_a)
        top_a = score_end(then, SC, top_a)
        mix(two)
        return top_a

    A = r["A"]
    base_o = comm.take(8)
    base_or = comm.take(8)

    def give(half, n):
        for i in range(4):
            yy, hh = 2 * half + i // 2, i % 2
            src = ON.at[pl.ds(pl.multiple_of(256 * (yy * 2 + hh), 256), 256)]
            dst = A.at[zh, :, pl.ds(pl.multiple_of(128 * y, 128), 128)]
            own = (yy == y) & (hh == zh)
            cp = comm.copy(src, dst, base_o + 4 * n + i, dev(x, yy, hh * 2 + zl, c), base_or + y * 2 + zh)
            keep = pltpu.make_async_copy(src, dst, comm.rs.at[base_or + y * 2 + zh])
            pl.when(own)(keep.start)
            pl.when(jnp.logical_not(own))(cp.start)
            comm.pending.append((cp, own))

    single = (3 * t + 1) % 2
    top_now = lax.fori_loop(0, 2, attend, first_scores(0))
    give(single, 0)
    top_now = lax.fori_loop(2, 3, attend, top_now)
    ff_a2.forward()
    ff_b2.forward()
    lax.fori_loop(3, STEPS // 2, attend, top_now)
    give(1 - single, 1)
    for yy in range(4):
        for hh in range(2):
            comm.recv(A.at[hh, :, pl.ds(128 * yy, 128)], base_or + yy * 2 + hh)
    comm.recv(TK.at[:, 1 - c], pair)
    comm.recv(CT.at[:, 1 - c], pair + 1)

    lane = iota((256, 128), 1)
    for hh in range(2):
        p0, p1, p2, p3 = [cast_up(A[hh, :, 128 * k : 128 * k + 128]) for k in range(4)]
        p1, p2 = pltpu.roll(p1, 64, 1), pltpu.roll(p2, 64, 1)
        A[hh, :, 0:128] = (p0 + jnp.where(lane >= 64, p1, 0.0)).astype(BF)
        A[hh, :, 128:256] = jnp.where(lane < 64, p1, p2).astype(BF)
        A[hh, :, 256:384] = (p3 + jnp.where(lane < 64, p2, 0.0)).astype(BF)
    for cc in range(2):
        for yy in range(3):
            comm.recv(WOF.at[:, :, :, pl.ds(128 * (cc * 3 + yy), 128)], base_wr + cc * 4 + yy)

    POS, POR, N2, N2T = r["POS"], r["POR"], r["N2"], r["N2T"]
    base_p = comm.take(2)
    for hh in range(2):
        term = dot(A[hh, :, 0:384], WOF[...].reshape(384, D))
        POS[hh] = term.astype(BF).reshape(2, 128, D)
        comm.send(POS.at[hh], POR.at[hh], base_p + hh, sib)
    second_gain = r["GS"][1:2, 0:768]
    for hh in range(2):
        comm.recv(POR.at[hh], base_p + hh)
        for k in range(2):
            middle = cast_up(TK[hh, k]) + (cast_up(POS[hh, k]) + cast_up(POR[hh, k]))
            S2[128 * hh : 128 * hh + 128, 768 * k : 768 * k + 768] = middle
            normed = middle * rms_scale(middle) * second_gain
            N2[128 * k : 128 * k + 128, 768 * hh : 768 * hh + 768] = normed.astype(BF)
            at = 256 * hh + 128 * k
            N2T[:, at : at + 128] = normed.T.astype(BF)

    HX, HIDT, GU = r["HX"], r["HIDT"], r["GU"]

    def gated(k, carry):
        gate_w = W1[:, :, :, k, :, 0:256].reshape(D, 256)
        up_w = W1[:, :, :, k, :, 256:512].reshape(D, 256)
        down_w = WD[k // 2, pl.ds((2 * k) % 4, 2)].reshape(256, D)
        for hh in range(2):
            gate = dot(N2[:, 768 * hh : 768 * hh + 768], gate_w)
            up = dot(N2[:, 768 * hh : 768 * hh + 768], up_w)
            back = dot_nt(CT[hh].reshape(256, D), down_w)
            square = gate * gate
            th = jnp.tanh(0.7978845608028654 * (gate + 0.044715 * (square * gate)))
            half = 0.5 * (1.0 + th)
            gelu = gate * half
            slope = half + (0.5 * gate) * (1.0 - th * th) * (
                0.7978845608028654 * (1.0 + 3 * 0.044715 * square)
            )
            hidden = gelu * up
            cols = pl.ds(pl.multiple_of(256 * k, 256), 256)
            HX[:, pl.ds(pl.multiple_of(1024 * hh + 256 * k, 256), 256)] = hidden.astype(BF)
            HIDT[cols, 256 * hh : 256 * hh + 256] = hidden.T.astype(BF)
            both = pl.multiple_of(512 * k, 512)
            GU[hh, :, :, pl.ds(both, 256)] = (back * up * slope).astype(BF).reshape(2, 128, 256)
            GU[hh, :, :, pl.ds(both + 256, 256)] = (back * gelu).astype(BF).reshape(2, 128, 256)
        return carry

    ff_a2.wait()
    ff_b2.wait()
    lax.fori_loop(0, 4, gated, 0)
    PNR, SC = r["PNR"], r["SC"]
    base_n = comm.take(2)
    comm.drain()
    for hh in range(2):
        term = dot_nt(GU[hh, :, :, 0:512].reshape(256, 512), W1[:, :, :, 0].reshape(D, 512))
        for k in range(1, 4):
            term += dot_nt(
                GU[hh, :, :, 512 * k : 512 * k + 512].reshape(256, 512), W1[:, :, :, k].reshape(D, 512)
            )
        POS[hh] = term.astype(BF).reshape(2, 128, D)
        comm.send(POS.at[hh], PNR.at[hh], base_n + hh, sib)
    PYS, PYR = r["PYS"], r["PYR"]
    yi = comm.take()
    down_all = WD[...].reshape(1024, D)
    for hh in range(2):
        PYS[hh] = dot(HX[pl.ds(pl.multiple_of(128 * (1 - c), 128), 128), 1024 * hh : 1024 * hh + 1024], down_all).astype(BF)
    comm.send(PYS, PYR, yi, sib)
    for hh in range(2):
        SC[128 * hh : 128 * hh + 128, 0:768] = dot(HX[pl.ds(pl.multiple_of(128 * c, 128), 128), 1024 * hh : 1024 * hh + 1024], down_all)

    low_r, high_r = pl.ds(0, 256), pl.ds(256, 512)
    def down_term(k, carry):
        res = dot(HIDT[pl.ds(pl.multiple_of(256 * k, 256), 256), :], CT[...].reshape(512, D))
        WD[k // 2, pl.ds((2 * k) % 4, 2)] = res.astype(BF).reshape(2, 2, 4, 16, D)
        return carry

    lax.fori_loop(0, 4, down_term, 0)
    wd_ra = Scatter(
        comm, "z", lambda zz: [WD.at[zz % 2, :, zz // 2, :, :, low_r]], [r["RA2"]]
    )
    wd_rb = Scatter(comm, "x", lambda xx: [WD.at[:, xx, :, :, :, high_r]], [r["RB2"]])
    wd_rb.start()

    ML, DOS, DO, VEC = r["ML"], r["DOS"], r["DO"], r["VEC"]
    VEC[...] = jnp.zeros((8, 1024), F32)
    base_d = comm.take(8)
    base_dr = comm.take(8)
    m = y * 2 + zh
    for hh in range(2):
        comm.recv(PNR.at[hh], base_n + hh)
        for k in range(2):
            grad = cast_up(POS[hh, k]) + cast_up(PNR[hh, k])
            middle = S2[128 * hh : 128 * hh + 128, 768 * k : 768 * k + 768]
            scale = rms_scale(middle)
            gained = grad * second_gain
            mean = jnp.mean(middle * gained, axis=-1, keepdims=True)
            full = cast_up(CT[hh, k]) + scale * gained - middle * (scale * scale * scale * mean)
            ML[hh, k] = full.astype(BF)

            @pl.when(c == k)
            def _():
                r["din"][hh] = full
                VEC[1:2, 0:768] += jnp.sum(grad * middle * scale, axis=0, keepdims=True)

        given = dot_nt(ML[hh].reshape(256, D), WOF[...].reshape(384, D))
        g0, g1, g2 = given[:, 0:128], given[:, 128:256], given[:, 256:384]
        r0, r1, r2 = pltpu.roll(g0, 64, 1), pltpu.roll(g1, 64, 1), pltpu.roll(g2, 64, 1)
        DOS[0, hh] = g0.astype(BF)
        DOS[1, hh] = jnp.where(lane < 64, r0, r1).astype(BF)
        DOS[2, hh] = jnp.where(lane < 64, r1, r2).astype(BF)
        DOS[3, hh] = g2.astype(BF)
        for yy in range(4):
            dst = DO.at[pl.ds(pl.multiple_of(256 * m, 256), 256)]
            own = (yy == y) & (hh == zh)
            cp = comm.copy(DOS.at[yy, hh], dst, base_d + 4 * hh + yy, dev(x, yy, hh * 2 + zl, c), base_dr + m)
            keep = pltpu.make_async_copy(DOS.at[yy, hh], dst, comm.rs.at[base_dr + m])
            pl.when(own)(keep.start)
            pl.when(jnp.logical_not(own))(cp.start)
            comm.pending.append((cp, own))


    def gated_term(k, carry):
        res = dot(N2T[...], GU[:, :, :, pl.ds(pl.multiple_of(512 * k, 512), 512)].reshape(512, 512))
        W1[:, :, :, k] = res.astype(BF).reshape(2, 4, 2, 48, 512)
        return carry

    lax.fori_loop(0, 4, gated_term, 0)
    pl.semaphore_signal(r["free_sem"], inc=1, device_id=sib, device_id_type=MESH)
    ff_ra = Scatter(comm, "z", lambda zz: [W1.at[zz % 2, :, zz // 2, :, :, low]], [r["RA1"]])
    ff_rb = Scatter(comm, "x", lambda xx: [W1.at[:, xx, :, :, :, high]], [r["RB1"]])
    ff_rb.start()
    attended_t = jnp.concatenate(
        [cast_up(A[hh, :, 0:384]).T.astype(BF) for hh in range(2)], axis=1
    )
    WOF[...] = dot(attended_t, ML[...].reshape(512, D)).astype(BF).reshape(4, 2, 48, D)
    base_g = comm.take(6)
    base_gr = comm.take(8)
    WOR = r["WOR"]
    for cc in range(2):
        for yy in range(3):
            src = WOF.at[:, :, :, pl.ds(128 * (cc * 3 + yy), 128)]
            cp = comm.copy(src, WOR.at[y, c], base_g + cc * 3 + yy, dev(x, yy, z, cc), base_gr + c * 4 + y)
            keep = pltpu.make_async_copy(src, WOR.at[y, c], comm.rs.at[base_gr + c * 4 + y])
            here = (yy == y) & (cc == c)
            pl.when(here)(keep.start)
            pl.when(jnp.logical_not(here))(cp.start)
            comm.pending.append((cp, here))
    comm.recv(PYR, yi)
    for hh in range(2):
        middle = S2[128 * hh : 128 * hh + 128, pl.ds(pl.multiple_of(768 * c, 128), 768)]
        r["out"][hh] = (middle + SC[128 * hh : 128 * hh + 128, 0:768] + cast_up(PYR[hh])).astype(BF)
    stores = [pltpu.make_async_copy(r["out"], r["h_out"], local_sem.at[10])]
    stores[0].start()

    SC[:, 0:2048] = jnp.zeros((256, SEQ), F32)
    S2[0:128, 0:2048] = jnp.zeros((128, SEQ), F32)
    N2[:, 0:1024] = jnp.zeros((BQ, 1024), BF)
    BT[...] = jnp.zeros((2, 256, 512), F32)
    for yy in range(4):
        for hh in range(2):
            comm.recv(DO.at[pl.ds(256 * (yy * 2 + hh), 256)], base_dr + yy * 2 + hh)
    wd_ra.start()
    ff_ra.start()

    GL, DL = r["GL"], r["DL"]

    def retreat(ui, carry):
        head, q0 = unit_of(4 * ui)
        rows = pl.ds(pl.multiple_of(q0, 1024), 1024)
        lane = iota((1024, 128), 1)
        inv = jnp.sum(jnp.where(lane == ui, LI[...], 0.0), axis=1, keepdims=True)
        given = jnp.where(lane // 64 == head, cast_up(DO[rows, :]) * inv, 0.0)
        GL[...] = given.astype(BF)
        delta = jnp.sum(cast_up(GL[...]) * cast_up(ON[rows, :]), axis=1, keepdims=True)
        DL[...] = jnp.broadcast_to(delta, (1024, 128))
        given_t = given.T.astype(BF)
        for j in range(8):
            S2[0:128, 256 * j : 256 * j + 256] += dot(given_t, PB[ui, :, 128 + 256 * j : 384 + 256 * j])

        def inner(b, more):
            block = pl.ds(pl.multiple_of(256 * b, 256), 256)
            low_rows = GL[block, :]
            shift = DL[block, 0:1]
            for j in range(8):
                cols = slice(128 + 256 * j, 384 + 256 * j)
                grad = dot(low_rows, VT[:, 256 * j : 256 * j + 256])
                PB[ui, block, cols] = (cast_up(PB[ui, block, cols]) * (grad - shift)).astype(BF)
            moved = dot(PB[ui, block, 128:2176], KN[...])
            at = q0 + 256 * b
            lane = iota((BQ, 128), 1)
            spot = pl.ds(pl.multiple_of(at // 2, 128), 128)
            N2[:, spot] = jnp.where(lane // 64 == head, moved, cast_up(N2[:, spot])).astype(BF)
            BT[head] += cast_up(PB[ui, block, pl.ds(pl.multiple_of(at, 256), 512)])
            return more

        lax.fori_loop(0, 4, inner, 0)
        query_t = cast_up(QA[head, rows, :]).T.astype(BF)
        key_rows = pl.ds(pl.multiple_of(128 * head, 128), 128)
        for j in range(8):
            SC[key_rows, 256 * j : 256 * j + 256] += dot(query_t, PB[ui, :, 128 + 256 * j : 384 + 256 * j])
        return carry

    def add_low(refs, bufs):
        for ref, buf in zip(refs, bufs):
            total = cast_up(ref[...])
            for k in range(3):
                total += cast_up(buf[k])
            ref[...] = total.astype(BF)

    lax.fori_loop(0, 3, retreat, 0)

    YR, DWQ = r["YR"], r["DWQ"]
    first_gain = r["GS"][0:1, 0:768]
    base_s = comm.take(4)
    S2[128:256, :] = jnp.zeros((128, 2304), F32)

    def sib_at(yy):
        return GU.at[yy // 2, :, :, pl.ds(pl.multiple_of((yy % 2) * 1024, 128), 768)]

    def place_of(k):
        return (y + jnp.where(k == 0, 2, jnp.where(k == 1, 1, jnp.where(k == 2, 3, 0)))) % 4

    def spread_back(k, carry):
        yy = place_of(k)

        def half(hh, inner):
            at = pl.ds(pl.multiple_of(512 * yy + 256 * hh, 256), 256)
            raw = cast_up(T5[yy, hh].reshape(256, D))
            scale = rms_scale(raw)
            normed = (raw * scale * first_gain).astype(BF)
            dq = N2[:, pl.ds(pl.multiple_of(256 * yy + 128 * hh, 128), 128)]
            sub = iota((128, 256), 0)
            dkt = jnp.where(sub < 64, SC[0:128, at], SC[128:256, at])
            dvt = S2[0:128, at]
            dk, dv = dkt.T.astype(BF), dvt.T.astype(BF)
            dqt = cast_up(dq).T.astype(BF)
            grad = dot_nt(jnp.concatenate([dq, dk, dv], axis=1), WQ[:, :, :, :, 0:384].reshape(D, 384))
            VEC[0:1, 0:768] += jnp.sum(grad * raw * scale, axis=0, keepdims=True)
            S2[128:256, 0:768] += dot(dqt, normed)
            S2[128:256, 768:1536] += dot(dkt.astype(BF), normed)
            S2[128:256, 1536:2304] += dot(dvt.astype(BF), normed)
            T5[yy, hh] = grad.astype(BF).reshape(2, 128, D)
            return inner

        lax.fori_loop(0, 2, half, 0)
        comm.copy(T5.at[yy, :, 1 - c], sib_at(yy), base_s + k, sib).start()
        return carry

    base_y = comm.take(3)

    def pass_on(k):
        yy = (y + (2, 1, 3, 0)[k]) % 4
        comm.recv(sib_at(yy), base_s + k)
        for hh in range(2):
            T5[yy, hh, c] = (cast_up(T5[yy, hh, c]) + cast_up(sib_at(yy)[hh])).astype(BF)
        if k < 3:
            comm.send(T5.at[yy, :, c], YR.at[k], base_y + k, comm.peer("y", (2, 1, 3)[k]))

    pl.semaphore_wait(r["free_sem"], 1)
    for k in range(4):
        spread_back(k, 0)
        if k:
            pass_on(k - 1)
    for i in range(3):
        DWQ[:, :, :, :, 128 * i : 128 * i + 128] = S2[128:256, 768 * i : 768 * i + 768].T.astype(BF).reshape(2, 4, 2, 48, 128)

    q_ra = Scatter(
        comm,
        "z",
        lambda zz: [DWQ.at[zz % 2, :, zz // 2, :, low]],
        [r["QA1"]],
    )
    q_ra.start()
    @pl.when(y == 3)
    def _():
        DWQ[:, :, :, :, 384:512] = jnp.zeros((2, 4, 2, 48, 128), BF)

    @pl.when(y < 3)
    def _():
        for k in range(4):
            for cc in range(2):
                comm.recv(WOR.at[k, cc], base_gr + cc * 4 + k)
        for cc in range(2):
            total = cast_up(WOR[0, cc])
            for k in range(1, 4):
                total += cast_up(WOR[k, cc])
            DWQ[cc, :, :, :, 384:512] = total.astype(BF)

    q_rb = Scatter(
        comm,
        "x",
        lambda xx: [DWQ.at[:, xx, :, :, high]],
        [r["QB1"]],
    )
    lane = iota((8, 128), 1)
    sub = iota((8, 128), 0)
    diagonals = []
    flip = jnp.where(iota((256, 256), 0) + iota((256, 256), 1) == 255, 1.0, 0.0).astype(BF)
    table_grad = jnp.zeros((1, 128), F32)
    one = iota((1, 128), 1)
    for h in range(2):
        near = jnp.zeros((1, 1024), F32)
        whole = BT[h]
        upper = whole.astype(BF)
        lower = (whole - cast_up(upper)).astype(BF)
        flipped = dot(flip, upper) + dot(flip, lower)
        for k in range(4):
            part = jnp.concatenate([flipped[64 * k : 64 * k + 64], jnp.zeros((64, 512), F32)], axis=1)
            part = pltpu.roll(part, 129 + 64 * k, 1, stride=1, stride_axis=0)
            near += jnp.sum(part, axis=0, keepdims=True)
        diagonals.append(near)
        base = 64 * (1 - h)
        rows_far = SC[128 * h + base : 128 * h + base + 8, 0:2048]
        key_at = iota((8, SEQ), 1)
        start = 256 * iota((8, SEQ), 0)
        left = jnp.sum(jnp.where(key_at < start - 128, rows_far, 0.0), axis=(0, 1), keepdims=True)
        right = jnp.sum(jnp.where(key_at >= start + 384, rows_far, 0.0), axis=(0, 1), keepdims=True)
        table_grad += jnp.where(one == 32 * h + 15, left, 0.0) + jnp.where(one == 32 * h + 31, right, 0.0)
    near = jnp.concatenate(diagonals + [jnp.zeros((6, 1024), F32)], axis=0)
    upper = near.astype(BF)
    lower = (near - cast_up(upper)).astype(BF)
    sums = dot_nt(upper, r["OH"][...]) + dot_nt(lower, r["OH"][...])
    table_grad += jnp.sum(jnp.where(lane // 32 == sub, sums, 0.0), axis=0, keepdims=True)
    spread = jnp.concatenate([table_grad, jnp.zeros((1, 256), F32)], axis=1)
    spread = pltpu.roll(jnp.broadcast_to(spread, (8, 384)), 32 * h0, 1)
    VEC[0:1, 768:1024] = spread[0:1, 0:256]
    VEC[1:2, 768:896] = spread[0:1, 256:384]

    v_z = Scatter(comm, "z", lambda zz: [VEC], [r["V1"]])
    q_rb.start()
    v_z.start()
    pass_on(3)
    wd_ra.wait()
    wd_rb.wait()
    ff_ra.wait()
    ff_rb.wait()

    def add_a(i, carry):
        add_low(
            [W1.at[zl, i, zh, :, :, low], WD.at[zl, i, zh, :, :, low_r]],
            [r["RA1"].at[:, i], r["RA2"].at[:, i]],
        )
        add_low(
            [W1.at[i // 2, x, i % 2, :, :, high], WD.at[i // 2, x, i % 2, :, :, high_r]],
            [r["RB1"].at[:, i // 2, i % 2], r["RB2"].at[:, i // 2, i % 2]],
        )
        return carry

    lax.fori_loop(0, 4, add_a, 0)
    ff_ra2 = Scatter(
        comm,
        "x",
        lambda xx: [W1.at[zl, xx, zh, :, :, low], WD.at[zl, xx, zh, :, :, low_r]],
        [r["SA1"], r["SA2"]],
    )
    ff_rb2 = Scatter(
        comm,
        "z",
        lambda zz: [
            W1.at[zz % 2, x, zz // 2, :, :, high],
            WD.at[zz % 2, x, zz // 2, :, :, high_r],
        ],
        [r["SB1"], r["SB2"]],
    )
    ff_ra2.start()
    ff_rb2.start()
    q_ra.wait()
    q_rb.wait()
    v_z.wait()
    for i in range(4):
        add_low([DWQ.at[zl, i, zh, :, low]], [r["QA1"].at[:, i]])
        add_low([DWQ.at[i // 2, x, i % 2, :, high]], [r["QB1"].at[:, i // 2, i % 2]])
    VE2 = r["VE2"]
    VE2[...] = VEC[...] + r["V1"][0] + r["V1"][1] + r["V1"][2]
    q_ra2 = Scatter(comm, "x", lambda xx: [DWQ.at[zl, xx, zh, :, low]], [r["QA2"]])
    q_rb2 = Scatter(comm, "z", lambda zz: [DWQ.at[zz % 2, x, zz // 2, :, high]], [r["QB2"]])
    v_x = Scatter(comm, "x", lambda xx: [VE2], [r["V2"]])
    q_ra2.start()
    q_rb2.start()
    v_x.start()
    ff_ra2.wait()
    ff_rb2.wait()
    add_low([W1.at[zl, x, zh, :, :, low], WD.at[zl, x, zh, :, :, low_r]], [r["SA1"], r["SA2"]])
    add_low([W1.at[zl, x, zh, :, :, high], WD.at[zl, x, zh, :, :, high_r]], [r["SB1"], r["SB2"]])
    ff_ry = Scatter(
        comm, "y", lambda yy: [W1.at[zl, x, zh, yy], WD.at[zl, x, zh, yy]], [r["SY1"], r["SY2"]]
    )
    ff_ry.start()

    for k in range(3):
        comm.recv(YR.at[k], base_y + k)
    zri = comm.take()
    ZS, ZR = r["ZS"], r["ZR"]

    def summed(hh):
        total = cast_up(T5[y, hh, c])
        for k in range(3):
            total += cast_up(YR[k, hh])
        return total

    ZS[...] = summed(1 - zh).astype(BF)
    comm.send(ZS, ZR, zri, other)

    def finish(hh, grad):
        raw = cast_up(TK[hh, c])
        scale = rms_scale(raw)
        gained = grad * first_gain
        mean = jnp.mean(raw * gained, axis=-1, keepdims=True)
        r["din"][hh] = r["din"][hh] + scale * gained - raw * (scale * scale * scale * mean)

    finish(zh, summed(zh))

    ff_ry.wait()
    total = cast_up(W1[zl, x, zh, y])
    for k in range(3):
        total += cast_up(r["SY1"][k])
    asm[:, 512:1024] = total
    q_ra2.wait()
    q_rb2.wait()
    v_x.wait()
    total = cast_up(WD[zl, x, zh, y])
    for k in range(3):
        total += cast_up(r["SY2"][k])
    r["WDG"][...] = total
    home = (2 * c + zh, y // 2, y % 2)
    own_home = (home[0] == y) & (home[1] == zh) & (home[2] == c)
    dwi = comm.take()
    comm.send_or_keep(
        r["WDG"], r["dwd_in"], dwi, dev(x, home[0], home[1] * 2 + zl, home[2]), dwi, own_home
    )
    for cols, buf in ((low, r["QA2"]), (high, r["QB2"])):
        total = cast_up(DWQ[zl, x, zh, :, cols])
        for k in range(3):
            total += cast_up(buf[k])
        asm[:, cols] = total
    sums = VE2[...] + r["V2"][0] + r["V2"][1] + r["V2"][2]
    W2R = r["W2R"]
    base_h = comm.take(8)
    base_hr = comm.take(8)
    mine = c * 4 + y
    for j in range(8):
        wst[j, 0:6, :] = asm[6 * j : 6 * j + 6, :]
        wst[j, 6:8, :] = sums[0:2]
        ys, hs, cs = 2 * zh + j // 4, (j // 2) % 2, j % 2
        own = (ys == y) & (hs == zh) & (cs == c)
        cp = comm.copy(wst.at[j], W2R.at[mine], base_h + j, dev(x, ys, hs * 2 + zl, cs), base_hr + mine)
        keep = pltpu.make_async_copy(wst.at[j], W2R.at[mine], comm.rs.at[base_hr + mine])
        pl.when(own)(keep.start)
        pl.when(jnp.logical_not(own))(cp.start)
        comm.pending.append((cp, own))
    comm.recv(ZR, zri)
    finish(1 - zh, cast_up(ZR[...]))
    for d in range(8):
        comm.recv(W2R.at[d], base_hr + d)
    for name in ("dwq", "dwk", "dwv"):
        r[name][...] = jnp.zeros((6, D), F32)
    rows_sum = jnp.zeros((2, 1024), F32)
    for cc in range(2):
        for yy in range(4):
            d, first = cc * 4 + yy, 64 * first_head(cc * 4 + yy)
            for i, name in enumerate(("dwq", "dwk", "dwv")):
                r[name][:, first : first + 128] += W2R[d, 0:6, 128 * i : 128 * i + 128]
            for i, name in enumerate(("dwg", "dwu")):
                for k in range(2):
                    tile = 2 * (2 * yy + k) + cc
                    at = 512 + 256 * i + 128 * k
                    r[name][:, 128 * tile : 128 * tile + 128] = W2R[d, 0:6, at : at + 128]
            if yy < 3:
                at = (cc * 3 + yy) * 128
                r["dwo"][:, at : at + 128] = W2R[d, 0:6, 384:512]
            rows_sum += W2R[d, 6:8, :]
    table = jnp.concatenate([rows_sum[0:1, 768:1024], rows_sum[1:2, 768:1024], rows_sum[0:1, 0:512]], axis=1)
    gains = jnp.broadcast_to(jnp.concatenate([rows_sum, jnp.zeros((6, 1024), F32)], axis=0), (8, 1024))
    gains = pltpu.roll(gains, 1024 - 6 * flat, 1)[0:2, 0:128]
    table = pltpu.roll(jnp.broadcast_to(table, (8, 1024)), 1024 - 3 * flat, 1)[0:1, 0:128]
    r["dvec"][...] = jnp.concatenate([gains, table, jnp.zeros((5, 128), F32)], axis=0)
    comm.recv(r["dwd_in"], dwi)
    names = ("din", "dwq", "dwk", "dwv", "dwo", "dwg", "dwu", "dwd", "dvec")
    for i, name in enumerate(names):
        src = r["dwd_in"] if name == "dwd" else r[name]
        stores.append(pltpu.make_async_copy(src, r["h_" + name], local_sem.at[11 + i]))
        stores[-1].start()
    for k in range(4):
        yy = (y + (2, 1, 3, 0)[k]) % 4
        comm.copy(T5.at[yy, :, 1 - c], sib_at(yy), base_s + k, sib).wait_send()
    comm.drain()
    for store in stores:
        store.wait()


INPUTS = [
    ("lens", "s"), ("g1", "s"), ("g2", "s"), ("bt", "s"),
    ("tok", "a"), ("cot", "a"), ("h_wq", "a"), ("h_wk", "a"), ("h_wv", "a"), ("h_wo", "a"),
    ("h_wg", "a"), ("h_wu", "a"), ("h_wd", "a"),
]
SCRATCH = [
    ("W1", ((2, 4, 2, 4, 48, 512), BF)),
    ("WD", ((2, 4, 2, 4, 16, 768), BF)),
    ("WQ", ((2, 4, 2, 48, 512), BF)),
    ("G5", ((2, 4, 2, 8, 1024), F32)),
    ("T5", ((4, 2, 2, 128, 768), BF)),
    ("TK", ((2, 2, 128, 768), BF)),
    ("CT", ((2, 2, 128, 768), BF)),
    ("wst", ((8, 8, 1024), F32)),
    ("w0", ((8, 8, 1024), F32)),
    ("asm", ((48, 1024), F32)),
    ("wdst", ((16, 768), BF)),
    ("GS", ((8, 1024), F32)),
    ("OH", ((128, 1024), BF)),
    ("BO", ((8, 1024), F32)),
    ("BT", ((2, 256, 512), F32)),
    ("QA", ((2, 2048, 128), BF)),
    ("KT", ((2, 128, 2048), BF)),
    ("KN", ((2048, 128), BF)),
    ("VN", ((2048, 256), BF)),
    ("VT", ((128, 2048), BF)),
    ("SC", ((256, 2304), F32)),
    ("S2", ((256, 2304), F32)),
    ("PB", ((3, 1024, 2304), BF)),
    ("ON", ((2048, 128), BF)),
    ("LI", ((1024, 128), F32)),
    ("GL", ((1024, 128), BF)),
    ("DL", ((1024, 128), F32)),
    ("A", ((2, 256, 512), BF)),
    ("WOF", ((4, 2, 48, 768), BF)),
    ("POS", ((2, 2, 128, 768), BF)),
    ("POR", ((2, 2, 128, 768), BF)),
    ("N2", ((256, 1536), BF)),
    ("N2T", ((768, 512), BF)),
    ("HIDT", ((1024, 512), BF)),
    ("GU", ((2, 2, 128, 2048), BF)),
    ("PNR", ((2, 2, 128, 768), BF)),
    ("PYS", ((2, 128, 768), BF)),
    ("PYR", ((2, 128, 768), BF)),
    ("ML", ((2, 2, 128, 768), BF)),
    ("DOS", ((4, 2, 256, 128), BF)),
    ("DO", ((2048, 128), BF)),
    ("RA1", ((3, 4, 4, 48, 256), BF)),
    ("RA2", ((3, 4, 4, 16, 256), BF)),
    ("RB1", ((3, 2, 2, 4, 48, 256), BF)),
    ("RB2", ((3, 2, 2, 4, 16, 512), BF)),
    ("SA1", ((3, 4, 48, 256), BF)),
    ("SA2", ((3, 4, 16, 256), BF)),
    ("SB1", ((3, 4, 48, 256), BF)),
    ("SB2", ((3, 4, 16, 512), BF)),
    ("SY1", ((3, 48, 512), BF)),
    ("SY2", ((3, 16, 768), BF)),
    ("WOR", ((4, 2, 4, 2, 48, 128), BF)),
    ("HX", ((256, 2304), BF)),
    ("YR", ((3, 2, 128, 768), BF)),
    ("ZS", ((128, 768), BF)),
    ("ZR", ((128, 768), BF)),
    ("DWQ", ((2, 4, 2, 48, 512), BF)),
    ("QA1", ((3, 4, 48, 256), BF)),
    ("QA2", ((3, 48, 256), BF)),
    ("QB1", ((3, 2, 2, 48, 256), BF)),
    ("QB2", ((3, 48, 256), BF)),
    ("VEC", ((8, 1024), F32)),
    ("V1", ((3, 8, 1024), F32)),
    ("V2", ((3, 8, 1024), F32)),
    ("VE2", ((8, 1024), F32)),
    ("W2R", ((8, 8, 1024), F32)),
    ("WDG", ((16, 768), F32)),
    ("dwd_in", ((16, 768), F32)),
    ("out", ((2, 128, 768), BF)),
    ("din", ((2, 128, 768), F32)),
    ("dwq", ((6, 768), F32)),
    ("dwk", ((6, 768), F32)),
    ("dwv", ((6, 768), F32)),
    ("dwo", ((6, 768), F32)),
    ("dwg", ((6, 2048), F32)),
    ("dwu", ((6, 2048), F32)),
    ("dvec", ((8, 128), F32)),
    ("wq", ((6, 768), F32)),
    ("wk", ((6, 768), F32)),
    ("wv", ((6, 768), F32)),
    ("wo", ((6, 768), F32)),
    ("wg", ((6, 2048), F32)),
    ("wu", ((6, 2048), F32)),
    ("wd", ((16, 768), F32)),
    ("free_sem", 0),
    ("local_sem", 32),
    ("send_sem", None),
    ("recv_sem", None),
]


OUTPUTS = [
    ("h_out", ((2, 128, 768), BF)),
    ("h_din", ((2, 128, 768), F32)),
    ("h_dwq", ((6, 768), F32)),
    ("h_dwk", ((6, 768), F32)),
    ("h_dwv", ((6, 768), F32)),
    ("h_dwo", ((6, 768), F32)),
    ("h_dwg", ((6, 2048), F32)),
    ("h_dwu", ((6, 2048), F32)),
    ("h_dwd", ((16, 768), F32)),
    ("h_dvec", ((8, 128), F32)),
]


def call_mega(*args):
    spec = {"s": pl.BlockSpec(memory_space=pltpu.SMEM), "a": pl.BlockSpec(memory_space=pl.ANY)}
    outs = OUTPUTS
    scratch = []
    for _, s in SCRATCH:
        if s == 0:
            scratch.append(pltpu.SemaphoreType.REGULAR)
        elif s is None or isinstance(s, int):
            scratch.append(pltpu.SemaphoreType.DMA((s or NSEM,)))
        else:
            scratch.append(pltpu.VMEM(s[0], s[1]))
    return pl.pallas_call(
        mega,
        out_shape=[jax.ShapeDtypeStruct(s[0], s[1]) for _, s in outs],
        in_specs=[spec[k] for _, k in INPUTS],
        out_specs=[pl.BlockSpec(memory_space=pl.ANY) for _ in outs],
        scratch_shapes=scratch,
        name="layer",
        compiler_params=pltpu.CompilerParams(
            collective_id=0, has_side_effects=True, vmem_limit_bytes=62 * 2**20
        ),
    )(*args)


def per_device(
    tokens,
    lengths,
    cotangent,
    query_weight,
    key_weight,
    value_weight,
    out_weight,
    gate_weight,
    up_weight,
    down_weight,
    first_gain,
    second_gain,
    bias_table,
):
    done = call_mega(
        lengths,
        first_gain,
        second_gain,
        bias_table,
        tokens,
        cotangent,
        query_weight,
        key_weight,
        value_weight,
        out_weight,
        gate_weight,
        up_weight,
        down_weight,
    )
    return hand_out(*done)


def hand_out_kernel(*refs):
    n = len(OUTPUTS)
    vectors, ins, outs, held, sem = refs[0], refs[1:n], refs[n : 2 * n + 2], refs[2 * n + 2 : -1], refs[-1]
    loads = [pltpu.make_async_copy(a, b, sem.at[i]) for i, (a, b) in enumerate(zip(ins, held))]
    copies = [pltpu.make_async_copy(a, b, sem.at[i]) for i, (a, b) in enumerate(zip(held, outs))]
    for load in loads:
        load.start()
    for load, copy in zip(loads, copies):
        load.wait()
        copy.start()
    for row, (ref, width) in enumerate(zip(outs[n - 1 :], (6, 6, 3))):
        for i in range(width):
            ref[i] = vectors[row, i]
    for copy in copies:
        copy.wait()


def hand_out(*done):
    shapes = [jax.ShapeDtypeStruct(s[0], s[1]) for _, s in OUTPUTS[:-1]]
    shapes += [jax.ShapeDtypeStruct((n,), F32) for n in (6, 6, 3)]
    smem, hbm = pl.BlockSpec(memory_space=pltpu.SMEM), pl.BlockSpec(memory_space=pl.ANY)
    n = len(done) - 1
    return tuple(
        pl.pallas_call(
            hand_out_kernel,
            out_shape=shapes,
            in_specs=[smem] + [hbm] * n,
            out_specs=[hbm] * n + [smem] * 3,
            scratch_shapes=[pltpu.VMEM(s[0], s[1]) for _, s in OUTPUTS[:-1]]
            + [pltpu.SemaphoreType.DMA((n,))],
            name="hand_out",
        )(done[-1], *done[:-1])
    )


def solution(mesh):
    tokens = P("rows", "seq", None)
    matrix = P(("rows", "seq"), None)
    vector = P(("rows", "seq"))
    return jax.shard_map(
        per_device,
        mesh=mesh,
        in_specs=(tokens, P("rows"), tokens, *([matrix] * 7), *([vector] * 3)),
        out_specs=(tokens, tokens, *([matrix] * 7), *([vector] * 3)),
        check_vma=False,
    )
```

```python
import jax
import jax.numpy as jnp
from jax import lax
from jax.experimental import pallas as pl
from jax.experimental.pallas import tpu as pltpu
from jax.sharding import PartitionSpec as P

MESH = pl.DeviceIdType.MESH
BF = jnp.bfloat16
F32 = jnp.float32
D = 768
SEQ = 2048
EPSILON = 1e-06
NEGATIVE = -1e30
LIMITS = (1, 2, 3, 4, 5, 6, 7, 8, 12, 16, 23, 32, 46, 64, 91)
NSEM = 240
BQ = 256
STEPS = 12


def dev(x, y, z, c):
    return ((z % 2) * 4 + x, (y * 2 + z // 2) * 2 + c)


def first_head(t):
    return (3 * t) // 2


def iota(shape, dim):
    return lax.broadcasted_iota(jnp.int32, shape, dim)


def dot(a, b):
    return jnp.dot(a, b, preferred_element_type=F32)


def dot_nt(a, b):
    return lax.dot_general(a, b, (((1,), (1,)), ((), ())), preferred_element_type=F32)


class Comm:
    def __init__(self, x, y, z, c, send_sem, recv_sem):
        self.x, self.y, self.z, self.c = x, y, z, c
        self.ss, self.rs = send_sem, recv_sem
        self.next = 0
        self.pending = []

    def take(self, n=1):
        at = self.next
        self.next += n
        assert self.next <= NSEM
        return at

    def peer(self, axis, offset):
        x, y, z, c = self.x, self.y, self.z, self.c
        if axis == "x":
            return dev((x + offset) % 4, y, z, c)
        if axis == "y":
            return dev(x, (y + offset) % 4, z, c)
        if axis == "z":
            return dev(x, y, (z + offset) % 4, c)
        return dev(x, y, z, 1 - c)

    def place(self, axis, offset):
        at = {"x": self.x, "y": self.y, "z": self.z}[axis]
        return (at + offset) % 4

    def copy(self, src, dst, i, to, j=None):
        return pltpu.make_async_remote_copy(
            src_ref=src,
            dst_ref=dst,
            send_sem=self.ss.at[i],
            recv_sem=self.rs.at[i if j is None else j],
            device_id=to,
            device_id_type=MESH,
        )

    def send(self, src, dst, i, to):
        cp = self.copy(src, dst, i, to)
        cp.start()
        self.pending.append(cp)

    def recv(self, dst, i):
        self.copy(dst, dst, i, self.peer("c", 0)).wait_recv()

    def send_or_keep(self, src, dst, i, to, j, own):
        cp = self.copy(src, dst, i, to, j)
        keep = pltpu.make_async_copy(src, dst, self.rs.at[j])

        @pl.when(own)
        def _():
            keep.start()

        @pl.when(jnp.logical_not(own))
        def _():
            cp.start()

        self.pending.append((cp, own))

    def drain(self):
        for cp in self.pending:
            if isinstance(cp, tuple):
                cp, own = cp

                @pl.when(jnp.logical_not(own))
                def _():
                    cp.wait_send()
            else:
                cp.wait_send()
        self.pending = []


class Direct:
    def __init__(self, comm, axis, views):
        self.comm, self.axis, self.views = comm, axis, views
        self.count = len(views(comm.place(axis, 0)))
        self.base = comm.take(3 * self.count)

    def start(self):
        for k, off in enumerate((1, 3, 2)):
            for n, ref in enumerate(self.views(self.comm.place(self.axis, 0))):
                self.comm.send(ref, ref, self.base + k * self.count + n, self.comm.peer(self.axis, off))

    def wait(self):
        for k, off in enumerate((1, 3, 2)):
            for n, ref in enumerate(self.views(self.comm.place(self.axis, -off + 4))):
                self.comm.recv(ref, self.base + k * self.count + n)


class Ring:
    def __init__(self, comm, axis, views, halves):
        self.comm, self.axis, self.views, self.halves = comm, axis, views, halves
        self.count = len(views(comm.place(axis, 0)))
        self.base = comm.take(4 * self.count)

    def start(self, source=None):
        own = self.views(self.comm.place(self.axis, 0))
        for n, ref in enumerate(own):
            src = ref if source is None else source[n]
            for k, off in enumerate((1, 3)):
                self.comm.send(src, ref, self.base + k * self.count + n, self.comm.peer(self.axis, off))

    def forward(self):
        for k, off in enumerate((1, 3)):
            came = self.comm.place(self.axis, -off + 4)
            for n, ref in enumerate(self.views(came)):
                self.comm.recv(ref, self.base + k * self.count + n)
            for n, ref in enumerate(self.halves(came, k)):
                self.comm.send(ref, ref, self.base + (2 + k) * self.count + n, self.comm.peer(self.axis, off))

    def wait(self):
        far = self.comm.place(self.axis, 2)
        for k in range(2):
            for n, ref in enumerate(self.halves(far, k)):
                self.comm.recv(ref, self.base + (2 + k) * self.count + n)


class Scatter:
    def __init__(self, comm, axis, views, bufs):
        self.comm, self.axis, self.views, self.bufs = comm, axis, views, bufs
        self.base = comm.take(3 * len(bufs))

    def start(self):
        for k, off in enumerate((1, 3, 2)):
            refs = self.views(self.comm.place(self.axis, off))
            for n, ref in enumerate(refs):
                self.comm.send(
                    ref, self.bufs[n].at[k], self.base + k * len(refs) + n, self.comm.peer(self.axis, off)
                )

    def wait(self):
        for k in range(3):
            for n, buf in enumerate(self.bufs):
                self.comm.recv(buf.at[k], self.base + k * len(self.bufs) + n)


def bucket_ids(offsets):
    distance = jnp.abs(offsets)
    bucket_sum = jnp.where(offsets > 0, 16, 0)
    for threshold in LIMITS:
        bucket_sum = bucket_sum + jnp.where(distance >= threshold, 1, 0)
    return bucket_sum


def fold_rows(two):
    return jnp.concatenate([two[k : k + 1, 256 * i : 256 * i + 256] for k in range(2) for i in range(4)], axis=0)


def unfold_rows(eight):
    rows = [jnp.concatenate([eight[4 * k + i : 4 * k + i + 1] for i in range(4)], axis=1) for k in range(2)]
    return jnp.concatenate(rows, axis=0)


def rms_scale(values):
    return lax.rsqrt(jnp.mean(values * values, axis=-1, keepdims=True) + EPSILON)


def greet(comm):
    x, y, z, c = comm.x, comm.y, comm.z, comm.c
    zl, zh = z % 2, z // 2
    barrier = pltpu.get_barrier_semaphore()
    count = 0
    peers = []
    for dy in range(4):
        for dh in range(2):
            for dc in range(2):
                if dy or dh or dc:
                    peers.append(dev(x, (y + dy) % 4, ((zh + dh) % 2) * 2 + zl, (c + dc) % 2))
    for off in (1, 2, 3):
        peers.append(comm.peer("x", off))
    for off in (1, 3):
        peers.append(comm.peer("z", off))
    for peer in peers:
        pl.semaphore_signal(barrier, inc=1, device_id=peer, device_id_type=MESH)
        count += 1
    return barrier, count


def cast_up(v):
    return v.astype(F32)


def head_bias(tables, o):
    return tables[o : o + 1, 0:1], tables[o : o + 1, 1023:1024]


def mega(*refs):
    names = [n for n, _ in INPUTS] + [n for n, _ in OUTPUTS] + [n for n, _ in SCRATCH]
    r = dict(zip(names, refs))
    rows, seq = lax.axis_index("rows"), lax.axis_index("seq")
    x, y, zl, zh, c = rows % 4, seq // 4, rows // 4, (seq // 2) % 2, seq % 2
    z = zh * 2 + zl
    flat = rows * 16 + seq
    t = c * 4 + y
    comm = Comm(x, y, z, c, r["send_sem"], r["recv_sem"])
    local_sem = r["local_sem"]
    TK, CT, T5, tok, cot = r["TK"], r["CT"], r["T5"], r["tok"], r["cot"]
    loads = []
    for i, name in enumerate(("wq", "wk", "wv", "wo", "wg", "wu", "wd")):
        loads.append(pltpu.make_async_copy(r["h_" + name], r[name], local_sem.at[i]))
        loads[-1].start()
    keep_tokens = pltpu.make_async_copy(tok.at[zh], T5.at[y, zh, c], local_sem.at[7])
    keep_tk = pltpu.make_async_copy(tok, TK.at[:, c], local_sem.at[8])
    keep_ct = pltpu.make_async_copy(cot, CT.at[:, c], local_sem.at[9])
    keep_tokens.start()
    keep_tk.start()
    keep_ct.start()
    barrier, count = greet(comm)

    lanes = iota((1, 1024), 1)
    first_row = jnp.zeros((1, 1024), F32)
    second_row = jnp.zeros((1, 1024), F32)
    for i in range(6):
        first_row += jnp.where(lanes == 6 * flat + i, r["g1"][i], 0.0)
        second_row += jnp.where(lanes == 6 * flat + i, r["g2"][i], 0.0)
    for i in range(3):
        at = 768 + 3 * flat + i
        first_row += jnp.where(lanes == at, r["bt"][i], 0.0)
        second_row += jnp.where((lanes >= 768) & (lanes == at - 256), r["bt"][i], 0.0)
    first_row = cast_up(first_row.astype(BF))
    second_row = cast_up(second_row.astype(BF))
    wst, w0 = r["wst"], r["w0"]
    for load in loads:
        load.wait()
    for cc in range(2):
        for yy in range(4):
            d, h0 = cc * 4 + yy, first_head(cc * 4 + yy)
            for i, name in enumerate(("wq", "wk", "wv")):
                wst[d, 0:6, 128 * i : 128 * (i + 1)] = r[name][:, 64 * h0 : 64 * h0 + 128]
            for i, name in enumerate(("wg", "wu")):
                for k in range(2):
                    tile = 2 * (2 * yy + k) + cc
                    at = 512 + 256 * i + 128 * k
                    wst[d, 0:6, at : at + 128] = r[name][:, 128 * tile : 128 * tile + 128]
            if yy < 3:
                at = (cc * 3 + yy) * 128
                wst[d, 0:6, 384:512] = r["wo"][:, at : at + 128]
            else:
                wst[d, 0:6, 384:512] = jnp.zeros((6, 128), F32)
            wst[d, 6:7, :] = first_row
            wst[d, 7:8, :] = second_row
    r["wdst"][...] = r["wd"][...].astype(BF)

    pl.semaphore_wait(barrier, count)

    W1, WD, WQ, G5 = r["W1"], r["WD"], r["WQ"], r["G5"]
    slot = (y % 2) * 4 + zh * 2 + c
    base0 = comm.take(8)
    baser = comm.take(8)
    for cc in range(2):
        for yy in range(4):
            to = dev(x, yy, (y // 2) * 2 + zl, cc)
            own = (y == yy) & (c == cc) & (zh == y // 2)
            cp = comm.copy(wst.at[cc * 4 + yy], w0.at[slot], base0 + cc * 4 + yy, to, baser + slot)
            keep = pltpu.make_async_copy(wst.at[cc * 4 + yy], w0.at[slot], comm.rs.at[baser + slot])
            pl.when(own)(keep.start)
            pl.when(jnp.logical_not(own))(cp.start)
            comm.pending.append((cp, own))
    wd_to = (zh * 2 + c, y % 2, y // 2)
    own_wd = (wd_to[0] == y) & (wd_to[1] == zh) & (wd_to[2] == c)
    wdi = comm.take()
    wd_region = WD.at[zl, x, wd_to[1], wd_to[0]]
    comm.send_or_keep(
        r["wdst"], wd_region, wdi, dev(x, wd_to[0], wd_to[1] * 2 + zl, wd_to[2]), wdi, own_wd
    )

    other = comm.peer("z", 2)
    zi = comm.take()
    comm.send(tok.at[1 - zh], T5.at[y, zh, c], zi, other)
    own_tokens = Ring(
        comm,
        "y",
        lambda yy: [T5.at[yy, zh, c]],
        lambda yy, k: [T5.at[yy, zh, c, pl.ds(64 * k, 64)]],
    )
    own_tokens.start(source=[tok.at[zh]])
    pair = comm.take(2)

    for j in range(8):
        comm.recv(w0.at[j], baser + j)
    asm = r["asm"]
    gsum = jnp.zeros((2, 1024), F32)
    for j in range(8):
        asm[6 * j : 6 * j + 6, :] = w0[j, 0:6, :]
        gsum += w0[j, 6:8, :]
    WQ[zl, x, zh] = asm[:, 0:512].astype(BF)
    G5[zl, x, zh] = fold_rows(gsum)
    W1[zl, x, zh, y] = asm[:, 512:1024].astype(BF)
    qkv_a1 = Direct(comm, "x", lambda xx: [WQ.at[zl, xx, zh, :, pl.ds(0, 256)], G5.at[zl, xx, zh]])
    qkv_b1 = Direct(comm, "z", lambda zz: [WQ.at[zz % 2, x, zz // 2, :, pl.ds(256, 256)]])
    qkv_a1.start()
    qkv_b1.start()
    comm.recv(WD.at[zl, x, zh, y], wdi)
    ff_y = Direct(comm, "y", lambda yy: [W1.at[zl, x, zh, yy], WD.at[zl, x, zh, yy]])
    ff_y.start()

    comm.recv(T5.at[y, 1 - zh, c], zi)
    far_tokens = Ring(
        comm,
        "y",
        lambda yy: [T5.at[yy, 1 - zh, c]],
        lambda yy, k: [T5.at[yy, 1 - zh, c, pl.ds(64 * k, 64)]],
    )
    far_tokens.start()
    keep_tokens.wait()
    sib = comm.peer("c", 0)
    across = comm.take(4)

    def cross(k):
        yy = (y + (0, 1, 3, 2)[k]) % 4
        comm.send(T5.at[yy, :, c], T5.at[yy, :, c], across + k, sib)

    def crossed(k):
        yy = (y + (0, 1, 3, 2)[k]) % 4
        comm.recv(T5.at[yy, :, 1 - c], across + k)

    cross(0)
    qkv_a1.wait()
    qkv_b1.wait()
    qkv_a2 = Direct(
        comm,
        "z",
        lambda zz: [WQ.at[zz % 2, :, zz // 2, :, pl.ds(0, 256)], G5.at[zz % 2, :, zz // 2]],
    )
    qkv_b2 = Direct(comm, "x", lambda xx: [WQ.at[:, xx, :, :, pl.ds(256, 256)]])
    qkv_a2.start()
    qkv_b2.start()
    own_tokens.forward()
    ff_y.wait()
    low, high = pl.ds(0, 256), pl.ds(256, 256)
    low_d, high_d = pl.ds(0, 256), pl.ds(256, 512)
    ff_a1 = Direct(
        comm, "x", lambda xx: [W1.at[zl, xx, zh, :, :, low], WD.at[zl, xx, zh, :, :, low_d]]
    )
    ff_b1 = Direct(
        comm,
        "z",
        lambda zz: [
            W1.at[zz % 2, x, zz // 2, :, :, high],
            WD.at[zz % 2, x, zz // 2, :, :, high_d],
        ],
    )
    ff_a1.start()
    ff_b1.start()
    far_tokens.forward()
    cross(1)
    cross(2)
    keep_tk.wait()
    keep_ct.wait()
    comm.send(TK.at[:, c], TK.at[:, c], pair, sib)
    comm.send(CT.at[:, c], CT.at[:, c], pair + 1, sib)

    qkv_a2.wait()
    qkv_b2.wait()
    WOF = r["WOF"]
    base_w = comm.take(8)
    base_wr = comm.take(8)
    for cc in range(2):
        for yy in range(4):
            src = WQ.at[cc, :, :, :, pl.ds(384, 128)]
            dst = WOF.at[:, :, :, pl.ds(pl.multiple_of((c * 3 + y % 3) * 128, 128), 128)]
            cp = comm.copy(src, dst, base_w + cc * 4 + yy, dev(x, yy, z, cc), base_wr + c * 4 + y)
            keep = pltpu.make_async_copy(src, dst, comm.rs.at[base_wr + c * 4 + y])
            here = (yy == y) & (cc == c)
            pl.when(here & (y < 3))(keep.start)
            pl.when(jnp.logical_not(here) & (y < 3))(cp.start)
            comm.pending.append((cp, here | (y == 3)))
    total = jnp.zeros((8, 256), F32)
    for a in range(2):
        for b in range(4):
            for e in range(2):
                total += G5[a, b, e]
    total = unfold_rows(total)
    r["GS"][0:2, :] = total
    h0 = first_head(t)
    table_row = jnp.concatenate([total[0:1, 768:1024], total[1:2, 768:896]], axis=1)
    table_row = jnp.broadcast_to(table_row, (8, 384))
    table_row = pltpu.roll(table_row, 384 - 32 * h0, 1)[:, 0:128]
    lane = iota((8, 128), 1)
    sub = iota((8, 128), 0)
    table_two = jnp.where((lane // 32) == sub, table_row, 0.0).astype(BF)
    r["OH"][...] = jnp.where(
        bucket_ids(iota((128, 1024), 1) - 512) == iota((128, 1024), 0) % 32, 1.0, 0.0
    ).astype(BF)
    by_offset = dot(table_two, r["OH"][...])
    r["BO"][...] = by_offset
    for h in range(2):
        for k in range(4):
            rolled = pltpu.roll(
                jnp.broadcast_to(by_offset[h : h + 1, :], (64, 1024)), 640 + 64 * k, 1, stride=1, stride_axis=0
            )
            r["BT"][h, 64 * k : 64 * k + 64, :] = rolled[:, 0:512]

    ff_a1.wait()
    ff_b1.wait()
    ff_a2 = Ring(
        comm,
        "z",
        lambda zz: [
            W1.at[zz % 2, :, zz // 2, :, :, low],
            WD.at[zz % 2, :, zz // 2, :, :, low_d],
        ],
        lambda zz, k: [
            W1.at[zz % 2, pl.ds(2 * k, 2), zz // 2, :, :, low],
            WD.at[zz % 2, pl.ds(2 * k, 2), zz // 2, :, :, low_d],
        ],
    )
    ff_b2 = Ring(
        comm,
        "x",
        lambda xx: [W1.at[:, xx, :, :, :, high], WD.at[:, xx, :, :, :, high_d]],
        lambda xx, k: [W1.at[k, xx, :, :, :, high], WD.at[k, xx, :, :, :, high_d]],
    )
    ff_a2.start()
    ff_b2.start()

    QA, KT, KN, VN, VT = r["QA"], r["KT"], r["KN"], r["VN"], r["VT"]
    row_len = r["lens"][zh]

    def project(i, carry):
        raw = cast_up(T5[i // 2, i % 2].reshape(256, D))
        normed = (raw * rms_scale(raw) * r["GS"][0:1, 0:768]).astype(BF)
        res = dot(normed, WQ[:, :, :, :, 0:384].reshape(D, 384))
        q, k_, v = res[:, 0:128], res[:, 128:256], res[:, 256:384]
        at = pl.ds(pl.multiple_of(i * 256, 256), 256)
        KN[at, :] = k_.astype(BF)
        VN[at, :] = jnp.concatenate([v, jnp.ones((256, 128), F32)], axis=1).astype(BF)
        VT[:, at] = v.T.astype(BF)
        kt = k_.T
        lane = iota((256, 128), 1)
        sub = iota((128, 256), 0)
        key_at = i * 256 + iota((128, 256), 1)
        for h in range(2):
            base = 64 * (1 - h)
            hot = jnp.where((lane == base + i) | (lane == base + 8), 1.0, 0.0)
            QA[h, at, :] = jnp.where(lane // 64 == h, q, hot).astype(BF)
            left, right = head_bias(r["BO"][...], h)
            start = 256 * (sub - base)
            extra = jnp.where(key_at < start - 128, left, 0.0) + jnp.where(
                key_at >= start + 384, right, 0.0
            )
            masked = jnp.where(key_at >= row_len, NEGATIVE, 0.0)
            extra = jnp.where(sub - base < 8, extra, jnp.where(sub - base == 8, masked, 0.0))
            KT[h, :, at] = jnp.where(sub // 64 == h, kt, extra).astype(BF)
        return carry

    for k in range(4):
        if k == 3:
            own_tokens.wait()
            far_tokens.wait()
            cross(3)
        crossed(k)
        first = 2 * ((y + (0, 1, 3, 2)[k]) % 4)
        lax.fori_loop(first, first + 2, project, 0)
    r["ON"][...] = jnp.zeros((SEQ, 128), BF)
    r["LI"][...] = jnp.zeros((1024, 128), F32)
    r["PB"][:, :, 0:128] = jnp.zeros((3, 1024, 128), BF)
    r["PB"][:, :, 2176:2304] = jnp.zeros((3, 1024, 128), BF)

    SC, PB, BT, ON, LI = r["SC"], r["PB"], r["BT"], r["ON"], r["LI"]

    def unit_of(step):
        ui = step // 4
        u = jnp.where(ui == 0, 1, jnp.where(ui == 1, 0, 2))
        number = 3 * t + u
        head = number // 2 - h0
        start = (number % 2) * 1024 + (step % 4) * 256
        return head, pl.multiple_of(start, 256)

    S2 = r["S2"]

    def score_part(step, buf, j, top):
        head, q0 = unit_of(step)
        s = dot(QA[head, pl.ds(q0, BQ), :], KT[head, :, 256 * j : 256 * j + 256])
        buf[:, 128 + 256 * j : 384 + 256 * j] = s
        most = jnp.maximum(s[:, 0:128], s[:, 128:256])
        return most if top is None else jnp.maximum(top, most)

    def score_end(step, buf, top):
        head, q0 = unit_of(step)
        buf[:, pl.ds(q0, 512)] = buf[:, pl.ds(q0, 512)] + BT[head]
        return jnp.max(top, axis=1, keepdims=True)

    def block_of(step):
        return pl.ds(pl.multiple_of((step % 4) * 256, 256), BQ)

    def prob_part(step, buf, j, top):
        for k in (2 * j + 1, 2 * j + 2):
            p = jnp.exp(buf[:, 128 * k : 128 * k + 128] - top)
            PB[step // 4, block_of(step), 128 * k : 128 * k + 128] = p.astype(BF)

    def mix(step):
        head, q0 = unit_of(step)
        mixed = dot(PB[step // 4, block_of(step), 128:2176], VN[...])
        inv = 1.0 / mixed[:, 128:129]
        lane = iota((BQ, 128), 1)
        LI[block_of(step), :] = jnp.where(lane == step // 4, inv, LI[block_of(step), :])
        mixed = mixed[:, 0:128] * inv
        ON[pl.ds(q0, BQ), :] = jnp.where(lane // 64 == head, mixed, cast_up(ON[pl.ds(q0, BQ), :])).astype(BF)

    def first_scores(step):
        top = None
        for j in range(8):
            top = score_part(step, SC, j, top)
        return score_end(step, SC, top)

    def attend(pair, top_a):
        one, two = 2 * pair, 2 * pair + 1
        top_b = None
        for j in range(8):
            top_b = score_part(two, S2, j, top_b)
            prob_part(one, SC, j, top_a)
        top_b = score_end(two, S2, top_b)
        mix(one)
        then = jnp.minimum(two + 1, STEPS - 1)
        top_a = None
        for j in range(8):
            prob_part(two, S2, j, top_b)
            top_a = score_part(then, SC, j, top_a)
        top_a = score_end(then, SC, top_a)
        mix(two)
        return top_a

    A = r["A"]
    base_o = comm.take(8)
    base_or = comm.take(8)

    def give(half, n):
        for i in range(4):
            yy, hh = 2 * half + i // 2, i % 2
            src = ON.at[pl.ds(pl.multiple_of(256 * (yy * 2 + hh), 256), 256)]
            dst = A.at[zh, :, pl.ds(pl.multiple_of(128 * y, 128), 128)]
            own = (yy == y) & (hh == zh)
            cp = comm.copy(src, dst, base_o + 4 * n + i, dev(x, yy, hh * 2 + zl, c), base_or + y * 2 + zh)
            keep = pltpu.make_async_copy(src, dst, comm.rs.at[base_or + y * 2 + zh])
            pl.when(own)(keep.start)
            pl.when(jnp.logical_not(own))(cp.start)
            comm.pending.append((cp, own))

    single = (3 * t + 1) % 2
    top_now = lax.fori_loop(0, 2, attend, first_scores(0))
    give(single, 0)
    top_now = lax.fori_loop(2, 3, attend, top_now)
    ff_a2.forward()
    ff_b2.forward()
    lax.fori_loop(3, STEPS // 2, attend, top_now)
    give(1 - single, 1)
    for yy in range(4):
        for hh in range(2):
            comm.recv(A.at[hh, :, pl.ds(128 * yy, 128)], base_or + yy * 2 + hh)
    comm.recv(TK.at[:, 1 - c], pair)
    comm.recv(CT.at[:, 1 - c], pair + 1)

    lane = iota((256, 128), 1)
    for hh in range(2):
        p0, p1, p2, p3 = [cast_up(A[hh, :, 128 * k : 128 * k + 128]) for k in range(4)]
        p1, p2 = pltpu.roll(p1, 64, 1), pltpu.roll(p2, 64, 1)
        A[hh, :, 0:128] = (p0 + jnp.where(lane >= 64, p1, 0.0)).astype(BF)
        A[hh, :, 128:256] = jnp.where(lane < 64, p1, p2).astype(BF)
        A[hh, :, 256:384] = (p3 + jnp.where(lane < 64, p2, 0.0)).astype(BF)
    for cc in range(2):
        for yy in range(3):
            comm.recv(WOF.at[:, :, :, pl.ds(128 * (cc * 3 + yy), 128)], base_wr + cc * 4 + yy)

    POS, POR, N2, N2T = r["POS"], r["POR"], r["N2"], r["N2T"]
    base_p = comm.take(2)
    for hh in range(2):
        term = dot(A[hh, :, 0:384], WOF[...].reshape(384, D))
        POS[hh] = term.astype(BF).reshape(2, 128, D)
        comm.send(POS.at[hh], POR.at[hh], base_p + hh, sib)
    second_gain = r["GS"][1:2, 0:768]
    for hh in range(2):
        comm.recv(POR.at[hh], base_p + hh)
        for k in range(2):
            middle = cast_up(TK[hh, k]) + (cast_up(POS[hh, k]) + cast_up(POR[hh, k]))
            S2[128 * hh : 128 * hh + 128, 768 * k : 768 * k + 768] = middle
            normed = middle * rms_scale(middle) * second_gain
            N2[128 * k : 128 * k + 128, 768 * hh : 768 * hh + 768] = normed.astype(BF)
            at = 256 * hh + 128 * k
            N2T[:, at : at + 128] = normed.T.astype(BF)

    HX, HIDT, GU = r["HX"], r["HIDT"], r["GU"]

    def gated(k, carry):
        gate_w = W1[:, :, :, k, :, 0:256].reshape(D, 256)
        up_w = W1[:, :, :, k, :, 256:512].reshape(D, 256)
        down_w = WD[k // 2, pl.ds((2 * k) % 4, 2)].reshape(256, D)
        for hh in range(2):
            gate = dot(N2[:, 768 * hh : 768 * hh + 768], gate_w)
            up = dot(N2[:, 768 * hh : 768 * hh + 768], up_w)
            back = dot_nt(CT[hh].reshape(256, D), down_w)
            square = gate * gate
            th = jnp.tanh(0.7978845608028654 * (gate + 0.044715 * (square * gate)))
            half = 0.5 * (1.0 + th)
            gelu = gate * half
            slope = half + (0.5 * gate) * (1.0 - th * th) * (
                0.7978845608028654 * (1.0 + 3 * 0.044715 * square)
            )
            hidden = gelu * up
            cols = pl.ds(pl.multiple_of(256 * k, 256), 256)
            HX[:, pl.ds(pl.multiple_of(1024 * hh + 256 * k, 256), 256)] = hidden.astype(BF)
            HIDT[cols, 256 * hh : 256 * hh + 256] = hidden.T.astype(BF)
            both = pl.multiple_of(512 * k, 512)
            GU[hh, :, :, pl.ds(both, 256)] = (back * up * slope).astype(BF).reshape(2, 128, 256)
            GU[hh, :, :, pl.ds(both + 256, 256)] = (back * gelu).astype(BF).reshape(2, 128, 256)
        return carry

    ff_a2.wait()
    ff_b2.wait()
    lax.fori_loop(0, 4, gated, 0)
    PNR, SC = r["PNR"], r["SC"]
    base_n = comm.take(2)
    comm.drain()
    for hh in range(2):
        term = dot_nt(GU[hh, :, :, 0:512].reshape(256, 512), W1[:, :, :, 0].reshape(D, 512))
        for k in range(1, 4):
            term += dot_nt(
                GU[hh, :, :, 512 * k : 512 * k + 512].reshape(256, 512), W1[:, :, :, k].reshape(D, 512)
            )
        POS[hh] = term.astype(BF).reshape(2, 128, D)
        comm.send(POS.at[hh], PNR.at[hh], base_n + hh, sib)
    PYS, PYR = r["PYS"], r["PYR"]
    yi = comm.take()
    down_all = WD[...].reshape(1024, D)
    for hh in range(2):
        PYS[hh] = dot(HX[pl.ds(pl.multiple_of(128 * (1 - c), 128), 128), 1024 * hh : 1024 * hh + 1024], down_all).astype(BF)
    comm.send(PYS, PYR, yi, sib)
    for hh in range(2):
        SC[128 * hh : 128 * hh + 128, 0:768] = dot(HX[pl.ds(pl.multiple_of(128 * c, 128), 128), 1024 * hh : 1024 * hh + 1024], down_all)

    low_r, high_r = pl.ds(0, 256), pl.ds(256, 512)
    def down_term(k, carry):
        res = dot(HIDT[pl.ds(pl.multiple_of(256 * k, 256), 256), :], CT[...].reshape(512, D))
        WD[k // 2, pl.ds((2 * k) % 4, 2)] = res.astype(BF).reshape(2, 2, 4, 16, D)
        return carry

    lax.fori_loop(0, 4, down_term, 0)
    wd_ra = Scatter(
        comm, "z", lambda zz: [WD.at[zz % 2, :, zz // 2, :, :, low_r]], [r["RA2"]]
    )
    wd_rb = Scatter(comm, "x", lambda xx: [WD.at[:, xx, :, :, :, high_r]], [r["RB2"]])
    wd_rb.start()

    ML, DOS, DO, VEC = r["ML"], r["DOS"], r["DO"], r["VEC"]
    VEC[...] = jnp.zeros((8, 1024), F32)
    base_d = comm.take(8)
    base_dr = comm.take(8)
    m = y * 2 + zh
    for hh in range(2):
        comm.recv(PNR.at[hh], base_n + hh)
        for k in range(2):
            grad = cast_up(POS[hh, k]) + cast_up(PNR[hh, k])
            middle = S2[128 * hh : 128 * hh + 128, 768 * k : 768 * k + 768]
            scale = rms_scale(middle)
            gained = grad * second_gain
            mean = jnp.mean(middle * gained, axis=-1, keepdims=True)
            full = cast_up(CT[hh, k]) + scale * gained - middle * (scale * scale * scale * mean)
            ML[hh, k] = full.astype(BF)

            @pl.when(c == k)
            def _():
                r["din"][hh] = full
                VEC[1:2, 0:768] += jnp.sum(grad * middle * scale, axis=0, keepdims=True)

        given = dot_nt(ML[hh].reshape(256, D), WOF[...].reshape(384, D))
        g0, g1, g2 = given[:, 0:128], given[:, 128:256], given[:, 256:384]
        r0, r1, r2 = pltpu.roll(g0, 64, 1), pltpu.roll(g1, 64, 1), pltpu.roll(g2, 64, 1)
        DOS[0, hh] = g0.astype(BF)
        DOS[1, hh] = jnp.where(lane < 64, r0, r1).astype(BF)
        DOS[2, hh] = jnp.where(lane < 64, r1, r2).astype(BF)
        DOS[3, hh] = g2.astype(BF)
        for yy in range(4):
            dst = DO.at[pl.ds(pl.multiple_of(256 * m, 256), 256)]
            own = (yy == y) & (hh == zh)
            cp = comm.copy(DOS.at[yy, hh], dst, base_d + 4 * hh + yy, dev(x, yy, hh * 2 + zl, c), base_dr + m)
            keep = pltpu.make_async_copy(DOS.at[yy, hh], dst, comm.rs.at[base_dr + m])
            pl.when(own)(keep.start)
            pl.when(jnp.logical_not(own))(cp.start)
            comm.pending.append((cp, own))


    def gated_term(k, carry):
        res = dot(N2T[...], GU[:, :, :, pl.ds(pl.multiple_of(512 * k, 512), 512)].reshape(512, 512))
        W1[:, :, :, k] = res.astype(BF).reshape(2, 4, 2, 48, 512)
        return carry

    lax.fori_loop(0, 4, gated_term, 0)
    pl.semaphore_signal(r["free_sem"], inc=1, device_id=sib, device_id_type=MESH)
    ff_ra = Scatter(comm, "z", lambda zz: [W1.at[zz % 2, :, zz // 2, :, :, low]], [r["RA1"]])
    ff_rb = Scatter(comm, "x", lambda xx: [W1.at[:, xx, :, :, :, high]], [r["RB1"]])
    ff_rb.start()
    attended_t = jnp.concatenate(
        [cast_up(A[hh, :, 0:384]).T.astype(BF) for hh in range(2)], axis=1
    )
    WOF[...] = dot(attended_t, ML[...].reshape(512, D)).astype(BF).reshape(4, 2, 48, D)
    base_g = comm.take(6)
    base_gr = comm.take(8)
    WOR = r["WOR"]
    for cc in range(2):
        for yy in range(3):
            src = WOF.at[:, :, :, pl.ds(128 * (cc * 3 + yy), 128)]
            cp = comm.copy(src, WOR.at[y, c], base_g + cc * 3 + yy, dev(x, yy, z, cc), base_gr + c * 4 + y)
            keep = pltpu.make_async_copy(src, WOR.at[y, c], comm.rs.at[base_gr + c * 4 + y])
            here = (yy == y) & (cc == c)
            pl.when(here)(keep.start)
            pl.when(jnp.logical_not(here))(cp.start)
            comm.pending.append((cp, here))
    comm.recv(PYR, yi)
    for hh in range(2):
        middle = S2[128 * hh : 128 * hh + 128, pl.ds(pl.multiple_of(768 * c, 128), 768)]
        r["out"][hh] = (middle + SC[128 * hh : 128 * hh + 128, 0:768] + cast_up(PYR[hh])).astype(BF)
    stores = [pltpu.make_async_copy(r["out"], r["h_out"], local_sem.at[10])]
    stores[0].start()

    SC[:, 0:2048] = jnp.zeros((256, SEQ), F32)
    S2[0:128, 0:2048] = jnp.zeros((128, SEQ), F32)
    N2[:, 0:1024] = jnp.zeros((BQ, 1024), BF)
    BT[...] = jnp.zeros((2, 256, 512), F32)
    for yy in range(4):
        for hh in range(2):
            comm.recv(DO.at[pl.ds(256 * (yy * 2 + hh), 256)], base_dr + yy * 2 + hh)
    wd_ra.start()
    ff_ra.start()

    GL, DL = r["GL"], r["DL"]

    def retreat(ui, carry):
        head, q0 = unit_of(4 * ui)
        rows = pl.ds(pl.multiple_of(q0, 1024), 1024)
        lane = iota((1024, 128), 1)
        inv = jnp.sum(jnp.where(lane == ui, LI[...], 0.0), axis=1, keepdims=True)
        given = jnp.where(lane // 64 == head, cast_up(DO[rows, :]) * inv, 0.0)
        GL[...] = given.astype(BF)
        delta = jnp.sum(cast_up(GL[...]) * cast_up(ON[rows, :]), axis=1, keepdims=True)
        DL[...] = jnp.broadcast_to(delta, (1024, 128))
        given_t = given.T.astype(BF)
        for j in range(8):
            S2[0:128, 256 * j : 256 * j + 256] += dot(given_t, PB[ui, :, 128 + 256 * j : 384 + 256 * j])

        def inner(b, more):
            block = pl.ds(pl.multiple_of(256 * b, 256), 256)
            low_rows = GL[block, :]
            shift = DL[block, 0:1]
            for j in range(8):
                cols = slice(128 + 256 * j, 384 + 256 * j)
                grad = dot(low_rows, VT[:, 256 * j : 256 * j + 256])
                PB[ui, block, cols] = (cast_up(PB[ui, block, cols]) * (grad - shift)).astype(BF)
            moved = dot(PB[ui, block, 128:2176], KN[...])
            at = q0 + 256 * b
            lane = iota((BQ, 128), 1)
            spot = pl.ds(pl.multiple_of(at // 2, 128), 128)
            N2[:, spot] = jnp.where(lane // 64 == head, moved, cast_up(N2[:, spot])).astype(BF)
            BT[head] += cast_up(PB[ui, block, pl.ds(pl.multiple_of(at, 256), 512)])
            return more

        lax.fori_loop(0, 4, inner, 0)
        query_t = cast_up(QA[head, rows, :]).T.astype(BF)
        key_rows = pl.ds(pl.multiple_of(128 * head, 128), 128)
        for j in range(8):
            SC[key_rows, 256 * j : 256 * j + 256] += dot(query_t, PB[ui, :, 128 + 256 * j : 384 + 256 * j])
        return carry

    def add_low(refs, bufs):
        for ref, buf in zip(refs, bufs):
            total = cast_up(ref[...])
            for k in range(3):
                total += cast_up(buf[k])
            ref[...] = total.astype(BF)

    lax.fori_loop(0, 3, retreat, 0)

    YR, DWQ = r["YR"], r["DWQ"]
    first_gain = r["GS"][0:1, 0:768]
    base_s = comm.take(4)
    S2[128:256, :] = jnp.zeros((128, 2304), F32)

    def sib_at(yy):
        return GU.at[yy // 2, :, :, pl.ds(pl.multiple_of((yy % 2) * 1024, 128), 768)]

    def place_of(k):
        return (y + jnp.where(k == 0, 2, jnp.where(k == 1, 1, jnp.where(k == 2, 3, 0)))) % 4

    def spread_back(k, carry):
        yy = place_of(k)

        def half(hh, inner):
            at = pl.ds(pl.multiple_of(512 * yy + 256 * hh, 256), 256)
            raw = cast_up(T5[yy, hh].reshape(256, D))
            scale = rms_scale(raw)
            normed = (raw * scale * first_gain).astype(BF)
            dq = N2[:, pl.ds(pl.multiple_of(256 * yy + 128 * hh, 128), 128)]
            sub = iota((128, 256), 0)
            dkt = jnp.where(sub < 64, SC[0:128, at], SC[128:256, at])
            dvt = S2[0:128, at]
            dk, dv = dkt.T.astype(BF), dvt.T.astype(BF)
            dqt = cast_up(dq).T.astype(BF)
            grad = dot_nt(jnp.concatenate([dq, dk, dv], axis=1), WQ[:, :, :, :, 0:384].reshape(D, 384))
            VEC[0:1, 0:768] += jnp.sum(grad * raw * scale, axis=0, keepdims=True)
            S2[128:256, 0:768] += dot(dqt, normed)
            S2[128:256, 768:1536] += dot(dkt.astype(BF), normed)
            S2[128:256, 1536:2304] += dot(dvt.astype(BF), normed)
            T5[yy, hh] = grad.astype(BF).reshape(2, 128, D)
            return inner

        lax.fori_loop(0, 2, half, 0)
        comm.copy(T5.at[yy, :, 1 - c], sib_at(yy), base_s + k, sib).start()
        return carry

    base_y = comm.take(3)

    def pass_on(k):
        yy = (y + (2, 1, 3, 0)[k]) % 4
        comm.recv(sib_at(yy), base_s + k)
        for hh in range(2):
            T5[yy, hh, c] = (cast_up(T5[yy, hh, c]) + cast_up(sib_at(yy)[hh])).astype(BF)
        if k < 3:
            comm.send(T5.at[yy, :, c], YR.at[k], base_y + k, comm.peer("y", (2, 1, 3)[k]))

    pl.semaphore_wait(r["free_sem"], 1)
    for k in range(4):
        spread_back(k, 0)
        if k:
            pass_on(k - 1)
    for i in range(3):
        DWQ[:, :, :, :, 128 * i : 128 * i + 128] = S2[128:256, 768 * i : 768 * i + 768].T.astype(BF).reshape(2, 4, 2, 48, 128)

    q_ra = Scatter(
        comm,
        "z",
        lambda zz: [DWQ.at[zz % 2, :, zz // 2, :, low]],
        [r["QA1"]],
    )
    q_ra.start()
    @pl.when(y == 3)
    def _():
        DWQ[:, :, :, :, 384:512] = jnp.zeros((2, 4, 2, 48, 128), BF)

    @pl.when(y < 3)
    def _():
        for k in range(4):
            for cc in range(2):
                comm.recv(WOR.at[k, cc], base_gr + cc * 4 + k)
        for cc in range(2):
            total = cast_up(WOR[0, cc])
            for k in range(1, 4):
                total += cast_up(WOR[k, cc])
            DWQ[cc, :, :, :, 384:512] = total.astype(BF)

    q_rb = Scatter(
        comm,
        "x",
        lambda xx: [DWQ.at[:, xx, :, :, high]],
        [r["QB1"]],
    )
    lane = iota((8, 128), 1)
    sub = iota((8, 128), 0)
    diagonals = []
    flip = jnp.where(iota((256, 256), 0) + iota((256, 256), 1) == 255, 1.0, 0.0).astype(BF)
    table_grad = jnp.zeros((1, 128), F32)
    one = iota((1, 128), 1)
    for h in range(2):
        near = jnp.zeros((1, 1024), F32)
        whole = BT[h]
        upper = whole.astype(BF)
        lower = (whole - cast_up(upper)).astype(BF)
        flipped = dot(flip, upper) + dot(flip, lower)
        for k in range(4):
            part = jnp.concatenate([flipped[64 * k : 64 * k + 64], jnp.zeros((64, 512), F32)], axis=1)
            part = pltpu.roll(part, 129 + 64 * k, 1, stride=1, stride_axis=0)
            near += jnp.sum(part, axis=0, keepdims=True)
        diagonals.append(near)
        base = 64 * (1 - h)
        rows_far = SC[128 * h + base : 128 * h + base + 8, 0:2048]
        key_at = iota((8, SEQ), 1)
        start = 256 * iota((8, SEQ), 0)
        left = jnp.sum(jnp.where(key_at < start - 128, rows_far, 0.0), axis=(0, 1), keepdims=True)
        right = jnp.sum(jnp.where(key_at >= start + 384, rows_far, 0.0), axis=(0, 1), keepdims=True)
        table_grad += jnp.where(one == 32 * h + 15, left, 0.0) + jnp.where(one == 32 * h + 31, right, 0.0)
    near = jnp.concatenate(diagonals + [jnp.zeros((6, 1024), F32)], axis=0)
    upper = near.astype(BF)
    lower = (near - cast_up(upper)).astype(BF)
    sums = dot_nt(upper, r["OH"][...]) + dot_nt(lower, r["OH"][...])
    table_grad += jnp.sum(jnp.where(lane // 32 == sub, sums, 0.0), axis=0, keepdims=True)
    spread = jnp.concatenate([table_grad, jnp.zeros((1, 256), F32)], axis=1)
    spread = pltpu.roll(jnp.broadcast_to(spread, (8, 384)), 32 * h0, 1)
    VEC[0:1, 768:1024] = spread[0:1, 0:256]
    VEC[1:2, 768:896] = spread[0:1, 256:384]

    VP = r["VP"]
    VP[...] = fold_rows(VEC[0:2, :])
    v_z = Scatter(comm, "z", lambda zz: [VP], [r["V1"]])
    q_rb.start()
    v_z.start()
    pass_on(3)
    wd_ra.wait()
    wd_rb.wait()
    ff_ra.wait()
    ff_rb.wait()

    def add_a(i, carry):
        add_low(
            [W1.at[zl, i, zh, :, :, low], WD.at[zl, i, zh, :, :, low_r]],
            [r["RA1"].at[:, i], r["RA2"].at[:, i]],
        )
        add_low(
            [W1.at[i // 2, x, i % 2, :, :, high], WD.at[i // 2, x, i % 2, :, :, high_r]],
            [r["RB1"].at[:, i // 2, i % 2], r["RB2"].at[:, i // 2, i % 2]],
        )
        return carry

    lax.fori_loop(0, 4, add_a, 0)
    ff_ra2 = Scatter(
        comm,
        "x",
        lambda xx: [W1.at[zl, xx, zh, :, :, low], WD.at[zl, xx, zh, :, :, low_r]],
        [r["SA1"], r["SA2"]],
    )
    ff_rb2 = Scatter(
        comm,
        "z",
        lambda zz: [
            W1.at[zz % 2, x, zz // 2, :, :, high],
            WD.at[zz % 2, x, zz // 2, :, :, high_r],
        ],
        [r["SB1"], r["SB2"]],
    )
    ff_ra2.start()
    ff_rb2.start()
    q_ra.wait()
    q_rb.wait()
    v_z.wait()
    for i in range(4):
        add_low([DWQ.at[zl, i, zh, :, low]], [r["QA1"].at[:, i]])
        add_low([DWQ.at[i // 2, x, i % 2, :, high]], [r["QB1"].at[:, i // 2, i % 2]])
    VE2 = r["VE2"]
    VE2[...] = VP[...] + r["V1"][0] + r["V1"][1] + r["V1"][2]
    q_ra2 = Scatter(comm, "x", lambda xx: [DWQ.at[zl, xx, zh, :, low]], [r["QA2"]])
    q_rb2 = Scatter(comm, "z", lambda zz: [DWQ.at[zz % 2, x, zz // 2, :, high]], [r["QB2"]])
    v_x = Scatter(comm, "x", lambda xx: [VE2], [r["V2"]])
    q_ra2.start()
    q_rb2.start()
    v_x.start()
    ff_ra2.wait()
    ff_rb2.wait()
    add_low([W1.at[zl, x, zh, :, :, low], WD.at[zl, x, zh, :, :, low_r]], [r["SA1"], r["SA2"]])
    add_low([W1.at[zl, x, zh, :, :, high], WD.at[zl, x, zh, :, :, high_r]], [r["SB1"], r["SB2"]])
    ff_ry = Scatter(
        comm, "y", lambda yy: [W1.at[zl, x, zh, yy], WD.at[zl, x, zh, yy]], [r["SY1"], r["SY2"]]
    )
    ff_ry.start()

    for k in range(3):
        comm.recv(YR.at[k], base_y + k)
    zri = comm.take()
    ZS, ZR = r["ZS"], r["ZR"]

    def summed(hh):
        total = cast_up(T5[y, hh, c])
        for k in range(3):
            total += cast_up(YR[k, hh])
        return total

    ZS[...] = summed(1 - zh).astype(BF)
    comm.send(ZS, ZR, zri, other)

    def finish(hh, grad):
        raw = cast_up(TK[hh, c])
        scale = rms_scale(raw)
        gained = grad * first_gain
        mean = jnp.mean(raw * gained, axis=-1, keepdims=True)
        r["din"][hh] = r["din"][hh] + scale * gained - raw * (scale * scale * scale * mean)

    finish(zh, summed(zh))

    ff_ry.wait()
    total = cast_up(W1[zl, x, zh, y])
    for k in range(3):
        total += cast_up(r["SY1"][k])
    asm[:, 512:1024] = total
    q_ra2.wait()
    q_rb2.wait()
    v_x.wait()
    total = cast_up(WD[zl, x, zh, y])
    for k in range(3):
        total += cast_up(r["SY2"][k])
    r["WDG"][...] = total
    home = (2 * c + zh, y // 2, y % 2)
    own_home = (home[0] == y) & (home[1] == zh) & (home[2] == c)
    dwi = comm.take()
    comm.send_or_keep(
        r["WDG"], r["dwd_in"], dwi, dev(x, home[0], home[1] * 2 + zl, home[2]), dwi, own_home
    )
    for cols, buf in ((low, r["QA2"]), (high, r["QB2"])):
        total = cast_up(DWQ[zl, x, zh, :, cols])
        for k in range(3):
            total += cast_up(buf[k])
        asm[:, cols] = total
    sums = unfold_rows(VE2[...] + r["V2"][0] + r["V2"][1] + r["V2"][2])
    W2R = r["W2R"]
    base_h = comm.take(8)
    base_hr = comm.take(8)
    mine = c * 4 + y
    for j in range(8):
        wst[j, 0:6, :] = asm[6 * j : 6 * j + 6, :]
        wst[j, 6:8, :] = sums[0:2]
        ys, hs, cs = 2 * zh + j // 4, (j // 2) % 2, j % 2
        own = (ys == y) & (hs == zh) & (cs == c)
        cp = comm.copy(wst.at[j], W2R.at[mine], base_h + j, dev(x, ys, hs * 2 + zl, cs), base_hr + mine)
        keep = pltpu.make_async_copy(wst.at[j], W2R.at[mine], comm.rs.at[base_hr + mine])
        pl.when(own)(keep.start)
        pl.when(jnp.logical_not(own))(cp.start)
        comm.pending.append((cp, own))
    comm.recv(ZR, zri)
    finish(1 - zh, cast_up(ZR[...]))
    for d in range(8):
        comm.recv(W2R.at[d], base_hr + d)
    for name in ("dwq", "dwk", "dwv"):
        r[name][...] = jnp.zeros((6, D), F32)
    rows_sum = jnp.zeros((2, 1024), F32)
    for cc in range(2):
        for yy in range(4):
            d, first = cc * 4 + yy, 64 * first_head(cc * 4 + yy)
            for i, name in enumerate(("dwq", "dwk", "dwv")):
                r[name][:, first : first + 128] += W2R[d, 0:6, 128 * i : 128 * i + 128]
            for i, name in enumerate(("dwg", "dwu")):
                for k in range(2):
                    tile = 2 * (2 * yy + k) + cc
                    at = 512 + 256 * i + 128 * k
                    r[name][:, 128 * tile : 128 * tile + 128] = W2R[d, 0:6, at : at + 128]
            if yy < 3:
                at = (cc * 3 + yy) * 128
                r["dwo"][:, at : at + 128] = W2R[d, 0:6, 384:512]
            rows_sum += W2R[d, 6:8, :]
    table = jnp.concatenate([rows_sum[0:1, 768:1024], rows_sum[1:2, 768:1024], rows_sum[0:1, 0:512]], axis=1)
    gains = jnp.broadcast_to(jnp.concatenate([rows_sum, jnp.zeros((6, 1024), F32)], axis=0), (8, 1024))
    gains = pltpu.roll(gains, 1024 - 6 * flat, 1)[0:2, 0:128]
    table = pltpu.roll(jnp.broadcast_to(table, (8, 1024)), 1024 - 3 * flat, 1)[0:1, 0:128]
    r["dvec"][...] = jnp.concatenate([gains, table, jnp.zeros((5, 128), F32)], axis=0)
    comm.recv(r["dwd_in"], dwi)
    names = ("din", "dwq", "dwk", "dwv", "dwo", "dwg", "dwu", "dwd", "dvec")
    for i, name in enumerate(names):
        src = r["dwd_in"] if name == "dwd" else r[name]
        stores.append(pltpu.make_async_copy(src, r["h_" + name], local_sem.at[11 + i]))
        stores[-1].start()
    for k in range(4):
        yy = (y + (2, 1, 3, 0)[k]) % 4
        comm.copy(T5.at[yy, :, 1 - c], sib_at(yy), base_s + k, sib).wait_send()
    comm.drain()
    for store in stores:
        store.wait()


INPUTS = [
    ("lens", "s"), ("g1", "s"), ("g2", "s"), ("bt", "s"),
    ("tok", "a"), ("cot", "a"), ("h_wq", "a"), ("h_wk", "a"), ("h_wv", "a"), ("h_wo", "a"),
    ("h_wg", "a"), ("h_wu", "a"), ("h_wd", "a"),
]
SCRATCH = [
    ("W1", ((2, 4, 2, 4, 48, 512), BF)),
    ("WD", ((2, 4, 2, 4, 16, 768), BF)),
    ("WQ", ((2, 4, 2, 48, 512), BF)),
    ("G5", ((2, 4, 2, 8, 256), F32)),
    ("T5", ((4, 2, 2, 128, 768), BF)),
    ("TK", ((2, 2, 128, 768), BF)),
    ("CT", ((2, 2, 128, 768), BF)),
    ("wst", ((8, 8, 1024), F32)),
    ("w0", ((8, 8, 1024), F32)),
    ("asm", ((48, 1024), F32)),
    ("wdst", ((16, 768), BF)),
    ("GS", ((8, 1024), F32)),
    ("OH", ((128, 1024), BF)),
    ("BO", ((8, 1024), F32)),
    ("BT", ((2, 256, 512), F32)),
    ("QA", ((2, 2048, 128), BF)),
    ("KT", ((2, 128, 2048), BF)),
    ("KN", ((2048, 128), BF)),
    ("VN", ((2048, 256), BF)),
    ("VT", ((128, 2048), BF)),
    ("SC", ((256, 2304), F32)),
    ("S2", ((256, 2304), F32)),
    ("PB", ((3, 1024, 2304), BF)),
    ("ON", ((2048, 128), BF)),
    ("LI", ((1024, 128), F32)),
    ("GL", ((1024, 128), BF)),
    ("DL", ((1024, 128), F32)),
    ("A", ((2, 256, 512), BF)),
    ("WOF", ((4, 2, 48, 768), BF)),
    ("POS", ((2, 2, 128, 768), BF)),
    ("POR", ((2, 2, 128, 768), BF)),
    ("N2", ((256, 1536), BF)),
    ("N2T", ((768, 512), BF)),
    ("HIDT", ((1024, 512), BF)),
    ("GU", ((2, 2, 128, 2048), BF)),
    ("PNR", ((2, 2, 128, 768), BF)),
    ("PYS", ((2, 128, 768), BF)),
    ("PYR", ((2, 128, 768), BF)),
    ("ML", ((2, 2, 128, 768), BF)),
    ("DOS", ((4, 2, 256, 128), BF)),
    ("DO", ((2048, 128), BF)),
    ("RA1", ((3, 4, 4, 48, 256), BF)),
    ("RA2", ((3, 4, 4, 16, 256), BF)),
    ("RB1", ((3, 2, 2, 4, 48, 256), BF)),
    ("RB2", ((3, 2, 2, 4, 16, 512), BF)),
    ("SA1", ((3, 4, 48, 256), BF)),
    ("SA2", ((3, 4, 16, 256), BF)),
    ("SB1", ((3, 4, 48, 256), BF)),
    ("SB2", ((3, 4, 16, 512), BF)),
    ("SY1", ((3, 48, 512), BF)),
    ("SY2", ((3, 16, 768), BF)),
    ("WOR", ((4, 2, 4, 2, 48, 128), BF)),
    ("HX", ((256, 2304), BF)),
    ("YR", ((3, 2, 128, 768), BF)),
    ("ZS", ((128, 768), BF)),
    ("ZR", ((128, 768), BF)),
    ("DWQ", ((2, 4, 2, 48, 512), BF)),
    ("QA1", ((3, 4, 48, 256), BF)),
    ("QA2", ((3, 48, 256), BF)),
    ("QB1", ((3, 2, 2, 48, 256), BF)),
    ("QB2", ((3, 48, 256), BF)),
    ("VEC", ((8, 1024), F32)),
    ("V1", ((3, 8, 256), F32)),
    ("V2", ((3, 8, 256), F32)),
    ("VE2", ((8, 256), F32)),
    ("VP", ((8, 256), F32)),
    ("W2R", ((8, 8, 1024), F32)),
    ("WDG", ((16, 768), F32)),
    ("dwd_in", ((16, 768), F32)),
    ("out", ((2, 128, 768), BF)),
    ("din", ((2, 128, 768), F32)),
    ("dwq", ((6, 768), F32)),
    ("dwk", ((6, 768), F32)),
    ("dwv", ((6, 768), F32)),
    ("dwo", ((6, 768), F32)),
    ("dwg", ((6, 2048), F32)),
    ("dwu", ((6, 2048), F32)),
    ("dvec", ((8, 128), F32)),
    ("wq", ((6, 768), F32)),
    ("wk", ((6, 768), F32)),
    ("wv", ((6, 768), F32)),
    ("wo", ((6, 768), F32)),
    ("wg", ((6, 2048), F32)),
    ("wu", ((6, 2048), F32)),
    ("wd", ((16, 768), F32)),
    ("free_sem", 0),
    ("local_sem", 32),
    ("send_sem", None),
    ("recv_sem", None),
]


OUTPUTS = [
    ("h_out", ((2, 128, 768), BF)),
    ("h_din", ((2, 128, 768), F32)),
    ("h_dwq", ((6, 768), F32)),
    ("h_dwk", ((6, 768), F32)),
    ("h_dwv", ((6, 768), F32)),
    ("h_dwo", ((6, 768), F32)),
    ("h_dwg", ((6, 2048), F32)),
    ("h_dwu", ((6, 2048), F32)),
    ("h_dwd", ((16, 768), F32)),
    ("h_dvec", ((8, 128), F32)),
]


def call_mega(*args):
    spec = {"s": pl.BlockSpec(memory_space=pltpu.SMEM), "a": pl.BlockSpec(memory_space=pl.ANY)}
    outs = OUTPUTS
    scratch = []
    for _, s in SCRATCH:
        if s == 0:
            scratch.append(pltpu.SemaphoreType.REGULAR)
        elif s is None or isinstance(s, int):
            scratch.append(pltpu.SemaphoreType.DMA((s or NSEM,)))
        else:
            scratch.append(pltpu.VMEM(s[0], s[1]))
    return pl.pallas_call(
        mega,
        out_shape=[jax.ShapeDtypeStruct(s[0], s[1]) for _, s in outs],
        in_specs=[spec[k] for _, k in INPUTS],
        out_specs=[pl.BlockSpec(memory_space=pl.ANY) for _ in outs],
        scratch_shapes=scratch,
        name="layer",
        compiler_params=pltpu.CompilerParams(
            collective_id=0, has_side_effects=True, vmem_limit_bytes=62 * 2**20
        ),
    )(*args)


def per_device(
    tokens,
    lengths,
    cotangent,
    query_weight,
    key_weight,
    value_weight,
    out_weight,
    gate_weight,
    up_weight,
    down_weight,
    first_gain,
    second_gain,
    bias_table,
):
    done = call_mega(
        lengths,
        first_gain,
        second_gain,
        bias_table,
        tokens,
        cotangent,
        query_weight,
        key_weight,
        value_weight,
        out_weight,
        gate_weight,
        up_weight,
        down_weight,
    )
    return hand_out(*done)


def hand_out_kernel(*refs):
    n = len(OUTPUTS)
    vectors, ins, outs, held, sem = refs[0], refs[1:n], refs[n : 2 * n + 2], refs[2 * n + 2 : -1], refs[-1]
    loads = [pltpu.make_async_copy(a, b, sem.at[i]) for i, (a, b) in enumerate(zip(ins, held))]
    copies = [pltpu.make_async_copy(a, b, sem.at[i]) for i, (a, b) in enumerate(zip(held, outs))]
    for load in loads:
        load.start()
    for load, copy in zip(loads, copies):
        load.wait()
        copy.start()
    for row, (ref, width) in enumerate(zip(outs[n - 1 :], (6, 6, 3))):
        for i in range(width):
            ref[i] = vectors[row, i]
    for copy in copies:
        copy.wait()


def hand_out(*done):
    shapes = [jax.ShapeDtypeStruct(s[0], s[1]) for _, s in OUTPUTS[:-1]]
    shapes += [jax.ShapeDtypeStruct((n,), F32) for n in (6, 6, 3)]
    smem, hbm = pl.BlockSpec(memory_space=pltpu.SMEM), pl.BlockSpec(memory_space=pl.ANY)
    n = len(done) - 1
    return tuple(
        pl.pallas_call(
            hand_out_kernel,
            out_shape=shapes,
            in_specs=[smem] + [hbm] * n,
            out_specs=[hbm] * n + [smem] * 3,
            scratch_shapes=[pltpu.VMEM(s[0], s[1]) for _, s in OUTPUTS[:-1]]
            + [pltpu.SemaphoreType.DMA((n,))],
            name="hand_out",
        )(done[-1], *done[:-1])
    )


def solution(mesh):
    tokens = P("rows", "seq", None)
    matrix = P(("rows", "seq"), None)
    vector = P(("rows", "seq"))
    return jax.shard_map(
        per_device,
        mesh=mesh,
        in_specs=(tokens, P("rows"), tokens, *([matrix] * 7), *([vector] * 3)),
        out_specs=(tokens, tokens, *([matrix] * 7), *([vector] * 3)),
        check_vma=False,
    )
```

```python
import jax
import jax.numpy as jnp
from jax import lax
from jax.experimental import pallas as pl
from jax.experimental.pallas import tpu as pltpu
from jax.sharding import PartitionSpec as P

MESH = pl.DeviceIdType.MESH
BF = jnp.bfloat16
F32 = jnp.float32
D = 768
SEQ = 2048
EPSILON = 1e-06
NEGATIVE = -1e30
LIMITS = (1, 2, 3, 4, 5, 6, 7, 8, 12, 16, 23, 32, 46, 64, 91)
NSEM = 240
BQ = 256
STEPS = 12


def dev(x, y, z, c):
    return ((z % 2) * 4 + x, (y * 2 + z // 2) * 2 + c)


def first_head(t):
    return (3 * t) // 2


def iota(shape, dim):
    return lax.broadcasted_iota(jnp.int32, shape, dim)


def dot(a, b):
    return jnp.dot(a, b, preferred_element_type=F32)


def dot_nt(a, b):
    return lax.dot_general(a, b, (((1,), (1,)), ((), ())), preferred_element_type=F32)


class Comm:
    def __init__(self, x, y, z, c, send_sem, recv_sem):
        self.x, self.y, self.z, self.c = x, y, z, c
        self.ss, self.rs = send_sem, recv_sem
        self.next = 0
        self.pending = []

    def take(self, n=1):
        at = self.next
        self.next += n
        assert self.next <= NSEM
        return at

    def peer(self, axis, offset):
        x, y, z, c = self.x, self.y, self.z, self.c
        if axis == "x":
            return dev((x + offset) % 4, y, z, c)
        if axis == "y":
            return dev(x, (y + offset) % 4, z, c)
        if axis == "z":
            return dev(x, y, (z + offset) % 4, c)
        return dev(x, y, z, 1 - c)

    def place(self, axis, offset):
        at = {"x": self.x, "y": self.y, "z": self.z}[axis]
        return (at + offset) % 4

    def copy(self, src, dst, i, to, j=None):
        return pltpu.make_async_remote_copy(
            src_ref=src,
            dst_ref=dst,
            send_sem=self.ss.at[i],
            recv_sem=self.rs.at[i if j is None else j],
            device_id=to,
            device_id_type=MESH,
        )

    def send(self, src, dst, i, to):
        cp = self.copy(src, dst, i, to)
        cp.start()
        self.pending.append(cp)

    def recv(self, dst, i):
        self.copy(dst, dst, i, self.peer("c", 0)).wait_recv()

    def send_or_keep(self, src, dst, i, to, j, own):
        cp = self.copy(src, dst, i, to, j)
        keep = pltpu.make_async_copy(src, dst, self.rs.at[j])

        @pl.when(own)
        def _():
            keep.start()

        @pl.when(jnp.logical_not(own))
        def _():
            cp.start()

        self.pending.append((cp, own))

    def drain(self):
        for cp in self.pending:
            if isinstance(cp, tuple):
                cp, own = cp

                @pl.when(jnp.logical_not(own))
                def _():
                    cp.wait_send()
            else:
                cp.wait_send()
        self.pending = []


class Direct:
    def __init__(self, comm, axis, views):
        self.comm, self.axis, self.views = comm, axis, views
        self.count = len(views(comm.place(axis, 0)))
        self.base = comm.take(3 * self.count)

    def start(self):
        for k, off in enumerate((1, 3, 2)):
            for n, ref in enumerate(self.views(self.comm.place(self.axis, 0))):
                self.comm.send(ref, ref, self.base + k * self.count + n, self.comm.peer(self.axis, off))

    def wait(self):
        for k, off in enumerate((1, 3, 2)):
            for n, ref in enumerate(self.views(self.comm.place(self.axis, -off + 4))):
                self.comm.recv(ref, self.base + k * self.count + n)


class Ring:
    def __init__(self, comm, axis, views, halves):
        self.comm, self.axis, self.views, self.halves = comm, axis, views, halves
        self.count = len(views(comm.place(axis, 0)))
        self.base = comm.take(4 * self.count)

    def start(self, source=None):
        own = self.views(self.comm.place(self.axis, 0))
        for n, ref in enumerate(own):
            src = ref if source is None else source[n]
            for k, off in enumerate((1, 3)):
                self.comm.send(src, ref, self.base + k * self.count + n, self.comm.peer(self.axis, off))

    def forward(self):
        for k, off in enumerate((1, 3)):
            came = self.comm.place(self.axis, -off + 4)
            for n, ref in enumerate(self.views(came)):
                self.comm.recv(ref, self.base + k * self.count + n)
            for n, ref in enumerate(self.halves(came, k)):
                self.comm.send(ref, ref, self.base + (2 + k) * self.count + n, self.comm.peer(self.axis, off))

    def wait(self):
        far = self.comm.place(self.axis, 2)
        for k in range(2):
            for n, ref in enumerate(self.halves(far, k)):
                self.comm.recv(ref, self.base + (2 + k) * self.count + n)


class Scatter:
    def __init__(self, comm, axis, views, bufs):
        self.comm, self.axis, self.views, self.bufs = comm, axis, views, bufs
        self.base = comm.take(3 * len(bufs))

    def start(self):
        for k, off in enumerate((1, 3, 2)):
            refs = self.views(self.comm.place(self.axis, off))
            for n, ref in enumerate(refs):
                self.comm.send(
                    ref, self.bufs[n].at[k], self.base + k * len(refs) + n, self.comm.peer(self.axis, off)
                )

    def wait(self):
        for k in range(3):
            for n, buf in enumerate(self.bufs):
                self.comm.recv(buf.at[k], self.base + k * len(self.bufs) + n)


def bucket_ids(offsets):
    distance = jnp.abs(offsets)
    bucket_sum = jnp.where(offsets > 0, 16, 0)
    for threshold in LIMITS:
        bucket_sum = bucket_sum + jnp.where(distance >= threshold, 1, 0)
    return bucket_sum


def fold_rows(two):
    return jnp.concatenate([two[k : k + 1, 256 * i : 256 * i + 256] for k in range(2) for i in range(4)], axis=0)


def unfold_rows(eight):
    rows = [jnp.concatenate([eight[4 * k + i : 4 * k + i + 1] for i in range(4)], axis=1) for k in range(2)]
    return jnp.concatenate(rows, axis=0)


def rms_scale(values):
    return lax.rsqrt(jnp.mean(values * values, axis=-1, keepdims=True) + EPSILON)


def greet(comm):
    x, y, z, c = comm.x, comm.y, comm.z, comm.c
    zl, zh = z % 2, z // 2
    barrier = pltpu.get_barrier_semaphore()
    count = 0
    peers = []
    for dy in range(4):
        for dh in range(2):
            for dc in range(2):
                if dy or dh or dc:
                    peers.append(dev(x, (y + dy) % 4, ((zh + dh) % 2) * 2 + zl, (c + dc) % 2))
    for off in (1, 2, 3):
        peers.append(comm.peer("x", off))
    for off in (1, 3):
        peers.append(comm.peer("z", off))
    for peer in peers:
        pl.semaphore_signal(barrier, inc=1, device_id=peer, device_id_type=MESH)
        count += 1
    return barrier, count


def cast_up(v):
    return v.astype(F32)


def head_bias(tables, o):
    return tables[o : o + 1, 0:1], tables[o : o + 1, 1023:1024]


def mega(*refs):
    names = [n for n, _ in INPUTS] + [n for n, _ in OUTPUTS] + [n for n, _ in SCRATCH]
    r = dict(zip(names, refs))
    rows, seq = lax.axis_index("rows"), lax.axis_index("seq")
    x, y, zl, zh, c = rows % 4, seq // 4, rows // 4, (seq // 2) % 2, seq % 2
    z = zh * 2 + zl
    flat = rows * 16 + seq
    t = c * 4 + y
    comm = Comm(x, y, z, c, r["send_sem"], r["recv_sem"])
    local_sem = r["local_sem"]
    TK, CT, T5, tok, cot = r["TK"], r["CT"], r["T5"], r["tok"], r["cot"]
    loads = []
    for i, name in enumerate(("wq", "wk", "wv", "wo", "wg", "wu", "wd")):
        loads.append(pltpu.make_async_copy(r["h_" + name], r[name], local_sem.at[i]))
        loads[-1].start()
    keep_tokens = pltpu.make_async_copy(tok.at[zh], T5.at[y, zh, c], local_sem.at[7])
    keep_tk = pltpu.make_async_copy(tok, TK.at[:, c], local_sem.at[8])
    keep_ct = pltpu.make_async_copy(cot, CT.at[:, c], local_sem.at[9])
    keep_tokens.start()
    keep_tk.start()
    keep_ct.start()
    barrier, count = greet(comm)

    lanes = iota((1, 1024), 1)
    first_row = jnp.zeros((1, 1024), F32)
    second_row = jnp.zeros((1, 1024), F32)
    for i in range(6):
        first_row += jnp.where(lanes == 6 * flat + i, r["g1"][i], 0.0)
        second_row += jnp.where(lanes == 6 * flat + i, r["g2"][i], 0.0)
    for i in range(3):
        at = 768 + 3 * flat + i
        first_row += jnp.where(lanes == at, r["bt"][i], 0.0)
        second_row += jnp.where((lanes >= 768) & (lanes == at - 256), r["bt"][i], 0.0)
    first_row = cast_up(first_row.astype(BF))
    second_row = cast_up(second_row.astype(BF))
    wst, w0 = r["wst"], r["w0"]
    for load in loads:
        load.wait()
    for cc in range(2):
        for yy in range(4):
            d, h0 = cc * 4 + yy, first_head(cc * 4 + yy)
            for i, name in enumerate(("wq", "wk", "wv")):
                wst[d, 0:6, 128 * i : 128 * (i + 1)] = r[name][:, 64 * h0 : 64 * h0 + 128]
            for i, name in enumerate(("wg", "wu")):
                for k in range(2):
                    tile = 2 * (2 * yy + k) + cc
                    at = 512 + 256 * i + 128 * k
                    wst[d, 0:6, at : at + 128] = r[name][:, 128 * tile : 128 * tile + 128]
            if yy < 3:
                at = (cc * 3 + yy) * 128
                wst[d, 0:6, 384:512] = r["wo"][:, at : at + 128]
            else:
                wst[d, 0:6, 384:512] = jnp.zeros((6, 128), F32)
            wst[d, 6:7, :] = first_row
            wst[d, 7:8, :] = second_row
    r["wdst"][...] = r["wd"][...].astype(BF)

    pl.semaphore_wait(barrier, count)

    W1, WD, WQ, G5 = r["W1"], r["WD"], r["WQ"], r["G5"]
    slot = (y % 2) * 4 + zh * 2 + c
    base0 = comm.take(8)
    baser = comm.take(8)
    for cc in range(2):
        for yy in range(4):
            to = dev(x, yy, (y // 2) * 2 + zl, cc)
            own = (y == yy) & (c == cc) & (zh == y // 2)
            cp = comm.copy(wst.at[cc * 4 + yy], w0.at[slot], base0 + cc * 4 + yy, to, baser + slot)
            keep = pltpu.make_async_copy(wst.at[cc * 4 + yy], w0.at[slot], comm.rs.at[baser + slot])
            pl.when(own)(keep.start)
            pl.when(jnp.logical_not(own))(cp.start)
            comm.pending.append((cp, own))
    wd_to = (zh * 2 + c, y % 2, y // 2)
    own_wd = (wd_to[0] == y) & (wd_to[1] == zh) & (wd_to[2] == c)
    wdi = comm.take()
    wd_region = WD.at[zl, x, wd_to[1], wd_to[0]]
    comm.send_or_keep(
        r["wdst"], wd_region, wdi, dev(x, wd_to[0], wd_to[1] * 2 + zl, wd_to[2]), wdi, own_wd
    )

    other = comm.peer("z", 2)
    zi = comm.take()
    comm.send(tok.at[1 - zh], T5.at[y, zh, c], zi, other)
    own_tokens = Ring(
        comm,
        "y",
        lambda yy: [T5.at[yy, zh, c]],
        lambda yy, k: [T5.at[yy, zh, c, pl.ds(64 * k, 64)]],
    )
    own_tokens.start(source=[tok.at[zh]])
    pair = comm.take(2)

    for j in range(8):
        comm.recv(w0.at[j], baser + j)
    asm = r["asm"]
    gsum = jnp.zeros((2, 1024), F32)
    for j in range(8):
        asm[6 * j : 6 * j + 6, :] = w0[j, 0:6, :]
        gsum += w0[j, 6:8, :]
    WQ[zl, x, zh] = asm[:, 0:512].astype(BF)
    G5[zl, x, zh] = fold_rows(gsum)
    W1[zl, x, zh, y] = asm[:, 512:1024].astype(BF)
    qkv_a1 = Direct(comm, "x", lambda xx: [WQ.at[zl, xx, zh, :, pl.ds(0, 256)], G5.at[zl, xx, zh]])
    qkv_b1 = Direct(comm, "z", lambda zz: [WQ.at[zz % 2, x, zz // 2, :, pl.ds(256, 256)]])
    qkv_a1.start()
    qkv_b1.start()
    comm.recv(WD.at[zl, x, zh, y], wdi)
    ff_y = Direct(comm, "y", lambda yy: [W1.at[zl, x, zh, yy], WD.at[zl, x, zh, yy]])
    ff_y.start()

    comm.recv(T5.at[y, 1 - zh, c], zi)
    far_tokens = Ring(
        comm,
        "y",
        lambda yy: [T5.at[yy, 1 - zh, c]],
        lambda yy, k: [T5.at[yy, 1 - zh, c, pl.ds(64 * k, 64)]],
    )
    far_tokens.start()
    keep_tokens.wait()
    sib = comm.peer("c", 0)
    across = comm.take(4)

    def cross(k):
        yy = (y + (0, 1, 3, 2)[k]) % 4
        comm.send(T5.at[yy, :, c], T5.at[yy, :, c], across + k, sib)

    def crossed(k):
        yy = (y + (0, 1, 3, 2)[k]) % 4
        comm.recv(T5.at[yy, :, 1 - c], across + k)

    cross(0)
    qkv_a1.wait()
    qkv_b1.wait()
    qkv_a2 = Direct(
        comm,
        "z",
        lambda zz: [WQ.at[zz % 2, :, zz // 2, :, pl.ds(0, 256)], G5.at[zz % 2, :, zz // 2]],
    )
    qkv_b2 = Direct(comm, "x", lambda xx: [WQ.at[:, xx, :, :, pl.ds(256, 256)]])
    qkv_a2.start()
    qkv_b2.start()
    own_tokens.forward()
    ff_y.wait()
    low, high = pl.ds(0, 256), pl.ds(256, 256)
    low_d, high_d = pl.ds(0, 256), pl.ds(256, 512)
    ff_a1 = Direct(
        comm, "x", lambda xx: [W1.at[zl, xx, zh, :, :, low], WD.at[zl, xx, zh, :, :, low_d]]
    )
    ff_b1 = Direct(
        comm,
        "z",
        lambda zz: [
            W1.at[zz % 2, x, zz // 2, :, :, high],
            WD.at[zz % 2, x, zz // 2, :, :, high_d],
        ],
    )
    ff_a1.start()
    ff_b1.start()
    far_tokens.forward()
    cross(1)
    cross(2)
    keep_tk.wait()
    keep_ct.wait()
    comm.send(TK.at[:, c], TK.at[:, c], pair, sib)
    comm.send(CT.at[:, c], CT.at[:, c], pair + 1, sib)

    qkv_a2.wait()
    qkv_b2.wait()
    WOF = r["WOF"]
    base_w = comm.take(8)
    base_wr = comm.take(8)
    for cc in range(2):
        for yy in range(4):
            src = WQ.at[cc, :, :, :, pl.ds(384, 128)]
            dst = WOF.at[:, :, :, pl.ds(pl.multiple_of((c * 3 + y % 3) * 128, 128), 128)]
            cp = comm.copy(src, dst, base_w + cc * 4 + yy, dev(x, yy, z, cc), base_wr + c * 4 + y)
            keep = pltpu.make_async_copy(src, dst, comm.rs.at[base_wr + c * 4 + y])
            here = (yy == y) & (cc == c)
            pl.when(here & (y < 3))(keep.start)
            pl.when(jnp.logical_not(here) & (y < 3))(cp.start)
            comm.pending.append((cp, here | (y == 3)))
    total = jnp.zeros((8, 256), F32)
    for a in range(2):
        for b in range(4):
            for e in range(2):
                total += G5[a, b, e]
    total = unfold_rows(total)
    r["GS"][0:2, :] = total
    h0 = first_head(t)
    table_row = jnp.concatenate([total[0:1, 768:1024], total[1:2, 768:896]], axis=1)
    table_row = jnp.broadcast_to(table_row, (8, 384))
    table_row = pltpu.roll(table_row, 384 - 32 * h0, 1)[:, 0:128]
    lane = iota((8, 128), 1)
    sub = iota((8, 128), 0)
    table_two = jnp.where((lane // 32) == sub, table_row, 0.0).astype(BF)
    r["OH"][...] = jnp.where(
        bucket_ids(iota((128, 1024), 1) - 512) == iota((128, 1024), 0) % 32, 1.0, 0.0
    ).astype(BF)
    by_offset = dot(table_two, r["OH"][...])
    r["BO"][...] = by_offset
    for h in range(2):
        for k in range(4):
            rolled = pltpu.roll(
                jnp.broadcast_to(by_offset[h : h + 1, :], (64, 1024)), 640 + 64 * k, 1, stride=1, stride_axis=0
            )
            r["BT"][h, 64 * k : 64 * k + 64, :] = rolled[:, 0:512]

    ff_a1.wait()
    ff_b1.wait()
    ff_a2 = Ring(
        comm,
        "z",
        lambda zz: [
            W1.at[zz % 2, :, zz // 2, :, :, low],
            WD.at[zz % 2, :, zz // 2, :, :, low_d],
        ],
        lambda zz, k: [
            W1.at[zz % 2, pl.ds(2 * k, 2), zz // 2, :, :, low],
            WD.at[zz % 2, pl.ds(2 * k, 2), zz // 2, :, :, low_d],
        ],
    )
    ff_b2 = Ring(
        comm,
        "x",
        lambda xx: [W1.at[:, xx, :, :, :, high], WD.at[:, xx, :, :, :, high_d]],
        lambda xx, k: [W1.at[k, xx, :, :, :, high], WD.at[k, xx, :, :, :, high_d]],
    )
    ff_a2.start()
    ff_b2.start()

    QA, KT, KN, VN, VT = r["QA"], r["KT"], r["KN"], r["VN"], r["VT"]
    row_len = r["lens"][zh]

    def project(i, carry):
        raw = cast_up(T5[i // 2, i % 2].reshape(256, D))
        normed = (raw * rms_scale(raw) * r["GS"][0:1, 0:768]).astype(BF)
        res = dot(normed, WQ[:, :, :, :, 0:384].reshape(D, 384))
        q, k_, v = res[:, 0:128], res[:, 128:256], res[:, 256:384]
        at = pl.ds(pl.multiple_of(i * 256, 256), 256)
        KN[at, :] = k_.astype(BF)
        VN[at, :] = jnp.concatenate([v, jnp.ones((256, 128), F32)], axis=1).astype(BF)
        VT[:, at] = v.T.astype(BF)
        kt = k_.T
        lane = iota((256, 128), 1)
        sub = iota((128, 256), 0)
        key_at = i * 256 + iota((128, 256), 1)
        for h in range(2):
            base = 64 * (1 - h)
            hot = jnp.where((lane == base + i) | (lane == base + 8), 1.0, 0.0)
            QA[h, at, :] = jnp.where(lane // 64 == h, q, hot).astype(BF)
            left, right = head_bias(r["BO"][...], h)
            start = 256 * (sub - base)
            extra = jnp.where(key_at < start - 128, left, 0.0) + jnp.where(
                key_at >= start + 384, right, 0.0
            )
            masked = jnp.where(key_at >= row_len, NEGATIVE, 0.0)
            extra = jnp.where(sub - base < 8, extra, jnp.where(sub - base == 8, masked, 0.0))
            KT[h, :, at] = jnp.where(sub // 64 == h, kt, extra).astype(BF)
        return carry

    for k in range(4):
        if k == 3:
            own_tokens.wait()
            far_tokens.wait()
            cross(3)
        crossed(k)
        first = 2 * ((y + (0, 1, 3, 2)[k]) % 4)
        lax.fori_loop(first, first + 2, project, 0)
    r["ON"][...] = jnp.zeros((SEQ, 128), BF)
    r["LI"][...] = jnp.zeros((1024, 128), F32)
    r["PB"][:, :, 0:128] = jnp.zeros((3, 1024, 128), BF)
    r["PB"][:, :, 2176:2304] = jnp.zeros((3, 1024, 128), BF)

    SC, PB, BT, ON, LI = r["SC"], r["PB"], r["BT"], r["ON"], r["LI"]

    def unit_of(step):
        ui = step // 4
        u = jnp.where(ui == 0, 1, jnp.where(ui == 1, 0, 2))
        number = 3 * t + u
        head = number // 2 - h0
        start = (number % 2) * 1024 + (step % 4) * 256
        return head, pl.multiple_of(start, 256)

    S2 = r["S2"]

    def score_part(step, buf, j, top):
        head, q0 = unit_of(step)
        s = dot(QA[head, pl.ds(q0, BQ), :], KT[head, :, 256 * j : 256 * j + 256])
        buf[:, 128 + 256 * j : 384 + 256 * j] = s
        most = jnp.maximum(s[:, 0:128], s[:, 128:256])
        return most if top is None else jnp.maximum(top, most)

    def score_end(step, buf, top):
        head, q0 = unit_of(step)
        buf[:, pl.ds(q0, 512)] = buf[:, pl.ds(q0, 512)] + BT[head]
        return jnp.max(top, axis=1, keepdims=True)

    def block_of(step):
        return pl.ds(pl.multiple_of((step % 4) * 256, 256), BQ)

    def prob_part(step, buf, j, top):
        for k in (2 * j + 1, 2 * j + 2):
            p = jnp.exp(buf[:, 128 * k : 128 * k + 128] - top)
            PB[step // 4, block_of(step), 128 * k : 128 * k + 128] = p.astype(BF)

    def mix(step):
        head, q0 = unit_of(step)
        mixed = dot(PB[step // 4, block_of(step), 128:2176], VN[...])
        inv = 1.0 / mixed[:, 128:129]
        lane = iota((BQ, 128), 1)
        LI[block_of(step), :] = jnp.where(lane == step // 4, inv, LI[block_of(step), :])
        mixed = mixed[:, 0:128] * inv
        ON[pl.ds(q0, BQ), :] = jnp.where(lane // 64 == head, mixed, cast_up(ON[pl.ds(q0, BQ), :])).astype(BF)

    def first_scores(step):
        top = None
        for j in range(8):
            top = score_part(step, SC, j, top)
        return score_end(step, SC, top)

    def attend(pair, top_a):
        one, two = 2 * pair, 2 * pair + 1
        top_b = None
        for j in range(8):
            top_b = score_part(two, S2, j, top_b)
            prob_part(one, SC, j, top_a)
        top_b = score_end(two, S2, top_b)
        mix(one)
        then = jnp.minimum(two + 1, STEPS - 1)
        top_a = None
        for j in range(8):
            prob_part(two, S2, j, top_b)
            top_a = score_part(then, SC, j, top_a)
        top_a = score_end(then, SC, top_a)
        mix(two)
        return top_a

    A = r["A"]
    base_o = comm.take(8)
    base_or = comm.take(8)

    def give(half, n):
        for i in range(4):
            yy, hh = 2 * half + i // 2, i % 2
            src = ON.at[pl.ds(pl.multiple_of(256 * (yy * 2 + hh), 256), 256)]
            dst = A.at[zh, :, pl.ds(pl.multiple_of(128 * y, 128), 128)]
            own = (yy == y) & (hh == zh)
            cp = comm.copy(src, dst, base_o + 4 * n + i, dev(x, yy, hh * 2 + zl, c), base_or + y * 2 + zh)
            keep = pltpu.make_async_copy(src, dst, comm.rs.at[base_or + y * 2 + zh])
            pl.when(own)(keep.start)
            pl.when(jnp.logical_not(own))(cp.start)
            comm.pending.append((cp, own))

    single = (3 * t + 1) % 2
    top_now = lax.fori_loop(0, 2, attend, first_scores(0))
    give(single, 0)
    top_now = lax.fori_loop(2, 4, attend, top_now)
    ff_a2.forward()
    ff_b2.forward()
    lax.fori_loop(4, STEPS // 2, attend, top_now)
    give(1 - single, 1)
    for yy in range(4):
        for hh in range(2):
            comm.recv(A.at[hh, :, pl.ds(128 * yy, 128)], base_or + yy * 2 + hh)
    comm.recv(TK.at[:, 1 - c], pair)
    comm.recv(CT.at[:, 1 - c], pair + 1)

    lane = iota((256, 128), 1)
    for hh in range(2):
        p0, p1, p2, p3 = [cast_up(A[hh, :, 128 * k : 128 * k + 128]) for k in range(4)]
        p1, p2 = pltpu.roll(p1, 64, 1), pltpu.roll(p2, 64, 1)
        A[hh, :, 0:128] = (p0 + jnp.where(lane >= 64, p1, 0.0)).astype(BF)
        A[hh, :, 128:256] = jnp.where(lane < 64, p1, p2).astype(BF)
        A[hh, :, 256:384] = (p3 + jnp.where(lane < 64, p2, 0.0)).astype(BF)
    for cc in range(2):
        for yy in range(3):
            comm.recv(WOF.at[:, :, :, pl.ds(128 * (cc * 3 + yy), 128)], base_wr + cc * 4 + yy)

    POS, POR, N2, N2T = r["POS"], r["POR"], r["N2"], r["N2T"]
    base_p = comm.take(2)
    for hh in range(2):
        term = dot(A[hh, :, 0:384], WOF[...].reshape(384, D))
        POS[hh] = term.astype(BF).reshape(2, 128, D)
        comm.send(POS.at[hh], POR.at[hh], base_p + hh, sib)
    second_gain = r["GS"][1:2, 0:768]
    for hh in range(2):
        comm.recv(POR.at[hh], base_p + hh)
        for k in range(2):
            middle = cast_up(TK[hh, k]) + (cast_up(POS[hh, k]) + cast_up(POR[hh, k]))
            S2[128 * hh : 128 * hh + 128, 768 * k : 768 * k + 768] = middle
            normed = middle * rms_scale(middle) * second_gain
            N2[128 * k : 128 * k + 128, 768 * hh : 768 * hh + 768] = normed.astype(BF)
            at = 256 * hh + 128 * k
            N2T[:, at : at + 128] = normed.T.astype(BF)

    HX, HIDT, GU = r["HX"], r["HIDT"], r["GU"]

    def gated(k, carry):
        gate_w = W1[:, :, :, k, :, 0:256].reshape(D, 256)
        up_w = W1[:, :, :, k, :, 256:512].reshape(D, 256)
        down_w = WD[k // 2, pl.ds((2 * k) % 4, 2)].reshape(256, D)
        for hh in range(2):
            gate = dot(N2[:, 768 * hh : 768 * hh + 768], gate_w)
            up = dot(N2[:, 768 * hh : 768 * hh + 768], up_w)
            back = dot_nt(CT[hh].reshape(256, D), down_w)
            square = gate * gate
            th = jnp.tanh(0.7978845608028654 * (gate + 0.044715 * (square * gate)))
            half = 0.5 * (1.0 + th)
            gelu = gate * half
            slope = half + (0.5 * gate) * (1.0 - th * th) * (
                0.7978845608028654 * (1.0 + 3 * 0.044715 * square)
            )
            hidden = gelu * up
            cols = pl.ds(pl.multiple_of(256 * k, 256), 256)
            HX[:, pl.ds(pl.multiple_of(1024 * hh + 256 * k, 256), 256)] = hidden.astype(BF)
            HIDT[cols, 256 * hh : 256 * hh + 256] = hidden.T.astype(BF)
            both = pl.multiple_of(512 * k, 512)
            GU[hh, :, :, pl.ds(both, 256)] = (back * up * slope).astype(BF).reshape(2, 128, 256)
            GU[hh, :, :, pl.ds(both + 256, 256)] = (back * gelu).astype(BF).reshape(2, 128, 256)
        return carry

    ff_a2.wait()
    ff_b2.wait()
    lax.fori_loop(0, 4, gated, 0)
    PNR, SC = r["PNR"], r["SC"]
    base_n = comm.take(2)
    comm.drain()
    for hh in range(2):
        term = dot_nt(GU[hh, :, :, 0:512].reshape(256, 512), W1[:, :, :, 0].reshape(D, 512))
        for k in range(1, 4):
            term += dot_nt(
                GU[hh, :, :, 512 * k : 512 * k + 512].reshape(256, 512), W1[:, :, :, k].reshape(D, 512)
            )
        POS[hh] = term.astype(BF).reshape(2, 128, D)
        comm.send(POS.at[hh], PNR.at[hh], base_n + hh, sib)
    PYS, PYR = r["PYS"], r["PYR"]
    yi = comm.take()
    down_all = WD[...].reshape(1024, D)
    for hh in range(2):
        PYS[hh] = dot(HX[pl.ds(pl.multiple_of(128 * (1 - c), 128), 128), 1024 * hh : 1024 * hh + 1024], down_all).astype(BF)
    comm.send(PYS, PYR, yi, sib)
    for hh in range(2):
        SC[128 * hh : 128 * hh + 128, 0:768] = dot(HX[pl.ds(pl.multiple_of(128 * c, 128), 128), 1024 * hh : 1024 * hh + 1024], down_all)

    low_r, high_r = pl.ds(0, 256), pl.ds(256, 512)
    def down_term(k, carry):
        res = dot(HIDT[pl.ds(pl.multiple_of(256 * k, 256), 256), :], CT[...].reshape(512, D))
        WD[k // 2, pl.ds((2 * k) % 4, 2)] = res.astype(BF).reshape(2, 2, 4, 16, D)
        return carry

    lax.fori_loop(0, 4, down_term, 0)
    wd_ra = Scatter(
        comm, "z", lambda zz: [WD.at[zz % 2, :, zz // 2, :, :, low_r]], [r["RA2"]]
    )
    wd_rb = Scatter(comm, "x", lambda xx: [WD.at[:, xx, :, :, :, high_r]], [r["RB2"]])
    wd_rb.start()

    ML, DOS, DO, VEC = r["ML"], r["DOS"], r["DO"], r["VEC"]
    VEC[...] = jnp.zeros((8, 1024), F32)
    base_d = comm.take(8)
    base_dr = comm.take(8)
    m = y * 2 + zh
    for hh in range(2):
        comm.recv(PNR.at[hh], base_n + hh)
        for k in range(2):
            grad = cast_up(POS[hh, k]) + cast_up(PNR[hh, k])
            middle = S2[128 * hh : 128 * hh + 128, 768 * k : 768 * k + 768]
            scale = rms_scale(middle)
            gained = grad * second_gain
            mean = jnp.mean(middle * gained, axis=-1, keepdims=True)
            full = cast_up(CT[hh, k]) + scale * gained - middle * (scale * scale * scale * mean)
            ML[hh, k] = full.astype(BF)

            @pl.when(c == k)
            def _():
                r["din"][hh] = full
                VEC[1:2, 0:768] += jnp.sum(grad * middle * scale, axis=0, keepdims=True)

        given = dot_nt(ML[hh].reshape(256, D), WOF[...].reshape(384, D))
        g0, g1, g2 = given[:, 0:128], given[:, 128:256], given[:, 256:384]
        r0, r1, r2 = pltpu.roll(g0, 64, 1), pltpu.roll(g1, 64, 1), pltpu.roll(g2, 64, 1)
        DOS[0, hh] = g0.astype(BF)
        DOS[1, hh] = jnp.where(lane < 64, r0, r1).astype(BF)
        DOS[2, hh] = jnp.where(lane < 64, r1, r2).astype(BF)
        DOS[3, hh] = g2.astype(BF)
        for yy in range(4):
            dst = DO.at[pl.ds(pl.multiple_of(256 * m, 256), 256)]
            own = (yy == y) & (hh == zh)
            cp = comm.copy(DOS.at[yy, hh], dst, base_d + 4 * hh + yy, dev(x, yy, hh * 2 + zl, c), base_dr + m)
            keep = pltpu.make_async_copy(DOS.at[yy, hh], dst, comm.rs.at[base_dr + m])
            pl.when(own)(keep.start)
            pl.when(jnp.logical_not(own))(cp.start)
            comm.pending.append((cp, own))


    def gated_term(k, carry):
        res = dot(N2T[...], GU[:, :, :, pl.ds(pl.multiple_of(512 * k, 512), 512)].reshape(512, 512))
        W1[:, :, :, k] = res.astype(BF).reshape(2, 4, 2, 48, 512)
        return carry

    lax.fori_loop(0, 4, gated_term, 0)
    pl.semaphore_signal(r["free_sem"], inc=1, device_id=sib, device_id_type=MESH)
    ff_ra = Scatter(comm, "z", lambda zz: [W1.at[zz % 2, :, zz // 2, :, :, low]], [r["RA1"]])
    ff_rb = Scatter(comm, "x", lambda xx: [W1.at[:, xx, :, :, :, high]], [r["RB1"]])
    ff_rb.start()
    attended_t = jnp.concatenate(
        [cast_up(A[hh, :, 0:384]).T.astype(BF) for hh in range(2)], axis=1
    )
    WOF[...] = dot(attended_t, ML[...].reshape(512, D)).astype(BF).reshape(4, 2, 48, D)
    base_g = comm.take(6)
    base_gr = comm.take(8)
    WOR = r["WOR"]
    for cc in range(2):
        for yy in range(3):
            src = WOF.at[:, :, :, pl.ds(128 * (cc * 3 + yy), 128)]
            cp = comm.copy(src, WOR.at[y, c], base_g + cc * 3 + yy, dev(x, yy, z, cc), base_gr + c * 4 + y)
            keep = pltpu.make_async_copy(src, WOR.at[y, c], comm.rs.at[base_gr + c * 4 + y])
            here = (yy == y) & (cc == c)
            pl.when(here)(keep.start)
            pl.when(jnp.logical_not(here))(cp.start)
            comm.pending.append((cp, here))
    comm.recv(PYR, yi)
    for hh in range(2):
        middle = S2[128 * hh : 128 * hh + 128, pl.ds(pl.multiple_of(768 * c, 128), 768)]
        r["out"][hh] = (middle + SC[128 * hh : 128 * hh + 128, 0:768] + cast_up(PYR[hh])).astype(BF)
    stores = [pltpu.make_async_copy(r["out"], r["h_out"], local_sem.at[10])]
    stores[0].start()

    SC[:, 0:2048] = jnp.zeros((256, SEQ), F32)
    S2[0:128, 0:2048] = jnp.zeros((128, SEQ), F32)
    N2[:, 0:1024] = jnp.zeros((BQ, 1024), BF)
    BT[...] = jnp.zeros((2, 256, 512), F32)
    for yy in range(4):
        for hh in range(2):
            comm.recv(DO.at[pl.ds(256 * (yy * 2 + hh), 256)], base_dr + yy * 2 + hh)
    wd_ra.start()
    ff_ra.start()

    GL, DL = r["GL"], r["DL"]

    def retreat(ui, carry):
        head, q0 = unit_of(4 * ui)
        rows = pl.ds(pl.multiple_of(q0, 1024), 1024)
        lane = iota((1024, 128), 1)
        inv = jnp.sum(jnp.where(lane == ui, LI[...], 0.0), axis=1, keepdims=True)
        given = jnp.where(lane // 64 == head, cast_up(DO[rows, :]) * inv, 0.0)
        GL[...] = given.astype(BF)
        delta = jnp.sum(cast_up(GL[...]) * cast_up(ON[rows, :]), axis=1, keepdims=True)
        DL[...] = jnp.broadcast_to(delta, (1024, 128))
        given_t = given.T.astype(BF)
        for j in range(8):
            S2[0:128, 256 * j : 256 * j + 256] += dot(given_t, PB[ui, :, 128 + 256 * j : 384 + 256 * j])

        def inner(b, more):
            block = pl.ds(pl.multiple_of(256 * b, 256), 256)
            low_rows = GL[block, :]
            shift = DL[block, 0:1]
            for j in range(8):
                cols = slice(128 + 256 * j, 384 + 256 * j)
                grad = dot(low_rows, VT[:, 256 * j : 256 * j + 256])
                PB[ui, block, cols] = (cast_up(PB[ui, block, cols]) * (grad - shift)).astype(BF)
            moved = dot(PB[ui, block, 128:2176], KN[...])
            at = q0 + 256 * b
            lane = iota((BQ, 128), 1)
            spot = pl.ds(pl.multiple_of(at // 2, 128), 128)
            N2[:, spot] = jnp.where(lane // 64 == head, moved, cast_up(N2[:, spot])).astype(BF)
            BT[head] += cast_up(PB[ui, block, pl.ds(pl.multiple_of(at, 256), 512)])
            return more

        lax.fori_loop(0, 4, inner, 0)
        query_t = cast_up(QA[head, rows, :]).T.astype(BF)
        key_rows = pl.ds(pl.multiple_of(128 * head, 128), 128)
        for j in range(8):
            SC[key_rows, 256 * j : 256 * j + 256] += dot(query_t, PB[ui, :, 128 + 256 * j : 384 + 256 * j])
        return carry

    def add_low(refs, bufs):
        for ref, buf in zip(refs, bufs):
            total = cast_up(ref[...])
            for k in range(3):
                total += cast_up(buf[k])
            ref[...] = total.astype(BF)

    lax.fori_loop(0, 3, retreat, 0)

    YR, DWQ = r["YR"], r["DWQ"]
    first_gain = r["GS"][0:1, 0:768]
    base_s = comm.take(4)
    S2[128:256, :] = jnp.zeros((128, 2304), F32)

    def sib_at(yy):
        return GU.at[yy // 2, :, :, pl.ds(pl.multiple_of((yy % 2) * 1024, 128), 768)]

    def place_of(k):
        return (y + jnp.where(k == 0, 2, jnp.where(k == 1, 1, jnp.where(k == 2, 3, 0)))) % 4

    def spread_back(k, carry):
        yy = place_of(k)

        def half(hh, inner):
            at = pl.ds(pl.multiple_of(512 * yy + 256 * hh, 256), 256)
            raw = cast_up(T5[yy, hh].reshape(256, D))
            scale = rms_scale(raw)
            normed = (raw * scale * first_gain).astype(BF)
            dq = N2[:, pl.ds(pl.multiple_of(256 * yy + 128 * hh, 128), 128)]
            sub = iota((128, 256), 0)
            dkt = jnp.where(sub < 64, SC[0:128, at], SC[128:256, at])
            dvt = S2[0:128, at]
            dk, dv = dkt.T.astype(BF), dvt.T.astype(BF)
            dqt = cast_up(dq).T.astype(BF)
            grad = dot_nt(jnp.concatenate([dq, dk, dv], axis=1), WQ[:, :, :, :, 0:384].reshape(D, 384))
            VEC[0:1, 0:768] += jnp.sum(grad * raw * scale, axis=0, keepdims=True)
            S2[128:256, 0:768] += dot(dqt, normed)
            S2[128:256, 768:1536] += dot(dkt.astype(BF), normed)
            S2[128:256, 1536:2304] += dot(dvt.astype(BF), normed)
            T5[yy, hh] = grad.astype(BF).reshape(2, 128, D)
            return inner

        lax.fori_loop(0, 2, half, 0)
        comm.copy(T5.at[yy, :, 1 - c], sib_at(yy), base_s + k, sib).start()
        return carry

    base_y = comm.take(3)

    def pass_on(k):
        yy = (y + (2, 1, 3, 0)[k]) % 4
        comm.recv(sib_at(yy), base_s + k)
        for hh in range(2):
            T5[yy, hh, c] = (cast_up(T5[yy, hh, c]) + cast_up(sib_at(yy)[hh])).astype(BF)
        if k < 3:
            comm.send(T5.at[yy, :, c], YR.at[k], base_y + k, comm.peer("y", (2, 1, 3)[k]))

    pl.semaphore_wait(r["free_sem"], 1)
    for k in range(4):
        spread_back(k, 0)
        if k:
            pass_on(k - 1)
    for i in range(3):
        DWQ[:, :, :, :, 128 * i : 128 * i + 128] = S2[128:256, 768 * i : 768 * i + 768].T.astype(BF).reshape(2, 4, 2, 48, 128)

    q_ra = Scatter(
        comm,
        "z",
        lambda zz: [DWQ.at[zz % 2, :, zz // 2, :, low]],
        [r["QA1"]],
    )
    q_ra.start()
    @pl.when(y == 3)
    def _():
        DWQ[:, :, :, :, 384:512] = jnp.zeros((2, 4, 2, 48, 128), BF)

    @pl.when(y < 3)
    def _():
        for k in range(4):
            for cc in range(2):
                comm.recv(WOR.at[k, cc], base_gr + cc * 4 + k)
        for cc in range(2):
            total = cast_up(WOR[0, cc])
            for k in range(1, 4):
                total += cast_up(WOR[k, cc])
            DWQ[cc, :, :, :, 384:512] = total.astype(BF)

    q_rb = Scatter(
        comm,
        "x",
        lambda xx: [DWQ.at[:, xx, :, :, high]],
        [r["QB1"]],
    )
    lane = iota((8, 128), 1)
    sub = iota((8, 128), 0)
    diagonals = []
    flip = jnp.where(iota((256, 256), 0) + iota((256, 256), 1) == 255, 1.0, 0.0).astype(BF)
    table_grad = jnp.zeros((1, 128), F32)
    one = iota((1, 128), 1)
    for h in range(2):
        near = jnp.zeros((1, 1024), F32)
        whole = BT[h]
        upper = whole.astype(BF)
        lower = (whole - cast_up(upper)).astype(BF)
        flipped = dot(flip, upper) + dot(flip, lower)
        for k in range(4):
            part = jnp.concatenate([flipped[64 * k : 64 * k + 64], jnp.zeros((64, 512), F32)], axis=1)
            part = pltpu.roll(part, 129 + 64 * k, 1, stride=1, stride_axis=0)
            near += jnp.sum(part, axis=0, keepdims=True)
        diagonals.append(near)
        base = 64 * (1 - h)
        rows_far = SC[128 * h + base : 128 * h + base + 8, 0:2048]
        key_at = iota((8, SEQ), 1)
        start = 256 * iota((8, SEQ), 0)
        left = jnp.sum(jnp.where(key_at < start - 128, rows_far, 0.0), axis=(0, 1), keepdims=True)
        right = jnp.sum(jnp.where(key_at >= start + 384, rows_far, 0.0), axis=(0, 1), keepdims=True)
        table_grad += jnp.where(one == 32 * h + 15, left, 0.0) + jnp.where(one == 32 * h + 31, right, 0.0)
    near = jnp.concatenate(diagonals + [jnp.zeros((6, 1024), F32)], axis=0)
    upper = near.astype(BF)
    lower = (near - cast_up(upper)).astype(BF)
    sums = dot_nt(upper, r["OH"][...]) + dot_nt(lower, r["OH"][...])
    table_grad += jnp.sum(jnp.where(lane // 32 == sub, sums, 0.0), axis=0, keepdims=True)
    spread = jnp.concatenate([table_grad, jnp.zeros((1, 256), F32)], axis=1)
    spread = pltpu.roll(jnp.broadcast_to(spread, (8, 384)), 32 * h0, 1)
    VEC[0:1, 768:1024] = spread[0:1, 0:256]
    VEC[1:2, 768:896] = spread[0:1, 256:384]

    VP = r["VP"]
    VP[...] = fold_rows(VEC[0:2, :])
    v_z = Scatter(comm, "z", lambda zz: [VP], [r["V1"]])
    q_rb.start()
    v_z.start()
    pass_on(3)
    wd_ra.wait()
    wd_rb.wait()
    ff_ra.wait()
    ff_rb.wait()

    def add_a(i, carry):
        add_low(
            [W1.at[zl, i, zh, :, :, low], WD.at[zl, i, zh, :, :, low_r]],
            [r["RA1"].at[:, i], r["RA2"].at[:, i]],
        )
        add_low(
            [W1.at[i // 2, x, i % 2, :, :, high], WD.at[i // 2, x, i % 2, :, :, high_r]],
            [r["RB1"].at[:, i // 2, i % 2], r["RB2"].at[:, i // 2, i % 2]],
        )
        return carry

    lax.fori_loop(0, 4, add_a, 0)
    ff_ra2 = Scatter(
        comm,
        "x",
        lambda xx: [W1.at[zl, xx, zh, :, :, low], WD.at[zl, xx, zh, :, :, low_r]],
        [r["SA1"], r["SA2"]],
    )
    ff_rb2 = Scatter(
        comm,
        "z",
        lambda zz: [
            W1.at[zz % 2, x, zz // 2, :, :, high],
            WD.at[zz % 2, x, zz // 2, :, :, high_r],
        ],
        [r["SB1"], r["SB2"]],
    )
    ff_ra2.start()
    ff_rb2.start()
    q_ra.wait()
    q_rb.wait()
    v_z.wait()
    for i in range(4):
        add_low([DWQ.at[zl, i, zh, :, low]], [r["QA1"].at[:, i]])
        add_low([DWQ.at[i // 2, x, i % 2, :, high]], [r["QB1"].at[:, i // 2, i % 2]])
    VE2 = r["VE2"]
    VE2[...] = VP[...] + r["V1"][0] + r["V1"][1] + r["V1"][2]
    q_ra2 = Scatter(comm, "x", lambda xx: [DWQ.at[zl, xx, zh, :, low]], [r["QA2"]])
    q_rb2 = Scatter(comm, "z", lambda zz: [DWQ.at[zz % 2, x, zz // 2, :, high]], [r["QB2"]])
    v_x = Scatter(comm, "x", lambda xx: [VE2], [r["V2"]])
    q_ra2.start()
    q_rb2.start()
    v_x.start()
    ff_ra2.wait()
    ff_rb2.wait()
    add_low([W1.at[zl, x, zh, :, :, low], WD.at[zl, x, zh, :, :, low_r]], [r["SA1"], r["SA2"]])
    add_low([W1.at[zl, x, zh, :, :, high], WD.at[zl, x, zh, :, :, high_r]], [r["SB1"], r["SB2"]])
    ff_ry = Scatter(
        comm, "y", lambda yy: [W1.at[zl, x, zh, yy], WD.at[zl, x, zh, yy]], [r["SY1"], r["SY2"]]
    )
    ff_ry.start()

    for k in range(3):
        comm.recv(YR.at[k], base_y + k)
    zri = comm.take()
    ZS, ZR = r["ZS"], r["ZR"]

    def summed(hh):
        total = cast_up(T5[y, hh, c])
        for k in range(3):
            total += cast_up(YR[k, hh])
        return total

    ZS[...] = summed(1 - zh).astype(BF)
    comm.send(ZS, ZR, zri, other)

    def finish(hh, grad):
        raw = cast_up(TK[hh, c])
        scale = rms_scale(raw)
        gained = grad * first_gain
        mean = jnp.mean(raw * gained, axis=-1, keepdims=True)
        r["din"][hh] = r["din"][hh] + scale * gained - raw * (scale * scale * scale * mean)

    finish(zh, summed(zh))

    ff_ry.wait()
    total = cast_up(W1[zl, x, zh, y])
    for k in range(3):
        total += cast_up(r["SY1"][k])
    asm[:, 512:1024] = total
    q_ra2.wait()
    q_rb2.wait()
    v_x.wait()
    total = cast_up(WD[zl, x, zh, y])
    for k in range(3):
        total += cast_up(r["SY2"][k])
    r["WDG"][...] = total
    home = (2 * c + zh, y // 2, y % 2)
    own_home = (home[0] == y) & (home[1] == zh) & (home[2] == c)
    dwi = comm.take()
    comm.send_or_keep(
        r["WDG"], r["dwd_in"], dwi, dev(x, home[0], home[1] * 2 + zl, home[2]), dwi, own_home
    )
    for cols, buf in ((low, r["QA2"]), (high, r["QB2"])):
        total = cast_up(DWQ[zl, x, zh, :, cols])
        for k in range(3):
            total += cast_up(buf[k])
        asm[:, cols] = total
    sums = unfold_rows(VE2[...] + r["V2"][0] + r["V2"][1] + r["V2"][2])
    W2R = r["W2R"]
    base_h = comm.take(8)
    base_hr = comm.take(8)
    mine = c * 4 + y
    for j in range(8):
        wst[j, 0:6, :] = asm[6 * j : 6 * j + 6, :]
        wst[j, 6:8, :] = sums[0:2]
        ys, hs, cs = 2 * zh + j // 4, (j // 2) % 2, j % 2
        own = (ys == y) & (hs == zh) & (cs == c)
        cp = comm.copy(wst.at[j], W2R.at[mine], base_h + j, dev(x, ys, hs * 2 + zl, cs), base_hr + mine)
        keep = pltpu.make_async_copy(wst.at[j], W2R.at[mine], comm.rs.at[base_hr + mine])
        pl.when(own)(keep.start)
        pl.when(jnp.logical_not(own))(cp.start)
        comm.pending.append((cp, own))
    comm.recv(ZR, zri)
    finish(1 - zh, cast_up(ZR[...]))
    for d in range(8):
        comm.recv(W2R.at[d], base_hr + d)
    for name in ("dwq", "dwk", "dwv"):
        r[name][...] = jnp.zeros((6, D), F32)
    rows_sum = jnp.zeros((2, 1024), F32)
    for cc in range(2):
        for yy in range(4):
            d, first = cc * 4 + yy, 64 * first_head(cc * 4 + yy)
            for i, name in enumerate(("dwq", "dwk", "dwv")):
                r[name][:, first : first + 128] += W2R[d, 0:6, 128 * i : 128 * i + 128]
            for i, name in enumerate(("dwg", "dwu")):
                for k in range(2):
                    tile = 2 * (2 * yy + k) + cc
                    at = 512 + 256 * i + 128 * k
                    r[name][:, 128 * tile : 128 * tile + 128] = W2R[d, 0:6, at : at + 128]
            if yy < 3:
                at = (cc * 3 + yy) * 128
                r["dwo"][:, at : at + 128] = W2R[d, 0:6, 384:512]
            rows_sum += W2R[d, 6:8, :]
    table = jnp.concatenate([rows_sum[0:1, 768:1024], rows_sum[1:2, 768:1024], rows_sum[0:1, 0:512]], axis=1)
    gains = jnp.broadcast_to(jnp.concatenate([rows_sum, jnp.zeros((6, 1024), F32)], axis=0), (8, 1024))
    gains = pltpu.roll(gains, 1024 - 6 * flat, 1)[0:2, 0:128]
    table = pltpu.roll(jnp.broadcast_to(table, (8, 1024)), 1024 - 3 * flat, 1)[0:1, 0:128]
    r["dvec"][...] = jnp.concatenate([gains, table, jnp.zeros((5, 128), F32)], axis=0)
    comm.recv(r["dwd_in"], dwi)
    names = ("din", "dwq", "dwk", "dwv", "dwo", "dwg", "dwu", "dwd", "dvec")
    for i, name in enumerate(names):
        src = r["dwd_in"] if name == "dwd" else r[name]
        stores.append(pltpu.make_async_copy(src, r["h_" + name], local_sem.at[11 + i]))
        stores[-1].start()
    for k in range(4):
        yy = (y + (2, 1, 3, 0)[k]) % 4
        comm.copy(T5.at[yy, :, 1 - c], sib_at(yy), base_s + k, sib).wait_send()
    comm.drain()
    for store in stores:
        store.wait()


INPUTS = [
    ("lens", "s"), ("g1", "s"), ("g2", "s"), ("bt", "s"),
    ("tok", "a"), ("cot", "a"), ("h_wq", "a"), ("h_wk", "a"), ("h_wv", "a"), ("h_wo", "a"),
    ("h_wg", "a"), ("h_wu", "a"), ("h_wd", "a"),
]
SCRATCH = [
    ("W1", ((2, 4, 2, 4, 48, 512), BF)),
    ("WD", ((2, 4, 2, 4, 16, 768), BF)),
    ("WQ", ((2, 4, 2, 48, 512), BF)),
    ("G5", ((2, 4, 2, 8, 256), F32)),
    ("T5", ((4, 2, 2, 128, 768), BF)),
    ("TK", ((2, 2, 128, 768), BF)),
    ("CT", ((2, 2, 128, 768), BF)),
    ("wst", ((8, 8, 1024), F32)),
    ("w0", ((8, 8, 1024), F32)),
    ("asm", ((48, 1024), F32)),
    ("wdst", ((16, 768), BF)),
    ("GS", ((8, 1024), F32)),
    ("OH", ((128, 1024), BF)),
    ("BO", ((8, 1024), F32)),
    ("BT", ((2, 256, 512), F32)),
    ("QA", ((2, 2048, 128), BF)),
    ("KT", ((2, 128, 2048), BF)),
    ("KN", ((2048, 128), BF)),
    ("VN", ((2048, 256), BF)),
    ("VT", ((128, 2048), BF)),
    ("SC", ((256, 2304), F32)),
    ("S2", ((256, 2304), F32)),
    ("PB", ((3, 1024, 2304), BF)),
    ("ON", ((2048, 128), BF)),
    ("LI", ((1024, 128), F32)),
    ("GL", ((1024, 128), BF)),
    ("DL", ((1024, 128), F32)),
    ("A", ((2, 256, 512), BF)),
    ("WOF", ((4, 2, 48, 768), BF)),
    ("POS", ((2, 2, 128, 768), BF)),
    ("POR", ((2, 2, 128, 768), BF)),
    ("N2", ((256, 1536), BF)),
    ("N2T", ((768, 512), BF)),
    ("HIDT", ((1024, 512), BF)),
    ("GU", ((2, 2, 128, 2048), BF)),
    ("PNR", ((2, 2, 128, 768), BF)),
    ("PYS", ((2, 128, 768), BF)),
    ("PYR", ((2, 128, 768), BF)),
    ("ML", ((2, 2, 128, 768), BF)),
    ("DOS", ((4, 2, 256, 128), BF)),
    ("DO", ((2048, 128), BF)),
    ("RA1", ((3, 4, 4, 48, 256), BF)),
    ("RA2", ((3, 4, 4, 16, 256), BF)),
    ("RB1", ((3, 2, 2, 4, 48, 256), BF)),
    ("RB2", ((3, 2, 2, 4, 16, 512), BF)),
    ("SA1", ((3, 4, 48, 256), BF)),
    ("SA2", ((3, 4, 16, 256), BF)),
    ("SB1", ((3, 4, 48, 256), BF)),
    ("SB2", ((3, 4, 16, 512), BF)),
    ("SY1", ((3, 48, 512), BF)),
    ("SY2", ((3, 16, 768), BF)),
    ("WOR", ((4, 2, 4, 2, 48, 128), BF)),
    ("HX", ((256, 2304), BF)),
    ("YR", ((3, 2, 128, 768), BF)),
    ("ZS", ((128, 768), BF)),
    ("ZR", ((128, 768), BF)),
    ("DWQ", ((2, 4, 2, 48, 512), BF)),
    ("QA1", ((3, 4, 48, 256), BF)),
    ("QA2", ((3, 48, 256), BF)),
    ("QB1", ((3, 2, 2, 48, 256), BF)),
    ("QB2", ((3, 48, 256), BF)),
    ("VEC", ((8, 1024), F32)),
    ("V1", ((3, 8, 256), F32)),
    ("V2", ((3, 8, 256), F32)),
    ("VE2", ((8, 256), F32)),
    ("VP", ((8, 256), F32)),
    ("W2R", ((8, 8, 1024), F32)),
    ("WDG", ((16, 768), F32)),
    ("dwd_in", ((16, 768), F32)),
    ("out", ((2, 128, 768), BF)),
    ("din", ((2, 128, 768), F32)),
    ("dwq", ((6, 768), F32)),
    ("dwk", ((6, 768), F32)),
    ("dwv", ((6, 768), F32)),
    ("dwo", ((6, 768), F32)),
    ("dwg", ((6, 2048), F32)),
    ("dwu", ((6, 2048), F32)),
    ("dvec", ((8, 128), F32)),
    ("wq", ((6, 768), F32)),
    ("wk", ((6, 768), F32)),
    ("wv", ((6, 768), F32)),
    ("wo", ((6, 768), F32)),
    ("wg", ((6, 2048), F32)),
    ("wu", ((6, 2048), F32)),
    ("wd", ((16, 768), F32)),
    ("free_sem", 0),
    ("local_sem", 32),
    ("send_sem", None),
    ("recv_sem", None),
]


OUTPUTS = [
    ("h_out", ((2, 128, 768), BF)),
    ("h_din", ((2, 128, 768), F32)),
    ("h_dwq", ((6, 768), F32)),
    ("h_dwk", ((6, 768), F32)),
    ("h_dwv", ((6, 768), F32)),
    ("h_dwo", ((6, 768), F32)),
    ("h_dwg", ((6, 2048), F32)),
    ("h_dwu", ((6, 2048), F32)),
    ("h_dwd", ((16, 768), F32)),
    ("h_dvec", ((8, 128), F32)),
]


def call_mega(*args):
    spec = {"s": pl.BlockSpec(memory_space=pltpu.SMEM), "a": pl.BlockSpec(memory_space=pl.ANY)}
    outs = OUTPUTS
    scratch = []
    for _, s in SCRATCH:
        if s == 0:
            scratch.append(pltpu.SemaphoreType.REGULAR)
        elif s is None or isinstance(s, int):
            scratch.append(pltpu.SemaphoreType.DMA((s or NSEM,)))
        else:
            scratch.append(pltpu.VMEM(s[0], s[1]))
    return pl.pallas_call(
        mega,
        out_shape=[jax.ShapeDtypeStruct(s[0], s[1]) for _, s in outs],
        in_specs=[spec[k] for _, k in INPUTS],
        out_specs=[pl.BlockSpec(memory_space=pl.ANY) for _ in outs],
        scratch_shapes=scratch,
        name="layer",
        compiler_params=pltpu.CompilerParams(
            collective_id=0, has_side_effects=True, vmem_limit_bytes=62 * 2**20
        ),
    )(*args)


def per_device(
    tokens,
    lengths,
    cotangent,
    query_weight,
    key_weight,
    value_weight,
    out_weight,
    gate_weight,
    up_weight,
    down_weight,
    first_gain,
    second_gain,
    bias_table,
):
    done = call_mega(
        lengths,
        first_gain,
        second_gain,
        bias_table,
        tokens,
        cotangent,
        query_weight,
        key_weight,
        value_weight,
        out_weight,
        gate_weight,
        up_weight,
        down_weight,
    )
    return hand_out(*done)


def hand_out_kernel(*refs):
    n = len(OUTPUTS)
    vectors, ins, outs, held, sem = refs[0], refs[1:n], refs[n : 2 * n + 2], refs[2 * n + 2 : -1], refs[-1]
    loads = [pltpu.make_async_copy(a, b, sem.at[i]) for i, (a, b) in enumerate(zip(ins, held))]
    copies = [pltpu.make_async_copy(a, b, sem.at[i]) for i, (a, b) in enumerate(zip(held, outs))]
    for load in loads:
        load.start()
    for load, copy in zip(loads, copies):
        load.wait()
        copy.start()
    for row, (ref, width) in enumerate(zip(outs[n - 1 :], (6, 6, 3))):
        for i in range(width):
            ref[i] = vectors[row, i]
    for copy in copies:
        copy.wait()


def hand_out(*done):
    shapes = [jax.ShapeDtypeStruct(s[0], s[1]) for _, s in OUTPUTS[:-1]]
    shapes += [jax.ShapeDtypeStruct((n,), F32) for n in (6, 6, 3)]
    smem, hbm = pl.BlockSpec(memory_space=pltpu.SMEM), pl.BlockSpec(memory_space=pl.ANY)
    n = len(done) - 1
    return tuple(
        pl.pallas_call(
            hand_out_kernel,
            out_shape=shapes,
            in_specs=[smem] + [hbm] * n,
            out_specs=[hbm] * n + [smem] * 3,
            scratch_shapes=[pltpu.VMEM(s[0], s[1]) for _, s in OUTPUTS[:-1]]
            + [pltpu.SemaphoreType.DMA((n,))],
            name="hand_out",
        )(done[-1], *done[:-1])
    )


def solution(mesh):
    tokens = P("rows", "seq", None)
    matrix = P(("rows", "seq"), None)
    vector = P(("rows", "seq"))
    return jax.shard_map(
        per_device,
        mesh=mesh,
        in_specs=(tokens, P("rows"), tokens, *([matrix] * 7), *([vector] * 3)),
        out_specs=(tokens, tokens, *([matrix] * 7), *([vector] * 3)),
        check_vma=False,
    )
```
